32 devices in a mesh: dp: 16 (over z, y, x), mp: 2 (over core).
Axes of the slice: x: 2, y: 2, z: 4, core: 2. Of those that a mesh axis runs over, the one named last changes fastest.
Arguments:
- inputs: bfloat16 [8192, 768], P('dp'), may hold values from -6 to 6
- norm_attn: float32 [768], replicated, may hold values from 0.1 to 1.9
- w_query: bfloat16 [768, 768], P(None, 'mp'), may hold values from -0.21875 to 0.21875
- w_key: bfloat16 [768, 768], P(None, 'mp'), may hold values from -0.21875 to 0.21875
- w_value: bfloat16 [768, 768], P(None, 'mp'), may hold values from -0.21875 to 0.21875
- w_out: bfloat16 [768, 768], P('mp'), may hold values from -1.25 to 1.25
- norm_mlp: float32 [768], replicated, may hold values from 0.1 to 1.9
- w_up: bfloat16 [768, 3072], P(None, 'mp'), may hold values from -0.21875 to 0.21875
- b_up: float32 [3072], P('mp'), may hold values from -3 to 3
- w_down: bfloat16 [3072, 768], P('mp'), may hold values from -0.109375 to 0.109375
- b_down: float32 [768], replicated, may hold values from -3 to 3
- cotangent: bfloat16 [8192, 768], P('dp'), may hold values from -6 to 6
- doc_lengths: int32 [16, 8], replicated, may hold values from 1 to 128, 256 in all within a row
- pad_counts: int32 [16], replicated, may hold values from 0 to 64
Outputs:
- output: bfloat16 [8192, 768], P('dp')
- grad_inputs: bfloat16 [8192, 768], P('dp')
- grad_norm_attn: float32 [768], replicated
- grad_query: float32 [768, 768], P(None, 'mp')
- grad_key: float32 [768, 768], P(None, 'mp')
- grad_value: float32 [768, 768], P(None, 'mp')
- grad_out: float32 [768, 768], P('mp')
- grad_norm_mlp: float32 [768], replicated
- grad_up: float32 [768, 3072], P(None, 'mp')
- grad_b_up: float32 [3072], P('mp')
- grad_down: float32 [3072, 768], P('mp')
- grad_b_down: float32 [768], replicated
The draws below stay inside these ranges and needn't reach their ends.
Inputs may be any that keep to these rules, and one draw needn't show every extreme that they name: `doc_lengths`: row n lists the document lengths of sequence n in order; each row sums to 256 and its largest entry is 128. The last pad_counts[n] positions of sequence n are padding.
All inputs are finite; a program needn't handle non-finite values.
Results may differ from the reference program's by a relative error of at most 0.011.
Values sent between devices are 32-bit elements; how exact they have to be, the bound alone decides.
No kernel may reach another device: no remote copies, remote signals or barrier semaphores. Data moves between devices by JAX's collectives and lax.ppermute only.
A program may use at most 128 MiB of HBM per device.

```python
import math
import jax
import jax.numpy as jnp
import numpy as np
from jax import lax

D = 768
HEADS = 12
HEAD = 64
FF = 3072
BLOCK = 16
LEN = 256
DOCS = 8
SEQS = 16
TOKENS = 8192
HH = 768


def with_ends(result, rng, smallest, top_value):
    longest = result.shape.index(max(result.shape))
    spots = []
    for shift in (0, 1):
        where = [jax.random.randint(jax.random.fold_in(rng, axis), (), 0, length) for axis, length in enumerate(result.shape)]
        where[longest] = (where[longest] + shift) % result.shape[longest]
        spots.append(tuple(where))
    return result.at[spots[0]].set(smallest).at[spots[1]].set(top_value)


def level_of(key, dims, cuts, smallest, largest):
    def one(dim, parts):
        draws = jax.random.uniform(jax.random.fold_in(jax.random.fold_in(key, 6), dim), (parts,), jnp.float32, smallest / len(cuts), largest / len(cuts))
        return jnp.repeat(jnp.exp(draws), dims[dim] // parts).reshape((-1,) + (1,) * (len(dims) - dim - 1))

    level = one(*cuts[0])
    for cut in cuts[1:]:
        level = level * one(*cut)
    return level


def profile(amount, total, reach, lean):
    weights = [(1 << 20) // math.isqrt(grade ** lean) + 1 for grade in range(2, amount + 1)]
    spare, holding = total - reach - (amount - 1), [1] * (amount - 1)
    while spare > 0:
        candidates = [i for i in range(amount - 1) if holding[i] < reach]
        pool, left = sum([weights[i] for i in candidates]), spare
        for i in candidates:
            more = min(reach - holding[i], max(1, left * weights[i] // pool), spare)
            holding[i] = holding[i] + more
            spare = spare - more
    return np.array([reach] + holding)


def uneven(stream_key, number_of, total, most, slope):
    if number_of == 2:
        one = jax.random.randint(stream_key, (), max(1, total - most), min(most, total - 1) + 1)
        return jnp.stack([one, total - one])
    sizes = jnp.asarray(profile(number_of, total, most, slope), jnp.int32)
    twos = (number_of - 1) // 2
    giver, sink = sizes[1:1 + 2 * twos:2], sizes[2:2 + 2 * twos:2]
    margin = jnp.minimum(giver - 1, most - sink)
    moved = jax.random.randint(jax.random.fold_in(stream_key, 1), (twos,), 0, 1 << 20) % (margin + 1)
    sizes = sizes.at[1:1 + 2 * twos:2].set(giver - moved).at[2:2 + 2 * twos:2].set(sink + moved)
    return sizes[jax.random.permutation(jax.random.fold_in(stream_key, 2), number_of)]


def bell_draw(rng, shape, width, most, pieces=(), held_as=jnp.bfloat16):
    loudness = level_of(rng, shape, pieces, -0.22, 0.18) if pieces else 1.0
    values = jax.random.normal(rng, shape, jnp.float32) * width * loudness
    return jnp.minimum(jnp.maximum(values, -most), most).astype(held_as)


def setup_inputs(seed: int = 0) -> dict:
    key_of = jax.random.split(jax.random.key(seed), 15)
    inputs = bell_draw(key_of[0], (TOKENS, D), 1.0, 6.0, ((0, 16),))
    norm_attn = jnp.clip(1.0 + 0.18 * jax.random.normal(key_of[1], (D,), jnp.float32), 0.1, 1.9)
    w_query = bell_draw(key_of[2], (D, HH), D ** -0.5, 0.21875, ((1, 2),))
    w_key = bell_draw(key_of[3], (D, HH), D ** -0.5, 0.21875, ((1, 2),))
    w_value = bell_draw(key_of[4], (D, HH), D ** -0.5, 0.21875, ((1, 2),))
    w_out = bell_draw(key_of[5], (HH, D), (HH // 32) ** -0.5, 1.25, ((0, 2),))
    norm_mlp = jnp.clip(1.0 + 0.18 * jax.random.normal(key_of[6], (D,), jnp.float32), 0.1, 1.9)
    w_up = bell_draw(key_of[7], (D, FF), D ** -0.5, 0.21875, ((1, 2),))
    b_up = bell_draw(key_of[8], (FF,), 0.5, 3.0, ((0, 2),), jnp.float32)
    w_down = bell_draw(key_of[9], (FF, D), FF ** -0.5, 0.109375, ((0, 2),))
    b_down = bell_draw(key_of[10], (D,), 0.5, 3.0, (), jnp.float32)
    cotangent = bell_draw(key_of[11], (TOKENS, D), 1.0, 6.0, ((0, 16),))
    doc_lengths = jax.vmap(lambda own: uneven(own, DOCS, LEN, LEN // 2, 2))(jax.random.split(key_of[12], SEQS)).reshape((SEQS, DOCS)).astype(jnp.int32)
    pad_counts = with_ends(jax.random.randint(key_of[13], (SEQS,), 0, LEN // 4 + 1), jax.random.fold_in(key_of[13], 1), 0, (LEN // 4 + 1) - 1).astype(jnp.int32)
    return dict(inputs=inputs, norm_attn=norm_attn, w_query=w_query, w_key=w_key, w_value=w_value, w_out=w_out, norm_mlp=norm_mlp, w_up=w_up, b_up=b_up, w_down=w_down, b_down=b_down, cotangent=cotangent, doc_lengths=doc_lengths, pad_counts=pad_counts)


norm_eps = 1e-05
rope_base = 10000.0
masked_score = -1e+30

@jax.custom_vjp
def low(v):
    return lax.optimization_barrier(v.astype(jnp.bfloat16)).astype(jnp.float32)

@jax.custom_vjp
def low_back(v):
    return v

def low_keep(v):
    return (low(v), None)

def low_pass(kept, grad):
    return (grad,)

def back_keep(v):
    return (v, None)

def back_low(kept, grad):
    return (low(grad),)
low.defvjp(low_keep, low_pass)
low_back.defvjp(back_keep, back_low)

def dense_dot(left, right):
    return jnp.dot(left, right, precision=lax.Precision.HIGHEST, preferred_element_type=jnp.float32)

def layer_norm(values, gain_row):
    centred = values - lax.optimization_barrier(jnp.mean(values, axis=-1, keepdims=True))
    spread = lax.optimization_barrier(jnp.mean(centred * centred, axis=-1, keepdims=True))
    return centred * lax.rsqrt(spread + norm_eps) * gain_row

def angles(places):
    half_head = HEAD // 2
    frequency = jnp.exp(jnp.arange(half_head, dtype=jnp.float32) * (-2.0 * math.log(rope_base) / HEAD))
    turn_angle = places.astype(jnp.float32)[:, None] * frequency[None, :]
    return (jnp.cos(turn_angle), jnp.sin(turn_angle))

def rotate(values, cosine_rows, sine_rows):
    row_count = values.shape[0]
    half_head = HEAD // 2
    head_grid = values.reshape(row_count, -1, HEAD)
    first_half = head_grid[:, :, :half_head]
    second_half = head_grid[:, :, half_head:]
    cos_rows = cosine_rows[:, None, :]
    sin_rows = sine_rows[:, None, :]
    turned = jnp.concatenate([first_half * cos_rows - second_half * sin_rows, second_half * cos_rows + first_half * sin_rows], axis=-1)
    return turned.reshape(row_count, -1)

def row_facts(lengths, pad_count, places):
    doc_ends = jnp.cumsum(lengths).astype(jnp.int32)
    segment = lax.optimization_barrier(jnp.sum((places[:, None] >= doc_ends[None, :]).astype(jnp.int32), axis=1)).astype(jnp.int32)
    padded = places >= LEN - pad_count
    return (segment, padded)

def permitted(query_kind, query_place, query_segment, key_kind, key_place, key_segment, key_padded):
    query_block = (query_place // BLOCK)[:, None]
    key_block = (key_place // BLOCK)[None, :]
    query_copy = query_kind[:, None]
    key_copy = key_kind[None, :]
    noisy_rule = jnp.where(key_copy == 0, key_block == query_block, key_block < query_block)
    clean_rule = (key_copy == 1) & (key_block <= query_block)
    shaped = jnp.where(query_copy == 0, noisy_rule, clean_rule)
    same_doc = (query_segment[:, None] == key_segment[None, :]) & jnp.logical_not(key_padded[None, :])
    itself = (query_place[:, None] == key_place[None, :]) & (query_copy == key_copy)
    return shaped & (same_doc | itself)

def attend_seq(query_rows, key_rows, value_rows, allowed):
    row_count = query_rows.shape[0]
    query_grid = query_rows.reshape(row_count, HEADS, HEAD)
    key_grid = key_rows.reshape(row_count, HEADS, HEAD)
    value_grid = value_rows.reshape(row_count, HEADS, HEAD)
    scores = jnp.einsum('qhe,khe->hqk', query_grid, key_grid, precision=lax.Precision.HIGHEST) * HEAD ** (-0.5)
    scores = low_back(scores)
    probabilities = jax.nn.softmax(jnp.where(allowed[None], scores, masked_score), axis=-1)
    mixed_rows = jnp.einsum('hqk,khe->qhe', low(probabilities), value_grid, precision=lax.Precision.HIGHEST)
    return mixed_rows.reshape(row_count, HEADS * HEAD)

def layer_seq(params, seq_input, lengths, pad_count):
    norm_attn, w_query, w_key, w_value, w_out, norm_mlp, w_up, b_up, w_down, b_down = params
    row_ids = jnp.arange(2 * LEN, dtype=jnp.int32)
    copy_kind = row_ids // LEN
    places = row_ids % LEN
    segment, padded = row_facts(lengths, pad_count, places)
    allowed = permitted(copy_kind, places, segment, copy_kind, places, segment, padded)
    cosine_rows, sine_rows = angles(places)
    normed = low(layer_norm(seq_input, norm_attn))
    queries = low(rotate(low_back(dense_dot(normed, w_query)), cosine_rows, sine_rows))
    key_rows = low(rotate(low_back(dense_dot(normed, w_key)), cosine_rows, sine_rows))
    value_rows = low(low_back(dense_dot(normed, w_value)))
    attended = low(low_back(attend_seq(queries, key_rows, value_rows, allowed)))
    residual = seq_input + low_back(dense_dot(attended, w_out))
    normed_mlp = low(layer_norm(residual, norm_mlp))
    up_rows = low_back(dense_dot(normed_mlp, w_up) + b_up)
    activation = low(jax.nn.gelu(up_rows, approximate=True))
    return residual + low_back(dense_dot(activation, w_down)) + b_down

def forward(wide_input, params, doc_lengths, pad_counts):
    feature_count = wide_input.shape[1]
    by_seq = wide_input.reshape(SEQS, 2 * LEN, feature_count)
    checked = jax.checkpoint(layer_seq)

    def one_sequence(packed):
        return checked(params, packed[0], packed[1], packed[2])
    results = lax.map(one_sequence, (by_seq, doc_lengths, pad_counts))
    return results.reshape(SEQS * 2 * LEN, feature_count)

def reference(inputs, norm_attn, w_query, w_key, w_value, w_out, norm_mlp, w_up, b_up, w_down, b_down, cotangent, doc_lengths, pad_counts):
    wide_input = inputs.astype(jnp.float32)
    params = tuple((weight.astype(jnp.float32) for weight in (norm_attn, w_query, w_key, w_value, w_out, norm_mlp, w_up, b_up, w_down, b_down)))

    def whole(layer_input, weights):
        return forward(layer_input, weights, doc_lengths, pad_counts)
    output, pullback = jax.vjp(whole, wide_input, params)
    grad_input, weight_grads = pullback(cotangent.astype(jnp.float32))
    return (output.astype(jnp.bfloat16), grad_input.astype(jnp.bfloat16), weight_grads[0], weight_grads[1], weight_grads[2], weight_grads[3], weight_grads[4], weight_grads[5], weight_grads[6], weight_grads[7], weight_grads[8], weight_grads[9])
```

```python
import math

import numpy as np

import jax
import jax.numpy as jnp
from jax import lax
from jax.experimental import pallas as pl
from jax.experimental.pallas import tpu as pltpu
from jax.sharding import PartitionSpec as P

HEAD = 64
BLOCK = 16
LEN = 256
HALF = 128
LANES = 128
GROUP = 16

norm_eps = 1e-05
rope_base = 10000.0
masked_score = -1e30
score_scale = HEAD ** (-0.5)
bf16 = jnp.bfloat16
f32 = jnp.float32

X, Y, Z1, Z2 = 1, 2, 4, 8
ORDERS_MLP = ((X, Y, Z1, Z2), (Y, X, Z1, Z2), (Z1, Z2, X, Y))
ORDERS_ATT = ((X, Y, Z1, Z2), (Y, X, Z1, Z2))

CASES = ((0, 0, 256, 0), (128, 256, 384, 128), (256, 640, 128, 128), (384, 768, 256, 128))
TILES = (
    (0, 0, 0, 0),
    (0, 1, 0, 0),
    (0, 1, 128, 0),
    (0, 1, 128, 128),
    (0, 0, 128, 128),
    (1, 1, 0, 0),
    (1, 1, 128, 0),
    (1, 1, 128, 128),
)
KEY_PLACE = (0, 3, 1, 2)


def mm(left, right):
    return jnp.dot(left, right, preferred_element_type=f32)


def tn(left, right):
    return lax.dot_general(left, right, (((0,), (0,)), ((), ())), preferred_element_type=f32)


def nt(left, right):
    return lax.dot_general(left, right, (((1,), (1,)), ((), ())), preferred_element_type=f32)


def rope_tables():
    half = HEAD // 2
    frequency = np.exp(np.arange(half) * (-2.0 * math.log(rope_base) / HEAD)).astype(np.float32)
    turn = (np.arange(LEN, dtype=np.float32)[:, None] * frequency[None, :]).astype(np.float32)
    cosine, sine = np.cos(turn.astype(np.float64)), np.sin(turn.astype(np.float64))
    cosine = np.tile(cosine, (1, LANES // half)).astype(np.float32)
    sine = np.tile(np.concatenate([-sine, sine], 1), (1, LANES // HEAD)).astype(np.float32)
    return cosine, sine


def swap_halves(values):
    lane = lax.broadcasted_iota(jnp.int32, values.shape, 1)
    return jnp.where(
        lane % HEAD < HEAD // 2, pltpu.roll(values, LANES - HEAD // 2, 1), pltpu.roll(values, HEAD // 2, 1)
    )


def head_mask(rows, which):
    lane = lax.broadcasted_iota(jnp.int32, (rows, LANES), 1)
    return (lane >= HEAD) if which else (lane < HEAD)


def layer_norm_rows(values, gain):
    centred = values - jnp.mean(values, axis=-1, keepdims=True)
    spread = jnp.mean(centred * centred, axis=-1, keepdims=True)
    return centred * lax.rsqrt(spread + norm_eps) * gain


def norm_back_rows(values, gain, delta):
    centred = values - jnp.mean(values, axis=-1, keepdims=True)
    spread = jnp.mean(centred * centred, axis=-1, keepdims=True)
    s = lax.rsqrt(spread + norm_eps)
    xhat = centred * s
    e = delta * gain
    back = s * (e - jnp.mean(e, axis=-1, keepdims=True) - xhat * jnp.mean(e * xhat, axis=-1, keepdims=True))
    return back, jnp.sum(delta * xhat, axis=0, keepdims=True)


def fill_bias(lengths_ref, pads_ref, bias_ref):
    sequence = lax.axis_index("dp")
    docs = lengths_ref.shape[1]
    ends, total = [], jnp.int32(0)
    for j in range(docs):
        total = total + lengths_ref[sequence, j]
        ends.append(total)
    first_pad = LEN - pads_ref[sequence]

    def segment(places):
        seg = jnp.zeros(places.shape, jnp.int32)
        for end in ends:
            seg = seg + (places >= end).astype(jnp.int32)
        return seg

    rows, cols, row_seg, col_seg = {}, {}, {}, {}
    for base in (0, HALF):
        rows[base] = lax.broadcasted_iota(jnp.int32, (HALF, LANES), 0) + base
        cols[base] = lax.broadcasted_iota(jnp.int32, (HALF, LANES), 1) + base
        row_seg[base] = segment(rows[base])
        col_seg[base] = segment(cols[base])
    for tile, (query_kind, key_kind, query_base, key_base) in enumerate(TILES):
        q, k = rows[query_base], cols[key_base]
        query_block, key_block = q // BLOCK, k // BLOCK
        same_doc = (row_seg[query_base] == col_seg[key_base]) & (k < first_pad)
        if query_kind == 0 and key_kind == 0:
            ok = (key_block == query_block) & (same_doc | (q == k))
        elif query_kind == 0:
            ok = (key_block < query_block) & same_doc
        else:
            ok = (key_block <= query_block) & (same_doc | (q == k))
        bias_ref[:, tile * LANES : (tile + 1) * LANES] = jnp.where(ok, 0.0, masked_score)


def attention_forward(
    lengths_ref, pads_ref, x_ref, gain_ref, wq_ref, wk_ref, wv_ref, wo_ref, cos_ref, sin_ref,
    normed_ref, q_ref, k_ref, v_ref, att_ref, prob_ref, part_ref, bias_ref,
):
    heads_cols = wq_ref.shape[1]
    pairs = heads_cols // LANES
    fill_bias(lengths_ref, pads_ref, bias_ref)

    @pl.loop(0, x_ref.shape[0] // 64)
    def _(i):
        rows = pl.ds(pl.multiple_of(i * 64, 64), 64)
        normed_ref[rows, :] = layer_norm_rows(x_ref[rows, :].astype(f32), gain_ref[...]).astype(bf16)

    for block in range(4):
        rows = slice(block * HALF, block * HALF + HALF)
        places = slice((block % 2) * HALF, (block % 2) * HALF + HALF)
        key_rows = slice(KEY_PLACE[block] * HALF, KEY_PLACE[block] * HALF + HALF)
        normed = normed_ref[rows, :]
        cosine, sine = cos_ref[places, :], sin_ref[places, :]
        query, key = mm(normed, wq_ref[...]), mm(normed, wk_ref[...])
        for t in range(pairs):
            cols = slice(t * LANES, (t + 1) * LANES)
            turned = query[:, cols] * cosine + swap_halves(query[:, cols]) * sine
            q_ref[rows, cols] = (turned.astype(bf16).astype(f32) * score_scale).astype(bf16)
            turned = key[:, cols] * cosine + swap_halves(key[:, cols]) * sine
            k_ref[key_rows, cols] = turned.astype(bf16)
        v_ref[key_rows, :] = mm(normed, wv_ref[...]).astype(bf16)

    for t in range(pairs):
        cols = slice(t * LANES, (t + 1) * LANES)
        key_pair, value_pair = k_ref[:, cols], v_ref[:, cols]
        mixed = [None] * 4
        for which in range(2):
            mask = head_mask(key_pair.shape[0], which)
            key_head = jnp.where(mask, key_pair, jnp.zeros_like(key_pair))
            value_head = jnp.where(mask, value_pair, jnp.zeros_like(value_pair))
            for case, (query_row, first, width, key_row) in enumerate(CASES):
                scores = nt(q_ref[query_row : query_row + HALF, cols], key_head[key_row : key_row + width])
                scores = scores + bias_ref[:, first : first + width]
                weights = jnp.exp(scores - jnp.max(scores, axis=1, keepdims=True))
                low = (weights * (1.0 / jnp.sum(weights, axis=1, keepdims=True))).astype(bf16)
                prob_ref[2 * t + which, :, first : first + width] = low
                part = mm(low, value_head[key_row : key_row + width])
                mixed[case] = part if mixed[case] is None else mixed[case] + part
        for case, (query_row, _, _, _) in enumerate(CASES):
            att_ref[query_row : query_row + HALF, cols] = mixed[case].astype(bf16)

    for block in range(2):
        rows = slice(block * 256, block * 256 + 256)
        part_ref[rows, :] = mm(att_ref[rows, :], wo_ref[...])


def pack(order, place):
    slot = 0
    for step, bit in enumerate(order):
        if place & (1 << (3 - step)):
            slot |= bit
    return slot


def mlp_kernel(
    x_ref, mine_ref, theirs_ref, gain_ref, wu_ref, bu_ref, wd_ref, cot_ref,
    residual_ref, normed_ref, act_ref, du_ref, gbu_ref, gbd_ref, *outs_and_scratch,
):
    *outs, gd_ref, gu_ref = outs_and_scratch
    row_count = x_ref.shape[0]
    units = wu_ref.shape[1]
    width = x_ref.shape[1]
    me = lax.axis_index("dp") % GROUP
    gbu_ref[...] = jnp.zeros_like(gbu_ref)
    gbd_ref[...] = jnp.zeros_like(gbd_ref)

    @pl.loop(0, row_count // 64)
    def _(i):
        rows = pl.ds(pl.multiple_of(i * 64, 64), 64)
        residual = x_ref[rows, :].astype(f32) + (mine_ref[rows, :] + theirs_ref[rows, :])
        residual_ref[rows, :] = residual
        normed_ref[rows, :] = layer_norm_rows(residual, gain_ref[...]).astype(bf16)
        gbd_ref[...] += jnp.sum(cot_ref[rows, :].astype(f32), axis=0, keepdims=True)

    c0 = math.sqrt(2.0 / math.pi)
    c1 = c0 * 0.044715

    @pl.loop(0, units // 256)
    def _(j):
        cols = pl.ds(pl.multiple_of(j * 256, 256), 256)
        for block in range(row_count // 256):
            rows = slice(block * 256, block * 256 + 256)
            u = mm(normed_ref[rows, :], wu_ref[:, cols]) + bu_ref[:, cols]
            delta = nt(cot_ref[rows, :], wd_ref[cols, :])
            square = u * u
            t = jnp.tanh(u * (c0 + c1 * square))
            half_up = 0.5 * (1.0 + t)
            act_ref[rows, cols] = (u * half_up).astype(bf16)
            slope = half_up + (0.5 * u) * (1.0 - t * t) * (c0 + (3.0 * c1) * square)
            low = (delta * slope).astype(bf16)
            du_ref[rows, cols] = low
            gbu_ref[:, cols] += jnp.sum(low.astype(f32), axis=0, keepdims=True)
        gd_ref[cols, :] = tn(act_ref[:, cols], cot_ref[...])
        gu_ref[:, cols] = tn(normed_ref[...], du_ref[:, cols])

    down_rows, up_rows = units // GROUP, width // GROUP
    part_cols = width // len(ORDERS_MLP)
    for p, order in enumerate(ORDERS_MLP):
        for place in range(GROUP):
            block = me ^ pack(order, place)
            out = outs[2 * p + (place >= 8)]
            spot = place % 8
            out[spot, 0:down_rows, :] = gd_ref[
                pl.ds(pl.multiple_of(block * down_rows, 8), down_rows), p * part_cols : (p + 1) * part_cols
            ]
            for half in range(units // width):
                start = half * width + p * part_cols
                at = down_rows + half * up_rows
                out[spot, at : at + up_rows, :] = gu_ref[
                    pl.ds(pl.multiple_of(block * up_rows, 8), up_rows), start : start + part_cols
                ]


def mlp_tail_kernel(act_ref, du_ref, wu_ref, wd_ref, delta_ref, out_ref):
    for block in range(act_ref.shape[0] // 256):
        rows = slice(block * 256, block * 256 + 256)
        delta_ref[rows, :] = nt(du_ref[rows, :], wu_ref[...])
    for block in range(act_ref.shape[0] // 256):
        rows = slice(block * 256, block * 256 + 256)
        out_ref[rows, :] = mm(act_ref[rows, :], wd_ref[...])


def attention_backward(
    mine_ref, theirs_ref, residual_ref, gain_ref, cot_ref, att_ref, wo_ref, q_ref, k_ref, v_ref, prob_ref,
    normed_ref, wq_ref, wk_ref, wv_ref, cos_ref, sin_ref,
    delta_ref, gnorm_ref, part_ref, *outs_and_scratch,
):
    *outs, branch_ref, datt_ref, dq_ref, dk_ref, dv_ref, dk_acc, dv_acc, go_ref, gq_ref, gk_ref, gv_ref = outs_and_scratch
    row_count = residual_ref.shape[0]
    heads_cols = wq_ref.shape[1]
    pairs = heads_cols // LANES
    me = lax.axis_index("dp") % GROUP
    gnorm_ref[...] = jnp.zeros_like(gnorm_ref)

    @pl.loop(0, row_count // 64)
    def _(i):
        rows = pl.ds(pl.multiple_of(i * 64, 64), 64)
        delta = mine_ref[rows, :] + theirs_ref[rows, :]
        back, gain_part = norm_back_rows(residual_ref[rows, :], gain_ref[...], delta)
        back = back + cot_ref[rows, :].astype(f32)
        delta_ref[rows, :] = back
        branch_ref[rows, :] = back.astype(bf16)
        gnorm_ref[...] += gain_part

    for block in range(2):
        rows = slice(block * 256, block * 256 + 256)
        datt_ref[rows, :] = nt(branch_ref[rows, :], wo_ref[...]).astype(bf16)
    go_ref[...] = tn(att_ref[...], branch_ref[...])

    for t in range(pairs):
        cols = slice(t * LANES, (t + 1) * LANES)
        key_pair, value_pair = k_ref[:, cols], v_ref[:, cols]
        dk_acc[...] = jnp.zeros_like(dk_acc)
        dv_acc[...] = jnp.zeros_like(dv_acc)
        query_grads = [None] * 4
        for which in range(2):
            mask = head_mask(key_pair.shape[0], which)
            key_head = jnp.where(mask, key_pair, jnp.zeros_like(key_pair))
            value_head = jnp.where(mask, value_pair, jnp.zeros_like(value_pair))
            small = head_mask(HALF, which)
            for case, (query_row, first, width, key_row) in enumerate(CASES):
                rows = slice(query_row, query_row + HALF)
                keys = slice(key_row, key_row + width)
                low = prob_ref[2 * t + which, :, first : first + width]
                wide = low.astype(f32)
                delta_head = datt_ref[rows, cols]
                g = nt(delta_head, value_head[keys])
                weighted = wide * g
                scores_back = (weighted - wide * jnp.sum(weighted, axis=1, keepdims=True)).astype(bf16)
                part = mm(scores_back, key_head[keys])
                query_grads[case] = part if query_grads[case] is None else query_grads[case] + part
                query = q_ref[rows, cols]
                query = jnp.where(small, query, jnp.zeros_like(query))
                delta_head = jnp.where(small, delta_head, jnp.zeros_like(delta_head))
                dk_acc[keys, :] += tn(scores_back, query)
                dv_acc[keys, :] += tn(low, delta_head)
        for block in range(4):
            rows = slice(block * HALF, block * HALF + HALF)
            places = slice((block % 2) * HALF, (block % 2) * HALF + HALF)
            key_rows = slice(KEY_PLACE[block] * HALF, KEY_PLACE[block] * HALF + HALF)
            cosine, sine = cos_ref[places, :], sin_ref[places, :]
            grad = query_grads[block] * score_scale
            dq_ref[rows, cols] = (grad * cosine - swap_halves(grad) * sine).astype(bf16)
            grad = dk_acc[key_rows, :]
            dk_ref[rows, cols] = (grad * cosine - swap_halves(grad) * sine).astype(bf16)
            dv_ref[rows, cols] = dv_acc[key_rows, :].astype(bf16)

    for block in range(2):
        rows = slice(block * 256, block * 256 + 256)
        part_ref[rows, :] = (
            nt(dq_ref[rows, :], wq_ref[...]) + nt(dk_ref[rows, :], wk_ref[...]) + nt(dv_ref[rows, :], wv_ref[...])
        )
    gq_ref[...] = tn(normed_ref[...], dq_ref[...])
    gk_ref[...] = tn(normed_ref[...], dk_ref[...])
    gv_ref[...] = tn(normed_ref[...], dv_ref[...])

    out_rows, in_rows = heads_cols // GROUP, normed_ref.shape[1] // GROUP
    half_rows = in_rows // 2
    for p, order in enumerate(ORDERS_ATT):
        for place in range(GROUP):
            block = me ^ pack(order, place)
            out = outs[2 * p + (place >= 8)]
            spot = place % 8
            out[spot, 0:out_rows, :] = go_ref[
                pl.ds(pl.multiple_of(block * out_rows, 8), out_rows), p * heads_cols : (p + 1) * heads_cols
            ]
            source = (gq_ref, gk_ref)[p]
            out[spot, out_rows : out_rows + in_rows, :] = source[pl.ds(pl.multiple_of(block * in_rows, 8), in_rows), :]
            out[spot, out_rows + in_rows : out_rows + in_rows + half_rows, :] = gv_ref[
                pl.ds(pl.multiple_of(block * in_rows + p * half_rows, 8), half_rows), :
            ]


def input_kernel(mine_ref, theirs_ref, x_ref, gain_ref, delta_ref, grad_ref, gnorm_ref):
    gnorm_ref[...] = jnp.zeros_like(gnorm_ref)

    @pl.loop(0, x_ref.shape[0] // 64)
    def _(i):
        rows = pl.ds(pl.multiple_of(i * 64, 64), 64)
        delta = mine_ref[rows, :] + theirs_ref[rows, :]
        back, gain_part = norm_back_rows(x_ref[rows, :].astype(f32), gain_ref[...], delta)
        grad_ref[rows, :] = (delta_ref[rows, :] + back).astype(bf16)
        gnorm_ref[...] += gain_part


def unpack_mlp_kernel(*refs):
    *ins, gd_ref, gu_ref = refs
    me = lax.axis_index("dp") % GROUP
    width = gd_ref.shape[1]
    units = gu_ref.shape[1]
    down_rows, up_rows = units // GROUP, width // GROUP
    part_cols = width // len(ORDERS_MLP)
    for p, order in enumerate(ORDERS_MLP):
        for place in range(GROUP):
            block = me ^ pack(order, place)
            source = ins[2 * p + (place >= 8)]
            spot = place % 8
            gd_ref[pl.ds(pl.multiple_of(block * down_rows, 8), down_rows), p * part_cols : (p + 1) * part_cols] = source[
                spot, 0:down_rows, :
            ]
            for half in range(units // width):
                start = half * width + p * part_cols
                at = down_rows + half * up_rows
                gu_ref[pl.ds(pl.multiple_of(block * up_rows, 8), up_rows), start : start + part_cols] = source[
                    spot, at : at + up_rows, :
                ]


def unpack_att_kernel(*refs):
    *ins, go_ref, gq_ref, gk_ref, gv_ref = refs
    me = lax.axis_index("dp") % GROUP
    heads_cols = gq_ref.shape[1]
    out_rows, in_rows = heads_cols // GROUP, gq_ref.shape[0] // GROUP
    half_rows = in_rows // 2
    for p, order in enumerate(ORDERS_ATT):
        for place in range(GROUP):
            block = me ^ pack(order, place)
            source = ins[2 * p + (place >= 8)]
            spot = place % 8
            go_ref[pl.ds(pl.multiple_of(block * out_rows, 8), out_rows), p * heads_cols : (p + 1) * heads_cols] = source[
                spot, 0:out_rows, :
            ]
            target = (gq_ref, gk_ref)[p]
            target[pl.ds(pl.multiple_of(block * in_rows, 8), in_rows), :] = source[spot, out_rows : out_rows + in_rows, :]
            gv_ref[pl.ds(pl.multiple_of(block * in_rows + p * half_rows, 8), half_rows), :] = source[
                spot, out_rows + in_rows : out_rows + in_rows + half_rows, :
            ]


VMEM = pl.BlockSpec(memory_space=pltpu.VMEM)
SMEM = pl.BlockSpec(memory_space=pltpu.SMEM)


def call(kernel, ins, outs, scratch=(), flops=0, limit=48, smem=0):
    shapes = [jax.ShapeDtypeStruct(shape, dtype) for shape, dtype in outs]
    moved = sum(math.prod(a.shape) * a.dtype.itemsize for a in list(ins) + shapes)
    return pl.pallas_call(
        kernel,
        out_shape=shapes,
        in_specs=[SMEM] * smem + [VMEM] * (len(ins) - smem),
        out_specs=[VMEM] * len(outs),
        scratch_shapes=[pltpu.VMEM(shape, dtype) for shape, dtype in scratch],
        compiler_params=pltpu.CompilerParams(vmem_limit_bytes=limit * 1024 * 1024),
        cost_estimate=pl.CostEstimate(flops=flops, bytes_accessed=moved, transcendentals=0),
    )(*ins)


def on_device(
    count,
    inputs, norm_attn, w_query, w_key, w_value, w_out, norm_mlp, w_up, b_up, w_down, b_down, cotangent,
    doc_lengths, pad_counts,
):
    rows, width = inputs.shape
    heads_cols = w_query.shape[1]
    units = w_up.shape[1]
    heads = heads_cols // HEAD
    cosine, sine = (jnp.asarray(t) for t in rope_tables())
    gain_attn, gain_mlp = norm_attn.reshape(1, -1), norm_mlp.reshape(1, -1)

    def swap(values):
        return lax.ppermute(values, "mp", [(0, 1), (1, 0)])

    def flip(values, bit):
        return lax.ppermute(values, "dp", [(i, i ^ bit) for i in range(count)])

    def across(values):
        if count == GROUP:
            return values
        groups = [[g * GROUP + j for g in range(count // GROUP)] for j in range(GROUP)]
        return lax.psum(values, "dp", axis_index_groups=groups)

    normed, q, k, v, attended, probs, part = call(
        attention_forward,
        [doc_lengths, pad_counts, inputs, gain_attn, w_query, w_key, w_value, w_out, cosine, sine],
        [
            ((rows, width), bf16),
            ((rows, heads_cols), bf16),
            ((rows, heads_cols), bf16),
            ((rows, heads_cols), bf16),
            ((rows, heads_cols), bf16),
            ((heads, HALF, 8 * LANES), bf16),
            ((rows, width), f32),
        ],
        [((HALF, 8 * LANES), f32)],
        flops=2 * rows * width * heads_cols * 4,
        smem=2,
    )
    part_other = swap(part)

    n_mlp = len(ORDERS_MLP)
    slot_rows = units // GROUP + (units // width) * (width // GROUP)
    portion = ((8, slot_rows, width // n_mlp), f32)
    residual, normed_mlp, act, du, grad_bu, grad_bd, *mlp_parts = call(
        mlp_kernel,
        [inputs, part, part_other, gain_mlp, w_up, b_up.reshape(1, -1), w_down, cotangent],
        [
            ((rows, width), f32),
            ((rows, width), bf16),
            ((rows, units), bf16),
            ((rows, units), bf16),
            ((1, units), f32),
            ((1, width), f32),
        ]
        + [portion] * (2 * n_mlp),
        [((units, width), f32), ((width, units), f32)],
        flops=2 * rows * width * units * 4,
        limit=56,
    )

    def scatter(keep, send, order):
        for step, bit in enumerate(order):
            got = flip(send, bit)
            if step == 3:
                return keep + got
            half = keep.shape[0] // 2
            send = keep[half:] + got[half:]
            keep = keep[:half] + got[:half]

    def gather(own, order):
        for step, bit in enumerate(reversed(order)):
            got = flip(own, bit)
            if step == 3:
                return own, got
            own = jnp.concatenate([own, got], 0)

    delta_part, out_part = call(
        mlp_tail_kernel,
        [act, du, w_up, w_down],
        [((rows, width), f32), ((rows, width), f32)],
        flops=2 * rows * width * units * 2,
    )
    delta_other, out_other = swap(delta_part), swap(out_part)

    n_att = len(ORDERS_ATT)
    slot_rows = heads_cols // GROUP + (width // GROUP) * 3 // 2
    portion = ((8, slot_rows, heads_cols), f32)
    delta_residual, grad_norm_mlp, normed_part, *att_parts = call(
        attention_backward,
        [
            delta_part, delta_other, residual, gain_mlp, cotangent, attended, w_out, q, k, v, probs,
            normed, w_query, w_key, w_value, cosine, sine,
        ],
        [((rows, width), f32), ((1, width), f32), ((rows, width), f32)] + [portion] * (2 * n_att),
        [
            ((rows, width), bf16),
            ((rows, heads_cols), bf16),
            ((rows, heads_cols), bf16),
            ((rows, heads_cols), bf16),
            ((rows, heads_cols), bf16),
            ((rows, LANES), f32),
            ((rows, LANES), f32),
            ((heads_cols, width), f32),
            ((width, heads_cols), f32),
            ((width, heads_cols), f32),
            ((width, heads_cols), f32),
        ],
        flops=2 * rows * width * heads_cols * 10,
    )
    normed_other = swap(normed_part)
    grad_inputs, grad_norm_attn = call(
        input_kernel,
        [normed_part, normed_other, inputs, gain_attn, delta_residual],
        [((rows, width), bf16), ((1, width), f32)],
    )
    output = (residual + (out_part + out_other) + b_down).astype(bf16)

    mlp_own = [across(scatter(mlp_parts[2 * p], mlp_parts[2 * p + 1], order)) for p, order in enumerate(ORDERS_MLP)]
    mlp_all = [a for own, order in zip(mlp_own, ORDERS_MLP) for a in gather(own, order)]
    att_own = [across(scatter(att_parts[2 * p], att_parts[2 * p + 1], order)) for p, order in enumerate(ORDERS_ATT)]
    att_all = [a for own, order in zip(att_own, ORDERS_ATT) for a in gather(own, order)]

    vectors = jnp.concatenate([grad_norm_attn, grad_norm_mlp, grad_bd, grad_bu], 1)
    for bit in (X, Y, Z1, Z2):
        vectors = vectors + flip(vectors, bit)
    vectors = across(vectors)[0]

    grad_down, grad_up = call(unpack_mlp_kernel, mlp_all, [((units, width), f32), ((width, units), f32)])
    grad_out, grad_query, grad_key, grad_value = call(
        unpack_att_kernel,
        att_all,
        [((heads_cols, width), f32), ((width, heads_cols), f32), ((width, heads_cols), f32), ((width, heads_cols), f32)],
    )
    return (
        output,
        grad_inputs,
        vectors[:width],
        grad_query,
        grad_key,
        grad_value,
        grad_out,
        vectors[width : 2 * width],
        grad_up,
        vectors[3 * width :],
        grad_down,
        vectors[2 * width : 3 * width],
    )


def solution(mesh):
    count = mesh.shape["dp"]

    def step(*args):
        return on_device(count, *args)

    return jax.shard_map(
        step,
        mesh=mesh,
        in_specs=(
            P("dp", None),
            P(),
            P(None, "mp"),
            P(None, "mp"),
            P(None, "mp"),
            P("mp", None),
            P(),
            P(None, "mp"),
            P("mp"),
            P("mp", None),
            P(),
            P("dp", None),
            P(),
            P(),
        ),
        out_specs=(
            P("dp", None),
            P("dp", None),
            P(),
            P(None, "mp"),
            P(None, "mp"),
            P(None, "mp"),
            P("mp", None),
            P(),
            P(None, "mp"),
            P("mp"),
            P("mp", None),
            P(),
        ),
        check_vma=False,
    )
```

```python
from functools import partial
import math

import numpy as np

import jax
import jax.numpy as jnp
from jax import lax
from jax.experimental import pallas as pl
from jax.experimental.pallas import tpu as pltpu
from jax.sharding import PartitionSpec as P

HEAD = 64
BLOCK = 16
LEN = 256
HALF = 128
LANES = 128
PLANE = 4
STACK = 4
GROUP = PLANE * STACK

norm_eps = 1e-05
rope_base = 10000.0
masked_score = -1e30
score_scale = HEAD ** (-0.5)
bf16 = jnp.bfloat16
f32 = jnp.float32

X, Y, Z1, Z2 = 1, 2, 4, 8
FIRST, SECOND = (X, Y), (Y, X)
Z_SLOTS = (0, 2, 1, 3)

ORDER = "dPcuTdcKcdudIuacbdudabudbudbcacbuabuabcabacdacuba"

CASES = ((0, 0, 256, 0), (128, 256, 384, 128), (256, 640, 128, 128), (384, 768, 256, 128))
TILES = (
    (0, 0, 0, 0),
    (0, 1, 0, 0),
    (0, 1, 128, 0),
    (0, 1, 128, 128),
    (0, 0, 128, 128),
    (1, 1, 0, 0),
    (1, 1, 128, 0),
    (1, 1, 128, 128),
)
KEY_PLACE = (0, 3, 1, 2)


def mm(left, right):
    return jnp.dot(left, right, preferred_element_type=f32)


def tn(left, right):
    return lax.dot_general(left, right, (((0,), (0,)), ((), ())), preferred_element_type=f32)


def nt(left, right):
    return lax.dot_general(left, right, (((1,), (1,)), ((), ())), preferred_element_type=f32)


def rope_tables():
    half = HEAD // 2
    frequency = np.exp(np.arange(half) * (-2.0 * math.log(rope_base) / HEAD)).astype(np.float32)
    turn = (np.arange(LEN, dtype=np.float32)[:, None] * frequency[None, :]).astype(np.float32)
    cosine, sine = np.cos(turn.astype(np.float64)), np.sin(turn.astype(np.float64))
    cosine = np.tile(cosine, (1, LANES // half)).astype(np.float32)
    sine = np.tile(np.concatenate([-sine, sine], 1), (1, LANES // HEAD)).astype(np.float32)
    return cosine, sine


def swap_halves(values):
    lane = lax.broadcasted_iota(jnp.int32, values.shape, 1)
    return jnp.where(
        lane % HEAD < HEAD // 2, pltpu.roll(values, LANES - HEAD // 2, 1), pltpu.roll(values, HEAD // 2, 1)
    )


def head_mask(rows, which):
    lane = lax.broadcasted_iota(jnp.int32, (rows, LANES), 1)
    return (lane >= HEAD) if which else (lane < HEAD)


def layer_norm_rows(values, gain):
    centred = values - jnp.mean(values, axis=-1, keepdims=True)
    spread = jnp.mean(centred * centred, axis=-1, keepdims=True)
    return centred * lax.rsqrt(spread + norm_eps) * gain


def scaled_rows(values):
    centred = values - jnp.mean(values, axis=-1, keepdims=True)
    return centred * lax.rsqrt(jnp.mean(centred * centred, axis=-1, keepdims=True) + norm_eps)


def norm_back_rows(values, gain, delta):
    centred = values - jnp.mean(values, axis=-1, keepdims=True)
    spread = jnp.mean(centred * centred, axis=-1, keepdims=True)
    s = lax.rsqrt(spread + norm_eps)
    xhat = centred * s
    e = delta * gain
    back = s * (e - jnp.mean(e, axis=-1, keepdims=True) - xhat * jnp.mean(e * xhat, axis=-1, keepdims=True))
    return back, jnp.sum(delta * xhat, axis=0, keepdims=True)


def fill_bias(lengths_ref, pads_ref, bias_ref):
    sequence = lax.axis_index("dp")
    docs = lengths_ref.shape[1]
    ends, total = [], jnp.int32(0)
    for j in range(docs):
        total = total + lengths_ref[sequence, j]
        ends.append(total)
    first_pad = LEN - pads_ref[sequence]

    def segment(places):
        seg = jnp.zeros(places.shape, jnp.int32)
        for end in ends:
            seg = seg + (places >= end).astype(jnp.int32)
        return seg

    rows, cols, row_seg, col_seg = {}, {}, {}, {}
    for base in (0, HALF):
        rows[base] = lax.broadcasted_iota(jnp.int32, (HALF, LANES), 0) + base
        cols[base] = lax.broadcasted_iota(jnp.int32, (HALF, LANES), 1) + base
        row_seg[base] = segment(rows[base])
        col_seg[base] = segment(cols[base])
    for tile, (query_kind, key_kind, query_base, key_base) in enumerate(TILES):
        q, k = rows[query_base], cols[key_base]
        query_block, key_block = q // BLOCK, k // BLOCK
        same_doc = (row_seg[query_base] == col_seg[key_base]) & (k < first_pad)
        if query_kind == 0 and key_kind == 0:
            ok = (key_block == query_block) & (same_doc | (q == k))
        elif query_kind == 0:
            ok = (key_block < query_block) & same_doc
        else:
            ok = (key_block <= query_block) & (same_doc | (q == k))
        bias_ref[:, tile * LANES : (tile + 1) * LANES] = jnp.where(ok, 0.0, masked_score)


def fetch(pairs, sems):
    copies = [pltpu.make_async_copy(source, target, sems.at[i]) for i, (source, target) in enumerate(pairs)]
    for copy in copies:
        copy.start()
    return copies


def attention_forward(
    lengths_ref, pads_ref, gain_ref, x_in, wq_in, wk_in, wv_in, cos_in, sin_in, wo_in,
    normed_ref, q_ref, k_ref, v_ref, att_ref, prob_ref, part_ref,
    bias_ref, x_ref, wq_ref, wk_ref, wv_ref, cos_ref, sin_ref, wo_ref, sems,
):
    copies = fetch(
        (
            (x_in, x_ref), (wq_in, wq_ref), (wk_in, wk_ref), (wv_in, wv_ref),
            (cos_in, cos_ref), (sin_in, sin_ref), (wo_in, wo_ref),
        ),
        sems,
    )
    heads_cols = wq_ref.shape[1]
    pairs = heads_cols // LANES
    fill_bias(lengths_ref, pads_ref, bias_ref)
    copies[0].wait()

    @pl.loop(0, x_ref.shape[0] // 64)
    def _(i):
        rows = pl.ds(pl.multiple_of(i * 64, 64), 64)
        normed_ref[rows, :] = layer_norm_rows(x_ref[rows, :].astype(f32), gain_ref[...]).astype(bf16)

    for copy in copies[1:6]:
        copy.wait()
    for block in range(4):
        rows = slice(block * HALF, block * HALF + HALF)
        places = slice((block % 2) * HALF, (block % 2) * HALF + HALF)
        key_rows = slice(KEY_PLACE[block] * HALF, KEY_PLACE[block] * HALF + HALF)
        normed = normed_ref[rows, :]
        cosine, sine = cos_ref[places, :], sin_ref[places, :]
        query, key = mm(normed, wq_ref[...]), mm(normed, wk_ref[...])
        for t in range(pairs):
            cols = slice(t * LANES, (t + 1) * LANES)
            turned = query[:, cols] * cosine + swap_halves(query[:, cols]) * sine
            q_ref[rows, cols] = (turned.astype(bf16).astype(f32) * score_scale).astype(bf16)
            turned = key[:, cols] * cosine + swap_halves(key[:, cols]) * sine
            k_ref[key_rows, cols] = turned.astype(bf16)
        v_ref[key_rows, :] = mm(normed, wv_ref[...]).astype(bf16)

    for t in range(pairs):
        cols = slice(t * LANES, (t + 1) * LANES)
        key_pair, value_pair = k_ref[:, cols], v_ref[:, cols]
        mixed = [None] * 4
        for which in range(2):
            mask = head_mask(key_pair.shape[0], which)
            key_head = jnp.where(mask, key_pair, jnp.zeros_like(key_pair))
            value_head = jnp.where(mask, value_pair, jnp.zeros_like(value_pair))
            for case, (query_row, first, width, key_row) in enumerate(CASES):
                scores = nt(q_ref[query_row : query_row + HALF, cols], key_head[key_row : key_row + width])
                scores = scores + bias_ref[:, first : first + width]
                weights = jnp.exp(scores - jnp.max(scores, axis=1, keepdims=True))
                low = (weights * (1.0 / jnp.sum(weights, axis=1, keepdims=True))).astype(bf16)
                prob_ref[2 * t + which, :, first : first + width] = low
                part = mm(low, value_head[key_row : key_row + width])
                mixed[case] = part if mixed[case] is None else mixed[case] + part
        for case, (query_row, _, _, _) in enumerate(CASES):
            att_ref[query_row : query_row + HALF, cols] = mixed[case].astype(bf16)

    copies[6].wait()
    for block in range(2):
        rows = slice(block * 256, block * 256 + 256)
        part_ref[rows, :] = mm(att_ref[rows, :], wo_ref[...])


def fourths(start, part):
    return pl.ds(pl.multiple_of(start * part, 8), part)


def z_place(me, block):
    relative = (me // PLANE) ^ block
    return (relative % 2) * 2 + relative // 2


def quarter_at(place):
    core = lax.axis_index("mp") % 2
    slot = (place // 2) * (X + core) + (place % 2) * (Y - core)
    return lax.axis_index("dp") % PLANE ^ slot


def place_quarter(outs, place, value):
    me = lax.axis_index("dp") % GROUP
    part = value.shape[0] // STACK
    for block in range(STACK):
        outs[place // 2][place % 2, z_place(me, block)] = value[block * part : (block + 1) * part]


def place_quarter_z_first(outs, place, value):
    me = lax.axis_index("dp") % GROUP
    part = value.shape[0] // STACK
    for block in range(STACK):
        z = z_place(me, block)
        for sent in range(2):

            @pl.when(z // 2 == sent)
            def _(out=outs[sent], z=z, piece=value[block * part : (block + 1) * part]):
                out[z % 2, place] = piece


def mlp_kernel(
    gain_ref, bu_ref, mine_ref, theirs_ref, x_in, wu_in, wd_in, cot_in,
    residual_ref, normed_ref, act_ref, du_ref, gbu_ref, gbd_ref, *outs_and_scratch,
):
    *outs, x_ref, wu_ref, wd_ref, cot_ref, sems = outs_and_scratch
    copies = fetch(((x_in, x_ref), (cot_in, cot_ref), (wu_in, wu_ref), (wd_in, wd_ref)), sems)
    row_count = x_ref.shape[0]
    units = wu_ref.shape[1]
    gbu_ref[...] = jnp.zeros_like(gbu_ref)
    gbd_ref[...] = jnp.zeros_like(gbd_ref)
    copies[0].wait()
    copies[1].wait()

    @pl.loop(0, row_count // 64)
    def _(i):
        rows = pl.ds(pl.multiple_of(i * 64, 64), 64)
        residual = x_ref[rows, :].astype(f32) + (mine_ref[rows, :] + theirs_ref[rows, :])
        residual_ref[rows, :] = residual
        normed_ref[rows, :] = layer_norm_rows(residual, gain_ref[...]).astype(bf16)
        gbd_ref[...] += jnp.sum(cot_ref[rows, :].astype(f32), axis=0, keepdims=True)

    copies[2].wait()
    copies[3].wait()
    c0 = math.sqrt(2.0 / math.pi)
    c1 = c0 * 0.044715

    @pl.loop(0, units // 256)
    def _(j):
        cols = pl.ds(pl.multiple_of(j * 256, 256), 256)
        for block in range(row_count // 256):
            rows = slice(block * 256, block * 256 + 256)
            u = mm(normed_ref[rows, :], wu_ref[:, cols]) + bu_ref[:, cols]
            delta = nt(cot_ref[rows, :], wd_ref[cols, :])
            square = u * u
            t = jnp.tanh(u * (c0 + c1 * square))
            half_up = 0.5 * (1.0 + t)
            act_ref[rows, cols] = (u * half_up).astype(bf16)
            slope = half_up + (0.5 * u) * (1.0 - t * t) * (c0 + (3.0 * c1) * square)
            low = (delta * slope).astype(bf16)
            du_ref[rows, cols] = low
            gbu_ref[:, cols] += jnp.sum(low.astype(f32), axis=0, keepdims=True)

    quarter = units // PLANE
    cut = cot_ref.shape[1] * 2 // 3
    for place in range(PLANE):
        cols = pl.ds(pl.multiple_of(quarter_at(place) * quarter, LANES), quarter)
        grad = tn(act_ref[:, cols], cot_ref[...])
        place_quarter(outs[:2], place, grad[:, :cut])
        place_quarter_z_first(outs[2:], place, grad[:, cut:])


def up_kernel(normed_ref, du_ref, *outs):
    quarter = du_ref.shape[1] // PLANE
    for place in range(PLANE):
        cols = pl.ds(pl.multiple_of(quarter_at(place) * quarter, LANES), quarter)
        place_quarter(outs, place, tn(normed_ref[...], du_ref[:, cols]))


def tail_kernel(act_ref, du_ref, wu_ref, wd_ref, out_ref):
    for block in range(act_ref.shape[0] // 256):
        rows = slice(block * 256, block * 256 + 256)
        out_ref[0, rows, :] = nt(du_ref[rows, :], wu_ref[...])
        out_ref[1, rows, :] = mm(act_ref[rows, :], wd_ref[...])


def attention_backward(
    mine_ref, theirs_ref, residual_ref, gain_ref, cot_ref, att_ref, wo_ref, q_ref, k_ref, v_ref, prob_ref,
    normed_ref, wq_ref, wk_ref, wv_ref, cos_ref, sin_ref, x_ref, bd_ref, gbd_ref, gbu_ref,
    output_ref, delta_ref, vec_ref, part_ref, *outs_and_scratch,
):
    *outs, branch_ref, datt_ref, dq_ref, dk_ref, dv_ref, dk_acc, dv_acc, grads_ref, gnorm_ref = outs_and_scratch
    row_count = residual_ref.shape[0]
    heads_cols = wq_ref.shape[1]
    pairs = heads_cols // LANES
    gnorm_ref[...] = jnp.zeros_like(gnorm_ref)

    @pl.loop(0, row_count // 64)
    def _(i):
        rows = pl.ds(pl.multiple_of(i * 64, 64), 64)
        delta = mine_ref[0, rows, :] + theirs_ref[0, rows, :]
        residual = residual_ref[rows, :]
        output_ref[rows, :] = (residual + (mine_ref[1, rows, :] + theirs_ref[1, rows, :]) + bd_ref[...]).astype(bf16)
        back, gain_part = norm_back_rows(residual, gain_ref[...], delta)
        back = back + cot_ref[rows, :].astype(f32)
        delta_ref[rows, :] = back
        branch_ref[rows, :] = back.astype(bf16)
        gnorm_ref[0:1, :] += gain_part

    for block in range(2):
        rows = slice(block * 256, block * 256 + 256)
        datt_ref[rows, :] = nt(branch_ref[rows, :], wo_ref[...]).astype(bf16)
    half = heads_cols
    grad = tn(att_ref[...], branch_ref[...])
    grads_ref[0, 0], grads_ref[0, 1] = grad[:, :half], grad[:, half:]

    for t in range(pairs):
        cols = slice(t * LANES, (t + 1) * LANES)
        key_pair, value_pair = k_ref[:, cols], v_ref[:, cols]
        dk_acc[...] = jnp.zeros_like(dk_acc)
        dv_acc[...] = jnp.zeros_like(dv_acc)
        query_grads = [None] * 4
        for which in range(2):
            mask = head_mask(key_pair.shape[0], which)
            key_head = jnp.where(mask, key_pair, jnp.zeros_like(key_pair))
            value_head = jnp.where(mask, value_pair, jnp.zeros_like(value_pair))
            small = head_mask(HALF, which)
            for case, (query_row, first, width, key_row) in enumerate(CASES):
                rows = slice(query_row, query_row + HALF)
                keys = slice(key_row, key_row + width)
                low = prob_ref[2 * t + which, :, first : first + width]
                wide = low.astype(f32)
                delta_head = datt_ref[rows, cols]
                g = nt(delta_head, value_head[keys])
                weighted = wide * g
                scores_back = (weighted - wide * jnp.sum(weighted, axis=1, keepdims=True)).astype(bf16)
                part = mm(scores_back, key_head[keys])
                query_grads[case] = part if query_grads[case] is None else query_grads[case] + part
                query = q_ref[rows, cols]
                query = jnp.where(small, query, jnp.zeros_like(query))
                delta_head = jnp.where(small, delta_head, jnp.zeros_like(delta_head))
                dk_acc[keys, :] += tn(scores_back, query)
                dv_acc[keys, :] += tn(low, delta_head)
        for block in range(4):
            rows = slice(block * HALF, block * HALF + HALF)
            places = slice((block % 2) * HALF, (block % 2) * HALF + HALF)
            key_rows = slice(KEY_PLACE[block] * HALF, KEY_PLACE[block] * HALF + HALF)
            cosine, sine = cos_ref[places, :], sin_ref[places, :]
            grad = query_grads[block] * score_scale
            dq_ref[rows, cols] = (grad * cosine - swap_halves(grad) * sine).astype(bf16)
            grad = dk_acc[key_rows, :]
            dk_ref[rows, cols] = (grad * cosine - swap_halves(grad) * sine).astype(bf16)
            dv_ref[rows, cols] = dv_acc[key_rows, :].astype(bf16)

    for block in range(2):
        rows = slice(block * 256, block * 256 + 256)
        part_ref[rows, :] = (
            nt(dq_ref[rows, :], wq_ref[...]) + nt(dk_ref[rows, :], wk_ref[...]) + nt(dv_ref[rows, :], wv_ref[...])
        )

    @pl.loop(0, row_count // 64)
    def _(i):
        rows = pl.ds(pl.multiple_of(i * 64, 64), 64)
        gnorm_ref[1:2, :] += jnp.sum(part_ref[rows, :] * scaled_rows(x_ref[rows, :].astype(f32)), axis=0, keepdims=True)

    vec_ref[...] = jnp.zeros_like(vec_ref)
    row = 0
    once = jnp.where(lax.axis_index("mp") == 0, 1.0, 0.0)
    for values in (gnorm_ref[1:2, :], gnorm_ref[0:1, :] * once, gbd_ref[...] * once, gbu_ref[...]):
        for first in range(0, values.shape[1], half):
            vec_ref[row : row + 1, :] = values[:, first : first + half]
            row += 1

    for matrix, grad_rows in ((1, dq_ref), (2, dk_ref), (3, dv_ref)):
        grad = tn(normed_ref[...], grad_rows[...])
        grads_ref[matrix, 0], grads_ref[matrix, 1] = grad[:half], grad[half:]
    for place in range(PLANE):
        quarter = quarter_at(place)
        place_quarter(outs[:2], place, grads_ref[quarter, 0])
        place_quarter(outs[2:], place, grads_ref[quarter, 1])


def input_kernel(mine_ref, theirs_ref, x_ref, gain_ref, delta_ref, grad_ref):
    @pl.loop(0, x_ref.shape[0] // 64)
    def _(i):
        rows = pl.ds(pl.multiple_of(i * 64, 64), 64)
        delta = mine_ref[rows, :] + theirs_ref[rows, :]
        back, _ = norm_back_rows(x_ref[rows, :].astype(f32), gain_ref[...], delta)
        grad_ref[rows, :] = (delta_ref[rows, :] + back).astype(bf16)


def each_block(own_ref, got_ref, put, z_first=False):
    me = lax.axis_index("dp") % GROUP
    for place in range(PLANE):
        for z in range(STACK):
            first, second = (z, place) if z_first else (place, z)
            value = (got_ref if first // 2 else own_ref)[first % 2, second]
            put(quarter_at(place), me // PLANE ^ Z_SLOTS[z], value)


def unpack_down(own_ref, got_ref, z_own_ref, z_got_ref, out_ref):
    cut = own_ref.shape[-1]

    def put(quarter, fourth, value):
        cols = slice(0, cut) if value.shape[1] == cut else slice(cut, None)
        out_ref[fourths(quarter * STACK + fourth, value.shape[0]), cols] = value

    each_block(own_ref, got_ref, put)
    each_block(z_own_ref, z_got_ref, put, True)


def unpack_up(own_ref, got_ref, out_ref):
    def put(quarter, fourth, value):
        part, cols = value.shape
        out_ref[fourths(fourth, part), pl.ds(pl.multiple_of(quarter * cols, LANES), cols)] = value

    each_block(own_ref, got_ref, put)


def unpack_attention(own_a, got_a, own_b, got_b, *outs):
    grads_ref = outs[4]
    for portion, (own_ref, got_ref) in enumerate(((own_a, got_a), (own_b, got_b))):

        def put(quarter, fourth, value, portion=portion):
            grads_ref[quarter, portion, fourths(fourth, value.shape[0])] = value

        each_block(own_ref, got_ref, put)
    finish_att(outs)


def finish_att(outs):
    *outs, grads_ref, sems = outs
    half = grads_ref.shape[-1]
    copies = []
    for matrix, out in enumerate(outs):
        for portion in range(2):
            place = pl.ds(portion * half, half)
            target = out.at[place, :] if matrix else out.at[:, place]
            copies.append((grads_ref.at[matrix, portion], target))
    for copy in fetch(copies, sems):
        copy.wait()


VMEM = pl.BlockSpec(memory_space=pltpu.VMEM)
SMEM = pl.BlockSpec(memory_space=pltpu.SMEM)
HBM = pl.BlockSpec(memory_space=pltpu.HBM)


def call(kernel, outs, scalars=(), held=(), loose=(), scratch=(), flops=0, limit=40, out_space=VMEM):
    ins = [*scalars, *held, *loose]
    shapes = [jax.ShapeDtypeStruct(shape, dtype) for shape, dtype in outs]
    moved = sum(math.prod(a.shape) * a.dtype.itemsize for a in ins + shapes)
    return pl.pallas_call(
        kernel,
        name=getattr(kernel, "__name__", "unpack_kernel"),
        out_shape=shapes,
        in_specs=[SMEM] * len(scalars) + [VMEM] * len(held) + [HBM] * len(loose),
        out_specs=[out_space] * len(outs),
        scratch_shapes=[s if not isinstance(s, tuple) else pltpu.VMEM(*s) for s in scratch],
        compiler_params=pltpu.CompilerParams(vmem_limit_bytes=limit * 1024 * 1024),
        cost_estimate=pl.CostEstimate(flops=flops, bytes_accessed=moved, transcendentals=0),
    )(*ins)


def on_device(
    count,
    inputs, norm_attn, w_query, w_key, w_value, w_out, norm_mlp, w_up, b_up, w_down, b_down, cotangent,
    doc_lengths, pad_counts,
):
    rows, width = inputs.shape
    heads_cols = w_query.shape[1]
    units = w_up.shape[1]
    heads = heads_cols // HEAD
    cosine, sine = (jnp.asarray(t) for t in rope_tables())
    gain_attn, gain_mlp = norm_attn.reshape(1, -1), norm_mlp.reshape(1, -1)

    def swap(values):
        return lax.ppermute(values, "mp", [(0, 1), (1, 0)])

    def flip(values, bits, name):
        pairs = [(2 * i + core, 2 * (i ^ bits[core]) + core) for i in range(count) for core in range(2)]
        with jax.named_scope(name):
            return lax.ppermute(values, ("dp", "mp"), pairs)

    def sems(n):
        return pltpu.SemaphoreType.DMA((n,))

    half = heads_cols

    def portions(*shape):
        return [((2, STACK) + shape, f32)] * 2

    last = []

    def turn(*values):
        if not last:
            return values
        values, _ = lax.optimization_barrier((values, last.pop()))
        return values

    def did(value):
        last[:] = [value]
        return value

    def over_groups(values):
        if count == GROUP:
            return values
        groups = [[k * GROUP + j for k in range(count // GROUP)] for j in range(GROUP)]
        return lax.psum(values, "dp", axis_index_groups=groups)

    def chain(name, parts, result, z_first=False, vec=None):
        keep, send = parts
        plane, stack = [(FIRST, "first"), (SECOND, "second")], [((Z1, Z1), "z1"), ((Z2, Z2), "z2")]
        steps = stack + plane if z_first else plane + stack

        def join(values):
            return values if vec is None else jnp.concatenate([values.reshape(-1, values.shape[-1]), vec], 0)

        def part_of(got, like, vec):
            if vec is None:
                return got, None
            return got[: -vec.shape[0]].reshape(like.shape), vec + got[-vec.shape[0] :]

        for step, (bits, label) in enumerate(steps):
            if step:
                keep, got, vec = turn(keep, got, vec)
                got, vec = part_of(got, keep, vec)
                cut = keep.shape[0] // 2
                send, keep = keep[cut:] + got[cut:], keep[:cut] + got[:cut]
                if step == 1:
                    keep, send = keep[0], send[0]
                send = did(join(send))
            else:
                send = join(send)
            got = flip(send, bits, f"{name}_sum_{label}")
            yield
        keep, got, vec = turn(keep, got, vec)
        got, vec = part_of(got, keep, vec)
        own = over_groups(did(keep + got))
        if vec is not None:
            result.append(over_groups(vec))
        for step, (bits, label) in enumerate(reversed(steps)):
            got = flip(own, bits, f"{name}_gather_{label}")
            yield
            own, got = turn(own, got)
            if step < 3:
                own = did(jnp.stack([own, got]) if step == 2 else jnp.concatenate([own, got], 0))
        result.extend((own, got))
        yield

    normed, q, k, v, attended, probs, branch = call(
        attention_forward,
        [
            ((rows, width), bf16),
            ((rows, heads_cols), bf16),
            ((rows, heads_cols), bf16),
            ((rows, heads_cols), bf16),
            ((rows, heads_cols), bf16),
            ((heads, HALF, 8 * LANES), bf16),
            ((rows, width), f32),
        ],
        scalars=[doc_lengths, pad_counts],
        held=[gain_attn],
        loose=[inputs, w_query, w_key, w_value, cosine, sine, w_out],
        scratch=[
            ((HALF, 8 * LANES), f32),
            ((rows, width), bf16),
            ((width, heads_cols), bf16),
            ((width, heads_cols), bf16),
            ((width, heads_cols), bf16),
            (cosine.shape, f32),
            (sine.shape, f32),
            ((heads_cols, width), bf16),
            sems(7),
        ],
        flops=2 * rows * width * heads_cols * 4,
    )
    branch_other = swap(branch)

    residual, normed_mlp, act, du, grad_bu, grad_bd, *down_parts = call(
        mlp_kernel,
        [
            ((rows, width), f32),
            ((rows, width), bf16),
            ((rows, units), bf16),
            ((rows, units), bf16),
            ((1, units), f32),
            ((1, width), f32),
        ]
        + portions(units // GROUP, width * 2 // 3)
        + portions(units // GROUP, width // 3),
        held=[gain_mlp, b_up.reshape(1, -1), branch, branch_other],
        loose=[inputs, w_up, w_down, cotangent],
        scratch=[
            ((rows, width), bf16),
            ((width, units), bf16),
            ((units, width), bf16),
            ((rows, width), bf16),
            sems(4),
        ],
        flops=2 * rows * width * units * 3,
    )
    made, grads = {key: [] for key in "dcuab"}, {}
    chains = {"d": chain("down", down_parts[:2], made["d"]), "c": chain("down_stack", down_parts[2:], made["c"], True)}
    state = {}

    def tail():
        operands = turn(act, du)
        (state["shares"],) = call(
            tail_kernel, [((2, rows, width), f32)], held=[*operands, w_up, w_down], flops=2 * rows * width * units * 2
        )
        state["shares_other"] = swap(did(state["shares"]))

    def grad_up_parts():
        operands = turn(normed_mlp, du)
        parts = call(
            up_kernel,
            portions(width // STACK, units // PLANE),
            held=operands,
            flops=2 * rows * width * units,
        )
        did(parts[0])
        chains["u"] = chain("up", parts, made["u"])

    def backward():
        (shares_other,) = turn(state["shares_other"])
        state["output"], state["delta_residual"], vec, state["normed_part"], *parts = call(
            attention_backward,
            [((rows, width), bf16), ((rows, width), f32), ((16, half), f32), ((rows, width), f32)]
            + portions(half // STACK, half) * 2,
            held=[
                state["shares"], shares_other, residual, gain_mlp, cotangent, attended, w_out, q, k, v, probs,
                normed, w_query, w_key, w_value, cosine, sine, inputs, b_down.reshape(1, -1), grad_bd, grad_bu,
            ],
            scratch=[
                ((rows, width), bf16),
                ((rows, heads_cols), bf16),
                ((rows, heads_cols), bf16),
                ((rows, heads_cols), bf16),
                ((rows, heads_cols), bf16),
                ((rows, LANES), f32),
                ((rows, LANES), f32),
                ((PLANE, 2, half, half), f32),
                ((8, width), f32),
            ],
            flops=2 * rows * width * heads_cols * 10,
        )
        did(vec)
        state["normed_other"] = swap(state["normed_part"])
        chains["a"] = chain("attention", parts[:2], made["a"], vec=vec)
        chains["b"] = chain("attention_rest", parts[2:], made["b"])

    def input_back():
        (normed_other,) = turn(state["normed_other"])
        (state["grad_inputs"],) = call(
            input_kernel,
            [((rows, width), bf16)],
            held=[state["normed_part"], normed_other, inputs, gain_attn, state["delta_residual"]],
        )
        did(state["grad_inputs"])

    def unpack():
        if "down" not in grads and len(made["d"]) == len(made["c"]) == 2:
            grads["down"] = call(unpack_down, [((units, width), f32)], held=made["d"] + made["c"])
            did(grads["down"][0])
        if "up" not in grads and len(made["u"]) == 2:
            grads["up"] = call(unpack_up, [((width, units), f32)], held=made["u"])
            did(grads["up"][0])
        if "attention" not in grads and len(made["a"]) == 3 and len(made["b"]) == 2:
            grads["attention"] = call(
                unpack_attention,
                [((heads_cols, width), f32)] + [((width, heads_cols), f32)] * 3,
                held=made["a"][1:] + made["b"],
                scratch=[((PLANE, 2, half, half), f32), sems(8)],
                out_space=HBM,
            )

    did(grad_bd)
    pieces = {"T": tail, "P": grad_up_parts, "K": backward, "I": input_back}
    for key in ORDER:
        if key in pieces:
            pieces[key]()
        else:
            next(chains[key])
            unpack()
    assert len(grads) == 3

    vec = made["a"][0]
    n = width // half
    shared = (vec[: 3 * n] + swap(vec[: 3 * n])).reshape(3, width)
    grad_bu = vec[3 * n :].reshape(-1)[:units]
    (grad_down,), (grad_up,) = grads["down"], grads["up"]
    grad_out, grad_query, grad_key, grad_value = grads["attention"]
    output, grad_inputs = state["output"], state["grad_inputs"]
    return (
        output,
        grad_inputs,
        shared[0],
        grad_query,
        grad_key,
        grad_value,
        grad_out,
        shared[1],
        grad_up,
        grad_bu,
        grad_down,
        shared[2],
    )


def solution(mesh):
    count = mesh.shape["dp"]

    def step(*args):
        return on_device(count, *args)

    return jax.shard_map(
        step,
        mesh=mesh,
        in_specs=(
            P("dp", None),
            P(),
            P(None, "mp"),
            P(None, "mp"),
            P(None, "mp"),
            P("mp", None),
            P(),
            P(None, "mp"),
            P("mp"),
            P("mp", None),
            P(),
            P("dp", None),
            P(),
            P(),
        ),
        out_specs=(
            P("dp", None),
            P("dp", None),
            P(),
            P(None, "mp"),
            P(None, "mp"),
            P(None, "mp"),
            P("mp", None),
            P(),
            P(None, "mp"),
            P("mp"),
            P("mp", None),
            P(),
        ),
        check_vma=False,
    )
```

```python
from functools import partial
import math

import numpy as np

import jax
import jax.numpy as jnp
from jax import lax
from jax.experimental import pallas as pl
from jax.experimental.pallas import tpu as pltpu
from jax.sharding import PartitionSpec as P

HEAD = 64
BLOCK = 16
LEN = 256
HALF = 128
LANES = 128
PLANE = 4
STACK = 4
GROUP = PLANE * STACK

norm_eps = 1e-05
rope_base = 10000.0
masked_score = -1e30
score_scale = HEAD ** (-0.5)
bf16 = jnp.bfloat16
f32 = jnp.float32

X, Y, Z1, Z2 = 1, 2, 4, 8
FIRST, SECOND = (X, Y), (Y, X)
Z_SLOTS = (0, 2, 1, 3)

ORDER = "dcudcKcdudIuacbdudabudbudbcacbuabuabcabacdacuba"

CASES = ((0, 0, 256, 0), (128, 256, 384, 128), (256, 640, 128, 128), (384, 768, 256, 128))
TILES = (
    (0, 0, 0, 0),
    (0, 1, 0, 0),
    (0, 1, 128, 0),
    (0, 1, 128, 128),
    (0, 0, 128, 128),
    (1, 1, 0, 0),
    (1, 1, 128, 0),
    (1, 1, 128, 128),
)
KEY_PLACE = (0, 3, 1, 2)


def mm(left, right):
    return jnp.dot(left, right, preferred_element_type=f32)


def tn(left, right):
    return lax.dot_general(left, right, (((0,), (0,)), ((), ())), preferred_element_type=f32)


def nt(left, right):
    return lax.dot_general(left, right, (((1,), (1,)), ((), ())), preferred_element_type=f32)


def rope_tables():
    half = HEAD // 2
    frequency = np.exp(np.arange(half) * (-2.0 * math.log(rope_base) / HEAD)).astype(np.float32)
    turn = (np.arange(LEN, dtype=np.float32)[:, None] * frequency[None, :]).astype(np.float32)
    cosine, sine = np.cos(turn.astype(np.float64)), np.sin(turn.astype(np.float64))
    cosine = np.tile(cosine, (1, LANES // half)).astype(np.float32)
    sine = np.tile(np.concatenate([-sine, sine], 1), (1, LANES // HEAD)).astype(np.float32)
    return cosine, sine


def swap_halves(values):
    lane = lax.broadcasted_iota(jnp.int32, values.shape, 1)
    return jnp.where(
        lane % HEAD < HEAD // 2, pltpu.roll(values, LANES - HEAD // 2, 1), pltpu.roll(values, HEAD // 2, 1)
    )


def head_mask(rows, which):
    lane = lax.broadcasted_iota(jnp.int32, (rows, LANES), 1)
    return (lane >= HEAD) if which else (lane < HEAD)


def layer_norm_rows(values, gain):
    centred = values - jnp.mean(values, axis=-1, keepdims=True)
    spread = jnp.mean(centred * centred, axis=-1, keepdims=True)
    return centred * lax.rsqrt(spread + norm_eps) * gain


def scaled_rows(values):
    centred = values - jnp.mean(values, axis=-1, keepdims=True)
    return centred * lax.rsqrt(jnp.mean(centred * centred, axis=-1, keepdims=True) + norm_eps)


def norm_back_rows(values, gain, delta):
    centred = values - jnp.mean(values, axis=-1, keepdims=True)
    spread = jnp.mean(centred * centred, axis=-1, keepdims=True)
    s = lax.rsqrt(spread + norm_eps)
    xhat = centred * s
    e = delta * gain
    back = s * (e - jnp.mean(e, axis=-1, keepdims=True) - xhat * jnp.mean(e * xhat, axis=-1, keepdims=True))
    return back, jnp.sum(delta * xhat, axis=0, keepdims=True)


def fill_bias(lengths_ref, pads_ref, bias_ref):
    sequence = lax.axis_index("dp")
    docs = lengths_ref.shape[1]
    ends, total = [], jnp.int32(0)
    for j in range(docs):
        total = total + lengths_ref[sequence, j]
        ends.append(total)
    first_pad = LEN - pads_ref[sequence]

    def segment(places):
        seg = jnp.zeros(places.shape, jnp.int32)
        for end in ends:
            seg = seg + (places >= end).astype(jnp.int32)
        return seg

    rows, cols, row_seg, col_seg = {}, {}, {}, {}
    for base in (0, HALF):
        rows[base] = lax.broadcasted_iota(jnp.int32, (HALF, LANES), 0) + base
        cols[base] = lax.broadcasted_iota(jnp.int32, (HALF, LANES), 1) + base
        row_seg[base] = segment(rows[base])
        col_seg[base] = segment(cols[base])
    for tile, (query_kind, key_kind, query_base, key_base) in enumerate(TILES):
        q, k = rows[query_base], cols[key_base]
        query_block, key_block = q // BLOCK, k // BLOCK
        same_doc = (row_seg[query_base] == col_seg[key_base]) & (k < first_pad)
        if query_kind == 0 and key_kind == 0:
            ok = (key_block == query_block) & (same_doc | (q == k))
        elif query_kind == 0:
            ok = (key_block < query_block) & same_doc
        else:
            ok = (key_block <= query_block) & (same_doc | (q == k))
        bias_ref[:, tile * LANES : (tile + 1) * LANES] = jnp.where(ok, 0.0, masked_score)


def fetch(pairs, sems):
    copies = [pltpu.make_async_copy(source, target, sems.at[i]) for i, (source, target) in enumerate(pairs)]
    for copy in copies:
        copy.start()
    return copies


class Sender:
    def __init__(self, sems):
        self.sems, self.copies = sems, []

    def send(self, source, target):
        self.copies.append(pltpu.make_async_copy(source, target, self.sems.at[len(self.copies)]))
        self.copies[-1].start()

    def finish(self):
        for copy in self.copies:
            copy.wait()


def attention_forward(
    lengths_in, pads_in, gain_in, x_in, wq_in, wk_in, wv_in, cos_in, sin_in, wo_in,
    normed_out, q_out, k_out, v_out, att_out, prob_out, part_out,
    bias_ref, lengths_ref, pads_ref, gain_ref, x_ref, wq_ref, wk_ref, wv_ref, cos_ref, sin_ref, wo_ref,
    normed_ref, q_ref, k_ref, v_ref, att_ref, prob_ref, part_ref, sems, out_sems,
):
    first = fetch(((lengths_in, lengths_ref), (pads_in, pads_ref), (x_in, x_ref), (gain_in, gain_ref)), sems.at[:4])
    copies = fetch(
        (
            (wq_in, wq_ref), (wk_in, wk_ref), (wv_in, wv_ref), (cos_in, cos_ref), (sin_in, sin_ref), (wo_in, wo_ref),
        ),
        sems.at[4:],
    )
    sender = Sender(out_sems)
    first[0].wait()
    first[1].wait()
    heads_cols = wq_ref.shape[1]
    pairs = heads_cols // LANES
    fill_bias(lengths_ref, pads_ref, bias_ref)
    first[2].wait()
    first[3].wait()
    gain = gain_ref[...].reshape(1, -1)

    @pl.loop(0, x_ref.shape[0] // 64)
    def _(i):
        rows = pl.ds(pl.multiple_of(i * 64, 64), 64)
        normed_ref[rows, :] = layer_norm_rows(x_ref[rows, :].astype(f32), gain).astype(bf16)

    sender.send(normed_ref, normed_out)
    for copy in copies[:5]:
        copy.wait()
    for block in range(4):
        rows = slice(block * HALF, block * HALF + HALF)
        places = slice((block % 2) * HALF, (block % 2) * HALF + HALF)
        key_rows = slice(KEY_PLACE[block] * HALF, KEY_PLACE[block] * HALF + HALF)
        normed = normed_ref[rows, :]
        cosine, sine = cos_ref[places, :], sin_ref[places, :]
        query, key = mm(normed, wq_ref[...]), mm(normed, wk_ref[...])
        for t in range(pairs):
            cols = slice(t * LANES, (t + 1) * LANES)
            turned = query[:, cols] * cosine + swap_halves(query[:, cols]) * sine
            q_ref[rows, cols] = (turned.astype(bf16).astype(f32) * score_scale).astype(bf16)
            turned = key[:, cols] * cosine + swap_halves(key[:, cols]) * sine
            k_ref[key_rows, cols] = turned.astype(bf16)
        v_ref[key_rows, :] = mm(normed, wv_ref[...]).astype(bf16)
    for source, target in ((q_ref, q_out), (k_ref, k_out), (v_ref, v_out)):
        sender.send(source, target)

    for t in range(pairs):
        cols = slice(t * LANES, (t + 1) * LANES)
        key_pair, value_pair = k_ref[:, cols], v_ref[:, cols]
        mixed = [None] * 4
        for which in range(2):
            mask = head_mask(key_pair.shape[0], which)
            key_head = jnp.where(mask, key_pair, jnp.zeros_like(key_pair))
            value_head = jnp.where(mask, value_pair, jnp.zeros_like(value_pair))
            for case, (query_row, first, width, key_row) in enumerate(CASES):
                scores = nt(q_ref[query_row : query_row + HALF, cols], key_head[key_row : key_row + width])
                scores = scores + bias_ref[:, first : first + width]
                weights = jnp.exp(scores - jnp.max(scores, axis=1, keepdims=True))
                low = (weights * (1.0 / jnp.sum(weights, axis=1, keepdims=True))).astype(bf16)
                prob_ref[2 * t + which, :, first : first + width] = low
                part = mm(low, value_head[key_row : key_row + width])
                mixed[case] = part if mixed[case] is None else mixed[case] + part
        for case, (query_row, _, _, _) in enumerate(CASES):
            att_ref[query_row : query_row + HALF, cols] = mixed[case].astype(bf16)
        sender.send(prob_ref.at[2 * t : 2 * t + 2], prob_out.at[2 * t : 2 * t + 2])

    sender.send(att_ref, att_out)
    copies[5].wait()
    for block in range(2):
        rows = slice(block * 256, block * 256 + 256)
        part_ref[rows, :] = mm(att_ref[rows, :], wo_ref[...])
        sender.send(part_ref.at[rows, :], part_out.at[rows, :])
    sender.finish()


def fourths(start, part):
    return pl.ds(pl.multiple_of(start * part, 8), part)


def z_place(me, block):
    relative = (me // PLANE) ^ block
    return (relative % 2) * 2 + relative // 2


def quarter_at(place):
    core = lax.axis_index("mp") % 2
    slot = (place // 2) * (X + core) + (place % 2) * (Y - core)
    return lax.axis_index("dp") % PLANE ^ slot


def place_quarter(outs, place, value):
    me = lax.axis_index("dp") % GROUP
    part = value.shape[0] // STACK
    for block in range(STACK):
        outs[place // 2][place % 2, z_place(me, block)] = value[block * part : (block + 1) * part]


def place_quarter_z_first(outs, place, value):
    me = lax.axis_index("dp") % GROUP
    part = value.shape[0] // STACK
    for block in range(STACK):
        z = z_place(me, block)
        for sent in range(2):

            @pl.when(z // 2 == sent)
            def _(out=outs[sent], z=z, piece=value[block * part : (block + 1) * part]):
                out[z % 2, place] = piece


def mlp_kernel(
    gain_in, bu_in, x_in, mine_in, theirs_in, cot_in, wu_in, wd_in,
    residual_out, gbu_ref, gbd_ref, d_kept, d_sent, c_kept, c_sent, u_kept, u_sent, shares_out,
    gain_ref, bu_ref, x_ref, mine_ref, theirs_ref, cot_ref, wu_ref, wd_ref,
    residual_ref, normed_ref, act_ref, du_ref, d_kept_ref, d_sent_ref, c_kept_ref, c_sent_ref, u_kept_ref, u_sent_ref, shares_ref,
    sems, out_sems,
):
    row_count = x_ref.shape[0]
    units = wu_ref.shape[1]
    halves = (slice(0, row_count // 2), slice(row_count // 2, row_count))
    pairs = [(gain_in, gain_ref), (bu_in, bu_ref)]
    for rows in halves:
        pairs += [(a.at[rows, :], b.at[rows, :]) for a, b in ((x_in, x_ref), (mine_in, mine_ref), (theirs_in, theirs_ref))]
    copies = fetch(pairs + [(cot_in, cot_ref), (wu_in, wu_ref), (wd_in, wd_ref)], sems)
    sender = Sender(out_sems)
    gbu_ref[...] = jnp.zeros_like(gbu_ref)
    gbd_ref[...] = jnp.zeros_like(gbd_ref)
    copies[0].wait()
    gain = gain_ref[...].reshape(1, -1)
    for half in range(2):
        for copy in copies[2 + 3 * half : 5 + 3 * half]:
            copy.wait()

        @pl.loop(0, row_count // 128)
        def _(i, half=half):
            rows = pl.ds(pl.multiple_of(half * (row_count // 2) + i * 64, 64), 64)
            residual = x_ref[rows, :].astype(f32) + (mine_ref[rows, :] + theirs_ref[rows, :])
            residual_ref[rows, :] = residual
            normed_ref[rows, :] = layer_norm_rows(residual, gain).astype(bf16)

    sender.send(residual_ref, residual_out)
    for copy in (copies[1], *copies[8:]):
        copy.wait()
    c0 = math.sqrt(2.0 / math.pi)
    c1 = c0 * 0.044715

    @pl.loop(0, units // 256)
    def _(j):
        cols = pl.ds(pl.multiple_of(j * 256, 256), 256)
        for block in range(row_count // 256):
            rows = slice(block * 256, block * 256 + 256)
            u = mm(normed_ref[rows, :], wu_ref[:, cols]) + bu_ref[cols].reshape(1, -1)
            delta = nt(cot_ref[rows, :], wd_ref[cols, :])
            square = u * u
            t = jnp.tanh(u * (c0 + c1 * square))
            half_up = 0.5 * (1.0 + t)
            act_ref[rows, cols] = (u * half_up).astype(bf16)
            slope = half_up + (0.5 * u) * (1.0 - t * t) * (c0 + (3.0 * c1) * square)
            low = (delta * slope).astype(bf16)
            du_ref[rows, cols] = low
            gbu_ref[:, cols] += jnp.sum(low.astype(f32), axis=0, keepdims=True)

    quarter = units // PLANE
    cut = cot_ref.shape[1] * 2 // 3
    quarters = {}
    for place in range(PLANE):
        quarters[place] = pl.ds(pl.multiple_of(quarter_at(place) * quarter, LANES), quarter)
    for place in (2, 3, 0, 1):
        grad = tn(act_ref[:, quarters[place]], cot_ref[...])
        place_quarter((d_kept_ref, d_sent_ref), place, grad[:, :cut])
        place_quarter_z_first((c_kept_ref, c_sent_ref), place, grad[:, cut:])
        if place == 3:
            sender.send(d_sent_ref, d_sent)
    for source, target in ((c_sent_ref, c_sent), (d_kept_ref, d_kept), (c_kept_ref, c_kept)):
        sender.send(source, target)
    for place in (2, 3, 0, 1):
        place_quarter((u_kept_ref, u_sent_ref), place, tn(normed_ref[...], du_ref[:, quarters[place]]))
        if place == 3:
            sender.send(u_sent_ref, u_sent)
    sender.send(u_kept_ref, u_kept)
    for share in range(2):
        for rows in halves:
            if share == 0:
                shares_ref[share, rows, :] = nt(du_ref[rows, :], wu_ref[...])
            else:
                shares_ref[share, rows, :] = mm(act_ref[rows, :], wd_ref[...])
        sender.send(shares_ref.at[share], shares_out.at[share])

    @pl.loop(0, row_count // 64)
    def _(i):
        rows = pl.ds(pl.multiple_of(i * 64, 64), 64)
        gbd_ref[...] += jnp.sum(cot_ref[rows, :].astype(f32), axis=0, keepdims=True)

    sender.finish()


def attention_backward(
    mine_ref, theirs_ref, residual_ref, gain_ref, cot_ref, att_ref, wo_ref, q_ref, k_ref, v_ref, prob_ref,
    normed_ref, wq_ref, wk_ref, wv_ref, cos_ref, sin_ref, x_ref, bd_ref, gbd_ref, gbu_ref,
    output_ref, delta_ref, vec_ref, part_ref, *outs_and_scratch,
):
    *outs, branch_ref, datt_ref, dq_ref, dk_ref, dv_ref, dk_acc, dv_acc, grads_ref, gnorm_ref = outs_and_scratch
    row_count = residual_ref.shape[0]
    heads_cols = wq_ref.shape[1]
    pairs = heads_cols // LANES
    gnorm_ref[...] = jnp.zeros_like(gnorm_ref)

    @pl.loop(0, row_count // 64)
    def _(i):
        rows = pl.ds(pl.multiple_of(i * 64, 64), 64)
        delta = mine_ref[0, rows, :] + theirs_ref[0, rows, :]
        residual = residual_ref[rows, :]
        output_ref[rows, :] = (residual + (mine_ref[1, rows, :] + theirs_ref[1, rows, :]) + bd_ref[...]).astype(bf16)
        back, gain_part = norm_back_rows(residual, gain_ref[...], delta)
        back = back + cot_ref[rows, :].astype(f32)
        delta_ref[rows, :] = back
        branch_ref[rows, :] = back.astype(bf16)
        gnorm_ref[0:1, :] += gain_part

    for block in range(2):
        rows = slice(block * 256, block * 256 + 256)
        datt_ref[rows, :] = nt(branch_ref[rows, :], wo_ref[...]).astype(bf16)
    half = heads_cols
    grad = tn(att_ref[...], branch_ref[...])
    grads_ref[0, 0], grads_ref[0, 1] = grad[:, :half], grad[:, half:]

    for t in range(pairs):
        cols = slice(t * LANES, (t + 1) * LANES)
        key_pair, value_pair = k_ref[:, cols], v_ref[:, cols]
        dk_acc[...] = jnp.zeros_like(dk_acc)
        dv_acc[...] = jnp.zeros_like(dv_acc)
        query_grads = [None] * 4
        for which in range(2):
            mask = head_mask(key_pair.shape[0], which)
            key_head = jnp.where(mask, key_pair, jnp.zeros_like(key_pair))
            value_head = jnp.where(mask, value_pair, jnp.zeros_like(value_pair))
            small = head_mask(HALF, which)
            for case, (query_row, first, width, key_row) in enumerate(CASES):
                rows = slice(query_row, query_row + HALF)
                keys = slice(key_row, key_row + width)
                low = prob_ref[2 * t + which, :, first : first + width]
                wide = low.astype(f32)
                delta_head = datt_ref[rows, cols]
                g = nt(delta_head, value_head[keys])
                weighted = wide * g
                scores_back = (weighted - wide * jnp.sum(weighted, axis=1, keepdims=True)).astype(bf16)
                part = mm(scores_back, key_head[keys])
                query_grads[case] = part if query_grads[case] is None else query_grads[case] + part
                query = q_ref[rows, cols]
                query = jnp.where(small, query, jnp.zeros_like(query))
                delta_head = jnp.where(small, delta_head, jnp.zeros_like(delta_head))
                dk_acc[keys, :] += tn(scores_back, query)
                dv_acc[keys, :] += tn(low, delta_head)
        for block in range(4):
            rows = slice(block * HALF, block * HALF + HALF)
            places = slice((block % 2) * HALF, (block % 2) * HALF + HALF)
            key_rows = slice(KEY_PLACE[block] * HALF, KEY_PLACE[block] * HALF + HALF)
            cosine, sine = cos_ref[places, :], sin_ref[places, :]
            grad = query_grads[block] * score_scale
            dq_ref[rows, cols] = (grad * cosine - swap_halves(grad) * sine).astype(bf16)
            grad = dk_acc[key_rows, :]
            dk_ref[rows, cols] = (grad * cosine - swap_halves(grad) * sine).astype(bf16)
            dv_ref[rows, cols] = dv_acc[key_rows, :].astype(bf16)

    for block in range(2):
        rows = slice(block * 256, block * 256 + 256)
        part_ref[rows, :] = (
            nt(dq_ref[rows, :], wq_ref[...]) + nt(dk_ref[rows, :], wk_ref[...]) + nt(dv_ref[rows, :], wv_ref[...])
        )

    @pl.loop(0, row_count // 64)
    def _(i):
        rows = pl.ds(pl.multiple_of(i * 64, 64), 64)
        gnorm_ref[1:2, :] += jnp.sum(part_ref[rows, :] * scaled_rows(x_ref[rows, :].astype(f32)), axis=0, keepdims=True)

    vec_ref[...] = jnp.zeros_like(vec_ref)
    row = 0
    once = jnp.where(lax.axis_index("mp") == 0, 1.0, 0.0)
    for values in (gnorm_ref[1:2, :], gnorm_ref[0:1, :] * once, gbd_ref[...] * once, gbu_ref[...]):
        for first in range(0, values.shape[1], half):
            vec_ref[row : row + 1, :] = values[:, first : first + half]
            row += 1

    for matrix, grad_rows in ((1, dq_ref), (2, dk_ref), (3, dv_ref)):
        grad = tn(normed_ref[...], grad_rows[...])
        grads_ref[matrix, 0], grads_ref[matrix, 1] = grad[:half], grad[half:]
    for place in range(PLANE):
        quarter = quarter_at(place)
        place_quarter(outs[:2], place, grads_ref[quarter, 0])
        place_quarter(outs[2:], place, grads_ref[quarter, 1])


def input_kernel(mine_ref, theirs_ref, x_ref, gain_ref, delta_ref, grad_ref):
    @pl.loop(0, x_ref.shape[0] // 64)
    def _(i):
        rows = pl.ds(pl.multiple_of(i * 64, 64), 64)
        delta = mine_ref[rows, :] + theirs_ref[rows, :]
        back, _ = norm_back_rows(x_ref[rows, :].astype(f32), gain_ref[...], delta)
        grad_ref[rows, :] = (delta_ref[rows, :] + back).astype(bf16)


def each_block(own_ref, got_ref, put, z_first=False):
    me = lax.axis_index("dp") % GROUP
    for place in range(PLANE):
        for z in range(STACK):
            first, second = (z, place) if z_first else (place, z)
            value = (got_ref if first // 2 else own_ref)[first % 2, second]
            put(quarter_at(place), me // PLANE ^ Z_SLOTS[z], value)


def unpack_down(own_ref, got_ref, z_own_ref, z_got_ref, out_ref):
    cut = own_ref.shape[-1]

    def put(quarter, fourth, value):
        cols = slice(0, cut) if value.shape[1] == cut else slice(cut, None)
        out_ref[fourths(quarter * STACK + fourth, value.shape[0]), cols] = value

    each_block(own_ref, got_ref, put)
    each_block(z_own_ref, z_got_ref, put, True)


def unpack_up(own_ref, got_ref, out_ref):
    def put(quarter, fourth, value):
        part, cols = value.shape
        out_ref[fourths(fourth, part), pl.ds(pl.multiple_of(quarter * cols, LANES), cols)] = value

    each_block(own_ref, got_ref, put)


def unpack_attention(own_a, got_a, own_b, got_b, *outs):
    grads_ref = outs[4]
    for portion, (own_ref, got_ref) in enumerate(((own_a, got_a), (own_b, got_b))):

        def put(quarter, fourth, value, portion=portion):
            grads_ref[quarter, portion, fourths(fourth, value.shape[0])] = value

        each_block(own_ref, got_ref, put)
    finish_att(outs)


def finish_att(outs):
    *outs, grads_ref, sems = outs
    half = grads_ref.shape[-1]
    copies = []
    for matrix, out in enumerate(outs):
        for portion in range(2):
            place = pl.ds(portion * half, half)
            target = out.at[place, :] if matrix else out.at[:, place]
            copies.append((grads_ref.at[matrix, portion], target))
    for copy in fetch(copies, sems):
        copy.wait()


VMEM = pl.BlockSpec(memory_space=pltpu.VMEM)
HBM = pl.BlockSpec(memory_space=pltpu.HBM)


def call(kernel, outs, held=(), loose=(), scratch=(), flops=0, limit=40, loose_outs=None):
    ins = [*held, *loose]
    shapes = [jax.ShapeDtypeStruct(shape, dtype) for shape, dtype in outs]
    moved = sum(math.prod(a.shape) * a.dtype.itemsize for a in ins + shapes)
    out_specs = [HBM if loose_outs and i in loose_outs else VMEM for i in range(len(outs))]
    return pl.pallas_call(
        kernel,
        name=kernel.__name__,
        out_shape=shapes,
        in_specs=[VMEM] * len(held) + [HBM] * len(loose),
        out_specs=out_specs,
        scratch_shapes=[s if not isinstance(s, tuple) else pltpu.VMEM(*s) for s in scratch],
        compiler_params=pltpu.CompilerParams(vmem_limit_bytes=limit * 1024 * 1024),
        cost_estimate=pl.CostEstimate(flops=flops, bytes_accessed=moved, transcendentals=0),
    )(*ins)


def on_device(
    count,
    inputs, norm_attn, w_query, w_key, w_value, w_out, norm_mlp, w_up, b_up, w_down, b_down, cotangent,
    doc_lengths, pad_counts,
):
    rows, width = inputs.shape
    heads_cols = w_query.shape[1]
    units = w_up.shape[1]
    heads = heads_cols // HEAD
    cosine, sine = (jnp.asarray(t) for t in rope_tables())
    gain_attn, gain_mlp = norm_attn.reshape(1, -1), norm_mlp.reshape(1, -1)

    def swap(values):
        return lax.ppermute(values, "mp", [(0, 1), (1, 0)])

    def flip(values, bits, name):
        pairs = [(2 * i + core, 2 * (i ^ bits[core]) + core) for i in range(count) for core in range(2)]
        with jax.named_scope(name):
            return lax.ppermute(values, ("dp", "mp"), pairs)

    def sems(n):
        return pltpu.SemaphoreType.DMA((n,))

    half = heads_cols

    def portions(*shape):
        return [((2, STACK) + shape, f32)] * 2

    last = []

    def turn(*values):
        if not last:
            return values
        values, _ = lax.optimization_barrier((values, last.pop()))
        return values

    def did(value):
        last[:] = [value]
        return value

    def over_groups(values):
        if count == GROUP:
            return values
        groups = [[k * GROUP + j for k in range(count // GROUP)] for j in range(GROUP)]
        return lax.psum(values, "dp", axis_index_groups=groups)

    def chain(name, parts, result, z_first=False, vec=None):
        keep, send = parts
        plane, stack = [(FIRST, "first"), (SECOND, "second")], [((Z1, Z1), "z1"), ((Z2, Z2), "z2")]
        steps = stack + plane if z_first else plane + stack

        def join(values):
            return values if vec is None else jnp.concatenate([values.reshape(-1, values.shape[-1]), vec], 0)

        def part_of(got, like, vec):
            if vec is None:
                return got, None
            return got[: -vec.shape[0]].reshape(like.shape), vec + got[-vec.shape[0] :]

        for step, (bits, label) in enumerate(steps):
            if step:
                keep, got, vec = turn(keep, got, vec)
                got, vec = part_of(got, keep, vec)
                cut = keep.shape[0] // 2
                send, keep = keep[cut:] + got[cut:], keep[:cut] + got[:cut]
                if step == 1:
                    keep, send = keep[0], send[0]
                send = did(join(send))
            else:
                send = join(send)
            got = flip(send, bits, f"{name}_sum_{label}")
            yield
        keep, got, vec = turn(keep, got, vec)
        got, vec = part_of(got, keep, vec)
        own = over_groups(did(keep + got))
        if vec is not None:
            result.append(over_groups(vec))
        for step, (bits, label) in enumerate(reversed(steps)):
            got = flip(own, bits, f"{name}_gather_{label}")
            yield
            own, got = turn(own, got)
            if step < 3:
                own = did(jnp.stack([own, got]) if step == 2 else jnp.concatenate([own, got], 0))
        result.extend((own, got))
        yield

    scores = (heads, HALF, 8 * LANES)
    rows_of = {"width": ((rows, width), bf16), "heads": ((rows, heads_cols), bf16), "sum": ((rows, width), f32)}
    outs = [rows_of["width"]] + [rows_of["heads"]] * 4 + [(scores, bf16), rows_of["sum"]]
    normed, q, k, v, attended, probs, branch = call(
        attention_forward,
        outs,
        loose=[doc_lengths, pad_counts, norm_attn, inputs, w_query, w_key, w_value, cosine, sine, w_out],
        scratch=[
            (scores[1:], f32),
            pltpu.SMEM(doc_lengths.shape, jnp.int32),
            pltpu.SMEM(pad_counts.shape, jnp.int32),
            (norm_attn.shape, f32),
            rows_of["width"],
            *[((width, heads_cols), bf16)] * 3,
            (cosine.shape, f32),
            (sine.shape, f32),
            ((heads_cols, width), bf16),
            *outs,
            sems(10),
            sems(10),
        ],
        flops=2 * rows * width * heads_cols * 4,
        limit=62,
        loose_outs=range(7),
    )
    branch_other = swap(branch)

    big = [
        *portions(units // GROUP, width * 2 // 3),
        *portions(units // GROUP, width // 3),
        *portions(width // STACK, units // PLANE),
        ((2, rows, width), f32),
    ]
    residual, grad_bu, grad_bd, *parts, shares = call(
        mlp_kernel,
        [rows_of["sum"], ((1, units), f32), ((1, width), f32), *big],
        loose=[norm_mlp, b_up, inputs, branch, branch_other, cotangent, w_up, w_down],
        scratch=[
            (norm_mlp.shape, f32),
            (b_up.shape, f32),
            rows_of["width"],
            rows_of["sum"],
            rows_of["sum"],
            rows_of["width"],
            ((width, units), bf16),
            ((units, width), bf16),
            rows_of["sum"],
            rows_of["width"],
            ((rows, units), bf16),
            ((rows, units), bf16),
            *big,
            sems(11),
            sems(9),
        ],
        flops=2 * rows * width * units * 6,
        limit=62,
        loose_outs=(0, *range(3, 10)),
    )
    made, grads = {key: [] for key in "dcuab"}, {}
    chains = {
        "d": chain("down", parts[:2], made["d"]),
        "c": chain("down_stack", parts[2:4], made["c"], True),
        "u": chain("up", parts[4:], made["u"]),
    }
    state = {"shares_other": swap(shares)}

    def backward():
        (shares_other,) = turn(state["shares_other"])
        state["output"], state["delta_residual"], vec, state["normed_part"], *parts = call(
            attention_backward,
            [((rows, width), bf16), ((rows, width), f32), ((16, half), f32), ((rows, width), f32)]
            + portions(half // STACK, half) * 2,
            held=[
                shares, shares_other, residual, gain_mlp, cotangent, attended, w_out, q, k, v, probs,
                normed, w_query, w_key, w_value, cosine, sine, inputs, b_down.reshape(1, -1), grad_bd, grad_bu,
            ],
            scratch=[
                ((rows, width), bf16),
                ((rows, heads_cols), bf16),
                ((rows, heads_cols), bf16),
                ((rows, heads_cols), bf16),
                ((rows, heads_cols), bf16),
                ((rows, LANES), f32),
                ((rows, LANES), f32),
                ((PLANE, 2, half, half), f32),
                ((8, width), f32),
            ],
            flops=2 * rows * width * heads_cols * 10,
        )
        did(vec)
        state["normed_other"] = swap(state["normed_part"])
        chains["a"] = chain("attention", parts[:2], made["a"], vec=vec)
        chains["b"] = chain("attention_rest", parts[2:], made["b"])

    def input_back():
        (normed_other,) = turn(state["normed_other"])
        (state["grad_inputs"],) = call(
            input_kernel,
            [((rows, width), bf16)],
            held=[state["normed_part"], normed_other, inputs, gain_attn, state["delta_residual"]],
        )
        did(state["grad_inputs"])

    def unpack():
        if "down" not in grads and len(made["d"]) == len(made["c"]) == 2:
            grads["down"] = call(unpack_down, [((units, width), f32)], held=made["d"] + made["c"])
            did(grads["down"][0])
        if "up" not in grads and len(made["u"]) == 2:
            grads["up"] = call(unpack_up, [((width, units), f32)], held=made["u"])
            did(grads["up"][0])
        if "attention" not in grads and len(made["a"]) == 3 and len(made["b"]) == 2:
            grads["attention"] = call(
                unpack_attention,
                [((heads_cols, width), f32)] + [((width, heads_cols), f32)] * 3,
                held=made["a"][1:] + made["b"],
                scratch=[((PLANE, 2, half, half), f32), sems(8)],
                loose_outs=range(4),
            )

    did(grad_bd)
    pieces = {"K": backward, "I": input_back}
    for key in ORDER:
        if key in pieces:
            pieces[key]()
        else:
            next(chains[key])
            unpack()
    assert len(grads) == 3

    vec = made["a"][0]
    n = width // half
    shared = (vec[: 3 * n] + swap(vec[: 3 * n])).reshape(3, width)
    grad_bu = vec[3 * n :].reshape(-1)[:units]
    (grad_down,), (grad_up,) = grads["down"], grads["up"]
    grad_out, grad_query, grad_key, grad_value = grads["attention"]
    output, grad_inputs = state["output"], state["grad_inputs"]
    return (
        output,
        grad_inputs,
        shared[0],
        grad_query,
        grad_key,
        grad_value,
        grad_out,
        shared[1],
        grad_up,
        grad_bu,
        grad_down,
        shared[2],
    )


def solution(mesh):
    count = mesh.shape["dp"]

    def step(*args):
        return on_device(count, *args)

    return jax.shard_map(
        step,
        mesh=mesh,
        in_specs=(
            P("dp", None),
            P(),
            P(None, "mp"),
            P(None, "mp"),
            P(None, "mp"),
            P("mp", None),
            P(),
            P(None, "mp"),
            P("mp"),
            P("mp", None),
            P(),
            P("dp", None),
            P(),
            P(),
        ),
        out_specs=(
            P("dp", None),
            P("dp", None),
            P(),
            P(None, "mp"),
            P(None, "mp"),
            P(None, "mp"),
            P("mp", None),
            P(),
            P(None, "mp"),
            P("mp"),
            P("mp", None),
            P(),
        ),
        check_vma=False,
    )
```

```python
from functools import partial
import math

import numpy as np

import jax
import jax.numpy as jnp
from jax import lax
from jax.experimental import pallas as pl
from jax.experimental.pallas import tpu as pltpu
from jax.sharding import PartitionSpec as P

HEAD = 64
BLOCK = 16
LEN = 256
HALF = 128
LANES = 128
PLANE = 4
STACK = 4
GROUP = PLANE * STACK

norm_eps = 1e-05
rope_base = 10000.0
masked_score = -1e30
score_scale = HEAD ** (-0.5)
bf16 = jnp.bfloat16
f32 = jnp.float32

X, Y, Z1, Z2 = 1, 2, 4, 8
FIRST, SECOND = (X, Y), (Y, X)
Z_FIRST, Z_SECOND = (Z1, Z2), (Z2, Z1)

ORDER = "cduKdcubdIucdabcudbaucdbaucdbaudbacabuabca"

CASES = ((0, 0, 256, 0), (128, 256, 384, 128), (256, 640, 128, 128), (384, 768, 256, 128))
TILES = (
    (0, 0, 0, 0),
    (0, 1, 0, 0),
    (0, 1, 128, 0),
    (0, 1, 128, 128),
    (0, 0, 128, 128),
    (1, 1, 0, 0),
    (1, 1, 128, 0),
    (1, 1, 128, 128),
)
KEY_PLACE = (0, 3, 1, 2)


def mm(left, right):
    return jnp.dot(left, right, preferred_element_type=f32)


def tn(left, right):
    return lax.dot_general(left, right, (((0,), (0,)), ((), ())), preferred_element_type=f32)


def nt(left, right):
    return lax.dot_general(left, right, (((1,), (1,)), ((), ())), preferred_element_type=f32)


def rope_tables():
    half = HEAD // 2
    frequency = np.exp(np.arange(half) * (-2.0 * math.log(rope_base) / HEAD)).astype(np.float32)
    turn = (np.arange(LEN, dtype=np.float32)[:, None] * frequency[None, :]).astype(np.float32)
    cosine, sine = np.cos(turn.astype(np.float64)), np.sin(turn.astype(np.float64))
    cosine = np.tile(cosine, (1, LANES // half)).astype(np.float32)
    sine = np.tile(np.concatenate([-sine, sine], 1), (1, LANES // HEAD)).astype(np.float32)
    return cosine, sine


def swap_halves(values):
    lane = lax.broadcasted_iota(jnp.int32, values.shape, 1)
    return jnp.where(
        lane % HEAD < HEAD // 2, pltpu.roll(values, LANES - HEAD // 2, 1), pltpu.roll(values, HEAD // 2, 1)
    )


def head_mask(rows, which):
    lane = lax.broadcasted_iota(jnp.int32, (rows, LANES), 1)
    return (lane >= HEAD) if which else (lane < HEAD)


def layer_norm_rows(values, gain):
    centred = values - jnp.mean(values, axis=-1, keepdims=True)
    spread = jnp.mean(centred * centred, axis=-1, keepdims=True)
    return centred * lax.rsqrt(spread + norm_eps) * gain


def scaled_rows(values):
    centred = values - jnp.mean(values, axis=-1, keepdims=True)
    return centred * lax.rsqrt(jnp.mean(centred * centred, axis=-1, keepdims=True) + norm_eps)


def norm_back_rows(values, gain, delta):
    centred = values - jnp.mean(values, axis=-1, keepdims=True)
    spread = jnp.mean(centred * centred, axis=-1, keepdims=True)
    s = lax.rsqrt(spread + norm_eps)
    xhat = centred * s
    e = delta * gain
    back = s * (e - jnp.mean(e, axis=-1, keepdims=True) - xhat * jnp.mean(e * xhat, axis=-1, keepdims=True))
    return back, jnp.sum(delta * xhat, axis=0, keepdims=True)


def fill_bias(lengths_ref, pads_ref, bias_ref):
    sequence = lax.axis_index("dp")
    docs = lengths_ref.shape[1]
    ends, total = [], jnp.int32(0)
    for j in range(docs):
        total = total + lengths_ref[sequence, j]
        ends.append(total)
    first_pad = LEN - pads_ref[sequence]

    def segment(places):
        seg = jnp.zeros(places.shape, jnp.int32)
        for end in ends:
            seg = seg + (places >= end).astype(jnp.int32)
        return seg

    rows, cols, row_seg, col_seg = {}, {}, {}, {}
    for base in (0, HALF):
        rows[base] = lax.broadcasted_iota(jnp.int32, (HALF, LANES), 0) + base
        cols[base] = lax.broadcasted_iota(jnp.int32, (HALF, LANES), 1) + base
        row_seg[base] = segment(rows[base])
        col_seg[base] = segment(cols[base])
    for tile, (query_kind, key_kind, query_base, key_base) in enumerate(TILES):
        q, k = rows[query_base], cols[key_base]
        query_block, key_block = q // BLOCK, k // BLOCK
        same_doc = (row_seg[query_base] == col_seg[key_base]) & (k < first_pad)
        if query_kind == 0 and key_kind == 0:
            ok = (key_block == query_block) & (same_doc | (q == k))
        elif query_kind == 0:
            ok = (key_block < query_block) & same_doc
        else:
            ok = (key_block <= query_block) & (same_doc | (q == k))
        bias_ref[:, tile * LANES : (tile + 1) * LANES] = jnp.where(ok, 0.0, masked_score)


def fetch(pairs, sems):
    copies = [pltpu.make_async_copy(source, target, sems.at[i]) for i, (source, target) in enumerate(pairs)]
    for copy in copies:
        copy.start()
    return copies


class Sender:
    def __init__(self, sems):
        self.sems, self.copies = sems, []

    def send(self, source, target):
        self.copies.append(pltpu.make_async_copy(source, target, self.sems.at[len(self.copies)]))
        self.copies[-1].start()

    def finish(self):
        for copy in self.copies:
            copy.wait()


def attention_forward(
    lengths_in, pads_in, gain_in, x_in, wq_in, wk_in, wv_in, cos_in, sin_in, wo_in,
    normed_out, q_out, k_out, v_out, att_out, prob_out, part_out,
    bias_ref, lengths_ref, pads_ref, gain_ref, x_ref, wq_ref, wk_ref, wv_ref, cos_ref, sin_ref, wo_ref,
    normed_ref, q_ref, k_ref, v_ref, att_ref, prob_ref, part_ref, sems, out_sems,
):
    first = fetch(((lengths_in, lengths_ref), (pads_in, pads_ref), (x_in, x_ref), (gain_in, gain_ref)), sems.at[:4])
    copies = fetch(
        (
            (wq_in, wq_ref), (wk_in, wk_ref), (wv_in, wv_ref), (cos_in, cos_ref), (sin_in, sin_ref), (wo_in, wo_ref),
        ),
        sems.at[4:],
    )
    sender = Sender(out_sems)
    first[0].wait()
    first[1].wait()
    heads_cols = wq_ref.shape[1]
    pairs = heads_cols // LANES
    fill_bias(lengths_ref, pads_ref, bias_ref)
    first[2].wait()
    first[3].wait()
    gain = gain_ref[...].reshape(1, -1)

    @pl.loop(0, x_ref.shape[0] // 64)
    def _(i):
        rows = pl.ds(pl.multiple_of(i * 64, 64), 64)
        normed_ref[rows, :] = layer_norm_rows(x_ref[rows, :].astype(f32), gain).astype(bf16)

    sender.send(normed_ref, normed_out)
    for copy in copies[:5]:
        copy.wait()
    for block in range(4):
        rows = slice(block * HALF, block * HALF + HALF)
        places = slice((block % 2) * HALF, (block % 2) * HALF + HALF)
        key_rows = slice(KEY_PLACE[block] * HALF, KEY_PLACE[block] * HALF + HALF)
        normed = normed_ref[rows, :]
        cosine, sine = cos_ref[places, :], sin_ref[places, :]
        query, key = mm(normed, wq_ref[...]), mm(normed, wk_ref[...])
        for t in range(pairs):
            cols = slice(t * LANES, (t + 1) * LANES)
            turned = query[:, cols] * cosine + swap_halves(query[:, cols]) * sine
            q_ref[rows, cols] = (turned.astype(bf16).astype(f32) * score_scale).astype(bf16)
            turned = key[:, cols] * cosine + swap_halves(key[:, cols]) * sine
            k_ref[key_rows, cols] = turned.astype(bf16)
        v_ref[key_rows, :] = mm(normed, wv_ref[...]).astype(bf16)
    for source, target in ((q_ref, q_out), (k_ref, k_out), (v_ref, v_out)):
        sender.send(source, target)

    for t in range(pairs):
        cols = slice(t * LANES, (t + 1) * LANES)
        key_pair, value_pair = k_ref[:, cols], v_ref[:, cols]
        mixed = [None] * 4
        for which in range(2):
            mask = head_mask(key_pair.shape[0], which)
            key_head = jnp.where(mask, key_pair, jnp.zeros_like(key_pair))
            value_head = jnp.where(mask, value_pair, jnp.zeros_like(value_pair))
            for case, (query_row, first, width, key_row) in enumerate(CASES):
                scores = nt(q_ref[query_row : query_row + HALF, cols], key_head[key_row : key_row + width])
                scores = scores + bias_ref[:, first : first + width]
                weights = jnp.exp(scores - jnp.max(scores, axis=1, keepdims=True))
                low = (weights * (1.0 / jnp.sum(weights, axis=1, keepdims=True))).astype(bf16)
                prob_ref[2 * t + which, :, first : first + width] = low
                part = mm(low, value_head[key_row : key_row + width])
                mixed[case] = part if mixed[case] is None else mixed[case] + part
        for case, (query_row, _, _, _) in enumerate(CASES):
            att_ref[query_row : query_row + HALF, cols] = mixed[case].astype(bf16)
        sender.send(prob_ref.at[2 * t : 2 * t + 2], prob_out.at[2 * t : 2 * t + 2])

    sender.send(att_ref, att_out)
    copies[5].wait()
    for block in range(2):
        rows = slice(block * 256, block * 256 + 256)
        part_ref[rows, :] = mm(att_ref[rows, :], wo_ref[...])
        sender.send(part_ref.at[rows, :], part_out.at[rows, :])
    sender.finish()


def fourths(start, part):
    return pl.ds(pl.multiple_of(start * part, 8), part)


def slot_at(place):
    core = lax.axis_index("mp") % 2
    return (place // 2) * (1 + core) + (place % 2) * (2 - core)


def quarter_at(place):
    return lax.axis_index("dp") % PLANE ^ slot_at(place)


def fourth_at(place):
    return lax.axis_index("dp") % GROUP // PLANE ^ slot_at(place)


def z_place(block):
    slot = lax.axis_index("dp") % GROUP // PLANE ^ block
    return jnp.where(lax.axis_index("mp") % 2 == 0, (slot % 2) * 2 + slot // 2, slot)


def place_quarter(outs, place, value):
    part = value.shape[0] // STACK
    for block in range(STACK):
        outs[place // 2][place % 2, z_place(block)] = value[block * part : (block + 1) * part]


def place_quarter_z_first(outs, place, first_row, value):
    part = value.shape[0] // STACK
    for block in range(STACK):
        z = z_place(block)
        for sent in range(2):

            @pl.when(z // 2 == sent)
            def _(out=outs[sent], z=z, piece=value[block * part : (block + 1) * part]):
                out[z % 2, place, first_row : first_row + part, :] = piece


def mlp_kernel(
    gain_in, bu_in, x_in, mine_in, theirs_in, cot_in, wu_in, wd_in,
    residual_out, gbu_ref, gbd_ref, d_kept, d_sent, c_kept, c_sent, u_kept, u_sent, shares_out,
    gain_ref, bu_ref, x_ref, mine_ref, theirs_ref, cot_ref, wu_ref, wd_ref,
    residual_ref, normed_ref, act_ref, du_ref, d_kept_ref, d_sent_ref, c_kept_ref, c_sent_ref, u_kept_ref, u_sent_ref, shares_ref,
    sems, out_sems,
):
    row_count = x_ref.shape[0]
    units = wu_ref.shape[1]
    halves = (slice(0, row_count // 2), slice(row_count // 2, row_count))
    pairs = [(gain_in, gain_ref), (bu_in, bu_ref)]
    for rows in halves:
        pairs += [(a.at[rows, :], b.at[rows, :]) for a, b in ((x_in, x_ref), (mine_in, mine_ref), (theirs_in, theirs_ref))]
    copies = fetch(pairs + [(cot_in, cot_ref), (wu_in, wu_ref), (wd_in, wd_ref)], sems)
    sender = Sender(out_sems)
    gbu_ref[...] = jnp.zeros_like(gbu_ref)
    gbd_ref[...] = jnp.zeros_like(gbd_ref)
    copies[0].wait()
    gain = gain_ref[...].reshape(1, -1)
    for half in range(2):
        for copy in copies[2 + 3 * half : 5 + 3 * half]:
            copy.wait()

        @pl.loop(0, row_count // 128)
        def _(i, half=half):
            rows = pl.ds(pl.multiple_of(half * (row_count // 2) + i * 64, 64), 64)
            residual = x_ref[rows, :].astype(f32) + (mine_ref[rows, :] + theirs_ref[rows, :])
            residual_ref[rows, :] = residual
            normed_ref[rows, :] = layer_norm_rows(residual, gain).astype(bf16)

    sender.send(residual_ref, residual_out)
    for copy in (copies[1], *copies[8:]):
        copy.wait()
    c0 = math.sqrt(2.0 / math.pi)
    c1 = c0 * 0.044715

    @pl.loop(0, units // 256)
    def _(j):
        cols = pl.ds(pl.multiple_of(j * 256, 256), 256)
        for block in range(row_count // 256):
            rows = slice(block * 256, block * 256 + 256)
            u = mm(normed_ref[rows, :], wu_ref[:, cols]) + bu_ref[cols].reshape(1, -1)
            delta = nt(cot_ref[rows, :], wd_ref[cols, :])
            square = u * u
            t = jnp.tanh(u * (c0 + c1 * square))
            half_up = 0.5 * (1.0 + t)
            act_ref[rows, cols] = (u * half_up).astype(bf16)
            slope = half_up + (0.5 * u) * (1.0 - t * t) * (c0 + (3.0 * c1) * square)
            low = (delta * slope).astype(bf16)
            du_ref[rows, cols] = low
            gbu_ref[:, cols] += jnp.sum(low.astype(f32), axis=0, keepdims=True)

    quarter = units // PLANE
    fourth = units // GROUP
    cut = cot_ref.shape[1] * 2 // 3
    up_cut = quarter * 2 // 3
    quarters = {}
    for place in range(PLANE):
        quarters[place] = pl.ds(pl.multiple_of(quarter_at(place) * quarter, LANES), quarter)
    for place in (2, 3, 0, 1):
        grad = tn(act_ref[:, quarters[place]], cot_ref[...])
        place_quarter((d_kept_ref, d_sent_ref), place, grad[:, :cut])
        place_quarter_z_first((c_kept_ref, c_sent_ref), place, 0, grad[:, cut:])
        if place == 3:
            sender.send(d_sent_ref, d_sent)
    sender.send(d_kept_ref, d_kept)
    for place in (2, 3, 0, 1):
        grad = tn(normed_ref[...], du_ref[:, quarters[place]])
        place_quarter((u_kept_ref, u_sent_ref), place, grad[:, :up_cut])
        rest = grad[:, up_cut:].reshape(STACK, 2, fourth, -1)
        rest = jnp.concatenate([rest[:, 0], rest[:, 1]], 2).reshape(STACK * fourth, -1)
        place_quarter_z_first((c_kept_ref, c_sent_ref), place, fourth, rest)
        if place == 3:
            sender.send(u_sent_ref, u_sent)
    for source, target in ((c_sent_ref, c_sent), (u_kept_ref, u_kept), (c_kept_ref, c_kept)):
        sender.send(source, target)
    for share in range(2):
        for rows in halves:
            if share == 0:
                shares_ref[share, rows, :] = nt(du_ref[rows, :], wu_ref[...])
            else:
                shares_ref[share, rows, :] = mm(act_ref[rows, :], wd_ref[...])
        sender.send(shares_ref.at[share], shares_out.at[share])

    @pl.loop(0, row_count // 64)
    def _(i):
        rows = pl.ds(pl.multiple_of(i * 64, 64), 64)
        gbd_ref[...] += jnp.sum(cot_ref[rows, :].astype(f32), axis=0, keepdims=True)

    sender.finish()


def attention_backward(
    mine_ref, theirs_ref, residual_ref, gain_ref, cot_ref, att_ref, wo_ref, q_ref, k_ref, v_ref, prob_ref,
    normed_ref, wq_ref, wk_ref, wv_ref, cos_ref, sin_ref, x_ref, bd_ref, gbd_ref, gbu_ref,
    output_ref, delta_ref, vec_ref, part_ref, *outs_and_scratch,
):
    *outs, branch_ref, datt_ref, dq_ref, dk_ref, dv_ref, dk_acc, dv_acc, grads_ref, gnorm_ref = outs_and_scratch
    row_count = residual_ref.shape[0]
    heads_cols = wq_ref.shape[1]
    pairs = heads_cols // LANES
    gnorm_ref[...] = jnp.zeros_like(gnorm_ref)

    @pl.loop(0, row_count // 64)
    def _(i):
        rows = pl.ds(pl.multiple_of(i * 64, 64), 64)
        delta = mine_ref[0, rows, :] + theirs_ref[0, rows, :]
        residual = residual_ref[rows, :]
        output_ref[rows, :] = (residual + (mine_ref[1, rows, :] + theirs_ref[1, rows, :]) + bd_ref[...]).astype(bf16)
        back, gain_part = norm_back_rows(residual, gain_ref[...], delta)
        back = back + cot_ref[rows, :].astype(f32)
        delta_ref[rows, :] = back
        branch_ref[rows, :] = back.astype(bf16)
        gnorm_ref[0:1, :] += gain_part

    for block in range(2):
        rows = slice(block * 256, block * 256 + 256)
        datt_ref[rows, :] = nt(branch_ref[rows, :], wo_ref[...]).astype(bf16)
    half = heads_cols
    grad = tn(att_ref[...], branch_ref[...])
    grads_ref[0, 0], grads_ref[0, 1] = grad[:, :half], grad[:, half:]

    for t in range(pairs):
        cols = slice(t * LANES, (t + 1) * LANES)
        key_pair, value_pair = k_ref[:, cols], v_ref[:, cols]
        dk_acc[...] = jnp.zeros_like(dk_acc)
        dv_acc[...] = jnp.zeros_like(dv_acc)
        query_grads = [None] * 4
        for which in range(2):
            mask = head_mask(key_pair.shape[0], which)
            key_head = jnp.where(mask, key_pair, jnp.zeros_like(key_pair))
            value_head = jnp.where(mask, value_pair, jnp.zeros_like(value_pair))
            small = head_mask(HALF, which)
            for case, (query_row, first, width, key_row) in enumerate(CASES):
                rows = slice(query_row, query_row + HALF)
                keys = slice(key_row, key_row + width)
                low = prob_ref[2 * t + which, :, first : first + width]
                wide = low.astype(f32)
                delta_head = datt_ref[rows, cols]
                g = nt(delta_head, value_head[keys])
                weighted = wide * g
                scores_back = (weighted - wide * jnp.sum(weighted, axis=1, keepdims=True)).astype(bf16)
                part = mm(scores_back, key_head[keys])
                query_grads[case] = part if query_grads[case] is None else query_grads[case] + part
                query = q_ref[rows, cols]
                query = jnp.where(small, query, jnp.zeros_like(query))
                delta_head = jnp.where(small, delta_head, jnp.zeros_like(delta_head))
                dk_acc[keys, :] += tn(scores_back, query)
                dv_acc[keys, :] += tn(low, delta_head)
        for block in range(4):
            rows = slice(block * HALF, block * HALF + HALF)
            places = slice((block % 2) * HALF, (block % 2) * HALF + HALF)
            key_rows = slice(KEY_PLACE[block] * HALF, KEY_PLACE[block] * HALF + HALF)
            cosine, sine = cos_ref[places, :], sin_ref[places, :]
            grad = query_grads[block] * score_scale
            dq_ref[rows, cols] = (grad * cosine - swap_halves(grad) * sine).astype(bf16)
            grad = dk_acc[key_rows, :]
            dk_ref[rows, cols] = (grad * cosine - swap_halves(grad) * sine).astype(bf16)
            dv_ref[rows, cols] = dv_acc[key_rows, :].astype(bf16)

    for block in range(2):
        rows = slice(block * 256, block * 256 + 256)
        part_ref[rows, :] = (
            nt(dq_ref[rows, :], wq_ref[...]) + nt(dk_ref[rows, :], wk_ref[...]) + nt(dv_ref[rows, :], wv_ref[...])
        )

    @pl.loop(0, row_count // 64)
    def _(i):
        rows = pl.ds(pl.multiple_of(i * 64, 64), 64)
        gnorm_ref[1:2, :] += jnp.sum(part_ref[rows, :] * scaled_rows(x_ref[rows, :].astype(f32)), axis=0, keepdims=True)

    vec_ref[...] = jnp.zeros_like(vec_ref)
    row = 0
    once = jnp.where(lax.axis_index("mp") == 0, 1.0, 0.0)
    for values in (gnorm_ref[1:2, :], gnorm_ref[0:1, :] * once, gbd_ref[...] * once, gbu_ref[...]):
        for first in range(0, values.shape[1], half):
            vec_ref[row : row + 1, :] = values[:, first : first + half]
            row += 1

    for matrix, grad_rows in ((1, dq_ref), (2, dk_ref), (3, dv_ref)):
        grad = tn(normed_ref[...], grad_rows[...])
        grads_ref[matrix, 0], grads_ref[matrix, 1] = grad[:half], grad[half:]
    for place in range(PLANE):
        quarter = quarter_at(place)
        place_quarter(outs[:2], place, grads_ref[quarter, 0])
        place_quarter(outs[2:], place, grads_ref[quarter, 1])


def input_kernel(mine_ref, theirs_ref, x_ref, gain_ref, delta_ref, grad_ref):
    @pl.loop(0, x_ref.shape[0] // 64)
    def _(i):
        rows = pl.ds(pl.multiple_of(i * 64, 64), 64)
        delta = mine_ref[rows, :] + theirs_ref[rows, :]
        back, _ = norm_back_rows(x_ref[rows, :].astype(f32), gain_ref[...], delta)
        grad_ref[rows, :] = (delta_ref[rows, :] + back).astype(bf16)


def each_block(own_ref, got_ref, put, z_first=False):
    for place in range(PLANE):
        for z in range(STACK):
            first, second = (z, place) if z_first else (place, z)
            value = (got_ref if first // 2 else own_ref)[first % 2, second]
            put(quarter_at(place), fourth_at(z), value)


def unpack_down(own_ref, got_ref, z_own_ref, z_got_ref, out_ref):
    cut, part = own_ref.shape[-1], own_ref.shape[-2]

    def put(quarter, fourth, value):
        out_ref[fourths(quarter * STACK + fourth, part), :cut] = value

    def put_z(quarter, fourth, value):
        out_ref[fourths(quarter * STACK + fourth, part), cut:] = value[:part]

    each_block(own_ref, got_ref, put)
    each_block(z_own_ref, z_got_ref, put_z, True)


def unpack_up(own_ref, got_ref, z_own_ref, z_got_ref, out_ref):
    cut, part = own_ref.shape[-1], own_ref.shape[-2]
    rest = z_own_ref.shape[-1] // 2

    def put(quarter, fourth, value):
        cols = pl.ds(pl.multiple_of(quarter * (cut + rest), LANES), cut)
        out_ref[fourths(fourth, part), cols] = value

    def put_z(quarter, fourth, value):
        cols = pl.ds(pl.multiple_of(quarter * (cut + rest) + cut, LANES), rest)
        for half in range(2):
            out_ref[fourths(fourth * 2 + half, part // 2), cols] = value[part // 2 :, half * rest : (half + 1) * rest]

    each_block(own_ref, got_ref, put)
    each_block(z_own_ref, z_got_ref, put_z, True)


def unpack_attention(own_a, got_a, own_b, got_b, *outs):
    grads_ref = outs[4]
    for portion, (own_ref, got_ref) in enumerate(((own_a, got_a), (own_b, got_b))):

        def put(quarter, fourth, value, portion=portion):
            grads_ref[quarter, portion, fourths(fourth, value.shape[0])] = value

        each_block(own_ref, got_ref, put)
    finish_att(outs)


def finish_att(outs):
    *outs, grads_ref, sems = outs
    half = grads_ref.shape[-1]
    copies = []
    for matrix, out in enumerate(outs):
        for portion in range(2):
            place = pl.ds(portion * half, half)
            target = out.at[place, :] if matrix else out.at[:, place]
            copies.append((grads_ref.at[matrix, portion], target))
    for copy in fetch(copies, sems):
        copy.wait()


VMEM = pl.BlockSpec(memory_space=pltpu.VMEM)
HBM = pl.BlockSpec(memory_space=pltpu.HBM)


def call(kernel, outs, held=(), loose=(), scratch=(), flops=0, limit=40, loose_outs=None):
    ins = [*held, *loose]
    shapes = [jax.ShapeDtypeStruct(shape, dtype) for shape, dtype in outs]
    moved = sum(math.prod(a.shape) * a.dtype.itemsize for a in ins + shapes)
    out_specs = [HBM if loose_outs and i in loose_outs else VMEM for i in range(len(outs))]
    return pl.pallas_call(
        kernel,
        name=kernel.__name__,
        out_shape=shapes,
        in_specs=[VMEM] * len(held) + [HBM] * len(loose),
        out_specs=out_specs,
        scratch_shapes=[s if not isinstance(s, tuple) else pltpu.VMEM(*s) for s in scratch],
        compiler_params=pltpu.CompilerParams(vmem_limit_bytes=limit * 1024 * 1024),
        cost_estimate=pl.CostEstimate(flops=flops, bytes_accessed=moved, transcendentals=0),
    )(*ins)


def on_device(
    count,
    inputs, norm_attn, w_query, w_key, w_value, w_out, norm_mlp, w_up, b_up, w_down, b_down, cotangent,
    doc_lengths, pad_counts,
):
    rows, width = inputs.shape
    heads_cols = w_query.shape[1]
    units = w_up.shape[1]
    heads = heads_cols // HEAD
    cosine, sine = (jnp.asarray(t) for t in rope_tables())
    gain_attn, gain_mlp = norm_attn.reshape(1, -1), norm_mlp.reshape(1, -1)

    def swap(values):
        return lax.ppermute(values, "mp", [(0, 1), (1, 0)])

    def flip(values, bits, name):
        pairs = [(2 * i + core, 2 * (i ^ bits[core]) + core) for i in range(count) for core in range(2)]
        with jax.named_scope(name):
            return lax.ppermute(values, ("dp", "mp"), pairs)

    def sems(n):
        return pltpu.SemaphoreType.DMA((n,))

    half = heads_cols

    def portions(*shape):
        return [((2, STACK) + shape, f32)] * 2

    last = []

    def turn(*values):
        if not last:
            return values
        values, _ = lax.optimization_barrier((values, last.pop()))
        return values

    def did(value):
        last[:] = [value]
        return value

    def over_groups(values):
        if count == GROUP:
            return values
        groups = [[k * GROUP + j for k in range(count // GROUP)] for j in range(GROUP)]
        return lax.psum(values, "dp", axis_index_groups=groups)

    def chain(name, parts, result, z_first=False, vec=None):
        keep, send = parts
        plane, stack = [(FIRST, "first"), (SECOND, "second")], [(Z_FIRST, "z_first"), (Z_SECOND, "z_second")]
        steps = stack + plane if z_first else plane + stack

        def join(values):
            return values if vec is None else jnp.concatenate([values.reshape(-1, values.shape[-1]), vec], 0)

        def part_of(got, like, vec):
            if vec is None:
                return got, None
            return got[: -vec.shape[0]].reshape(like.shape), vec + got[-vec.shape[0] :]

        for step, (bits, label) in enumerate(steps):
            if step:
                keep, got, vec = turn(keep, got, vec)
                got, vec = part_of(got, keep, vec)
            if step == 0:
                send = join(send)
            elif step == 1:
                send, keep = did(join(keep[1] + got[1])), keep[0] + got[0]
            elif step == 2:
                send, keep = did(join(keep[2:] + got[2:])), keep[:2] + got[:2]
            else:
                keep = keep + got
                send = did(join(keep))
            got = flip(send, bits, f"{name}_sum_{label}")
            yield
        keep, got, vec = turn(keep, got, vec)
        got, vec = part_of(got, keep, vec)
        own = over_groups(did(keep + got[::-1]))
        if vec is not None:
            result.append(over_groups(vec))
        for step, (bits, label) in enumerate(reversed(steps[:3])):
            got = flip(own, bits, f"{name}_gather_{label}")
            yield
            own, got = turn(own, got)
            if step < 2:
                own = did(jnp.stack([own, got]) if step == 1 else jnp.concatenate([own, got], 0))
        did(got)
        result.extend((own, got))
        yield

    scores = (heads, HALF, 8 * LANES)
    rows_of = {"width": ((rows, width), bf16), "heads": ((rows, heads_cols), bf16), "sum": ((rows, width), f32)}
    outs = [rows_of["width"]] + [rows_of["heads"]] * 4 + [(scores, bf16), rows_of["sum"]]
    normed, q, k, v, attended, probs, branch = call(
        attention_forward,
        outs,
        loose=[doc_lengths, pad_counts, norm_attn, inputs, w_query, w_key, w_value, cosine, sine, w_out],
        scratch=[
            (scores[1:], f32),
            pltpu.SMEM(doc_lengths.shape, jnp.int32),
            pltpu.SMEM(pad_counts.shape, jnp.int32),
            (norm_attn.shape, f32),
            rows_of["width"],
            *[((width, heads_cols), bf16)] * 3,
            (cosine.shape, f32),
            (sine.shape, f32),
            ((heads_cols, width), bf16),
            *outs,
            sems(10),
            sems(10),
        ],
        flops=2 * rows * width * heads_cols * 4,
        limit=62,
        loose_outs=range(7),
    )
    branch_other = swap(branch)

    big = [
        *portions(units // GROUP, width * 2 // 3),
        *portions(units // GROUP + width // STACK // 2, width // 3),
        *portions(width // STACK, units // PLANE * 2 // 3),
        ((2, rows, width), f32),
    ]
    residual, grad_bu, grad_bd, *parts, shares = call(
        mlp_kernel,
        [rows_of["sum"], ((1, units), f32), ((1, width), f32), *big],
        loose=[norm_mlp, b_up, inputs, branch, branch_other, cotangent, w_up, w_down],
        scratch=[
            (norm_mlp.shape, f32),
            (b_up.shape, f32),
            rows_of["width"],
            rows_of["sum"],
            rows_of["sum"],
            rows_of["width"],
            ((width, units), bf16),
            ((units, width), bf16),
            rows_of["sum"],
            rows_of["width"],
            ((rows, units), bf16),
            ((rows, units), bf16),
            *big,
            sems(11),
            sems(9),
        ],
        flops=2 * rows * width * units * 6,
        limit=62,
        loose_outs=(0, *range(3, 10)),
    )
    made, grads = {key: [] for key in "dcuab"}, {}
    chains = {
        "d": chain("down", parts[:2], made["d"]),
        "c": chain("down_stack", parts[2:4], made["c"], True),
        "u": chain("up", parts[4:], made["u"]),
    }
    state = {"shares_other": swap(shares)}

    def backward():
        (shares_other,) = turn(state["shares_other"])
        state["output"], state["delta_residual"], vec, state["normed_part"], *parts = call(
            attention_backward,
            [((rows, width), bf16), ((rows, width), f32), ((16, half), f32), ((rows, width), f32)]
            + portions(half // STACK, half) * 2,
            held=[
                shares, shares_other, residual, gain_mlp, cotangent, attended, w_out, q, k, v, probs,
                normed, w_query, w_key, w_value, cosine, sine, inputs, b_down.reshape(1, -1), grad_bd, grad_bu,
            ],
            scratch=[
                ((rows, width), bf16),
                ((rows, heads_cols), bf16),
                ((rows, heads_cols), bf16),
                ((rows, heads_cols), bf16),
                ((rows, heads_cols), bf16),
                ((rows, LANES), f32),
                ((rows, LANES), f32),
                ((PLANE, 2, half, half), f32),
                ((8, width), f32),
            ],
            flops=2 * rows * width * heads_cols * 10,
        )
        did(vec)
        state["normed_other"] = swap(state["normed_part"])
        chains["a"] = chain("attention", parts[:2], made["a"], vec=vec)
        chains["b"] = chain("attention_rest", parts[2:], made["b"])

    def input_back():
        (normed_other,) = turn(state["normed_other"])
        (state["grad_inputs"],) = call(
            input_kernel,
            [((rows, width), bf16)],
            held=[state["normed_part"], normed_other, inputs, gain_attn, state["delta_residual"]],
        )
        did(state["grad_inputs"])

    def unpack():
        if "down" not in grads and len(made["d"]) == len(made["c"]) == 2:
            grads["down"] = call(unpack_down, [((units, width), f32)], held=made["d"] + made["c"])
            did(grads["down"][0])
        if "up" not in grads and len(made["u"]) == len(made["c"]) == 2:
            grads["up"] = call(unpack_up, [((width, units), f32)], held=made["u"] + made["c"])
            did(grads["up"][0])
        if "attention" not in grads and len(made["a"]) == 3 and len(made["b"]) == 2:
            grads["attention"] = call(
                unpack_attention,
                [((heads_cols, width), f32)] + [((width, heads_cols), f32)] * 3,
                held=made["a"][1:] + made["b"],
                scratch=[((PLANE, 2, half, half), f32), sems(8)],
                loose_outs=range(4),
            )

    did(grad_bd)
    pieces = {"K": backward, "I": input_back}
    for key in ORDER:
        if key in pieces:
            pieces[key]()
        else:
            next(chains[key])
            unpack()
    assert len(grads) == 3

    vec = made["a"][0]
    n = width // half
    shared = (vec[: 3 * n] + swap(vec[: 3 * n])).reshape(3, width)
    grad_bu = vec[3 * n :].reshape(-1)[:units]
    (grad_down,), (grad_up,) = grads["down"], grads["up"]
    grad_out, grad_query, grad_key, grad_value = grads["attention"]
    output, grad_inputs = state["output"], state["grad_inputs"]
    return (
        output,
        grad_inputs,
        shared[0],
        grad_query,
        grad_key,
        grad_value,
        grad_out,
        shared[1],
        grad_up,
        grad_bu,
        grad_down,
        shared[2],
    )


def solution(mesh):
    count = mesh.shape["dp"]

    def step(*args):
        return on_device(count, *args)

    return jax.shard_map(
        step,
        mesh=mesh,
        in_specs=(
            P("dp", None),
            P(),
            P(None, "mp"),
            P(None, "mp"),
            P(None, "mp"),
            P("mp", None),
            P(),
            P(None, "mp"),
            P("mp"),
            P("mp", None),
            P(),
            P("dp", None),
            P(),
            P(),
        ),
        out_specs=(
            P("dp", None),
            P("dp", None),
            P(),
            P(None, "mp"),
            P(None, "mp"),
            P(None, "mp"),
            P("mp", None),
            P(),
            P(None, "mp"),
            P("mp"),
            P("mp", None),
            P(),
        ),
        check_vma=False,
    )
```

```python
from functools import partial
import math

import numpy as np

import jax
import jax.numpy as jnp
from jax import lax
from jax.experimental import pallas as pl
from jax.experimental.pallas import tpu as pltpu
from jax.sharding import PartitionSpec as P

HEAD = 64
BLOCK = 16
LEN = 256
HALF = 128
LANES = 128
PLANE = 4
STACK = 4
GROUP = PLANE * STACK

norm_eps = 1e-05
rope_base = 10000.0
masked_score = -1e30
score_scale = HEAD ** (-0.5)
bf16 = jnp.bfloat16
f32 = jnp.float32

X, Y, Z1, Z2 = 1, 2, 4, 8
FIRST, SECOND = (X, Y), (Y, X)
Z_FIRST, Z_SECOND = (Z1, Z2), (Z2, Z1)

ORDER = "cduKdcudbuIbdcuabdcaucbdaucdabuabcdaubabac"

CASES = ((0, 0, 256, 0), (128, 256, 384, 128), (256, 640, 128, 128), (384, 768, 256, 128))
TILES = (
    (0, 0, 0, 0),
    (0, 1, 0, 0),
    (0, 1, 128, 0),
    (0, 1, 128, 128),
    (0, 0, 128, 128),
    (1, 1, 0, 0),
    (1, 1, 128, 0),
    (1, 1, 128, 128),
)
KEY_PLACE = (0, 3, 1, 2)


def mm(left, right):
    return jnp.dot(left, right, preferred_element_type=f32)


def tn(left, right):
    return lax.dot_general(left, right, (((0,), (0,)), ((), ())), preferred_element_type=f32)


def nt(left, right):
    return lax.dot_general(left, right, (((1,), (1,)), ((), ())), preferred_element_type=f32)


def rope_tables():
    half = HEAD // 2
    frequency = np.exp(np.arange(half) * (-2.0 * math.log(rope_base) / HEAD)).astype(np.float32)
    turn = (np.arange(LEN, dtype=np.float32)[:, None] * frequency[None, :]).astype(np.float32)
    cosine, sine = np.cos(turn.astype(np.float64)), np.sin(turn.astype(np.float64))
    cosine = np.tile(cosine, (1, LANES // half)).astype(np.float32)
    sine = np.tile(np.concatenate([-sine, sine], 1), (1, LANES // HEAD)).astype(np.float32)
    return cosine, sine


def swap_halves(values):
    lane = lax.broadcasted_iota(jnp.int32, values.shape, 1)
    return jnp.where(
        lane % HEAD < HEAD // 2, pltpu.roll(values, LANES - HEAD // 2, 1), pltpu.roll(values, HEAD // 2, 1)
    )


def head_mask(rows, which):
    lane = lax.broadcasted_iota(jnp.int32, (rows, LANES), 1)
    return (lane >= HEAD) if which else (lane < HEAD)


def layer_norm_rows(values, gain):
    centred = values - jnp.mean(values, axis=-1, keepdims=True)
    spread = jnp.mean(centred * centred, axis=-1, keepdims=True)
    return centred * lax.rsqrt(spread + norm_eps) * gain


def scaled_rows(values):
    centred = values - jnp.mean(values, axis=-1, keepdims=True)
    return centred * lax.rsqrt(jnp.mean(centred * centred, axis=-1, keepdims=True) + norm_eps)


def norm_back_rows(values, gain, delta):
    centred = values - jnp.mean(values, axis=-1, keepdims=True)
    spread = jnp.mean(centred * centred, axis=-1, keepdims=True)
    s = lax.rsqrt(spread + norm_eps)
    xhat = centred * s
    e = delta * gain
    back = s * (e - jnp.mean(e, axis=-1, keepdims=True) - xhat * jnp.mean(e * xhat, axis=-1, keepdims=True))
    return back, jnp.sum(delta * xhat, axis=0, keepdims=True)


def fill_bias(lengths_ref, pads_ref, bias_ref):
    sequence = lax.axis_index("dp")
    docs = lengths_ref.shape[1]
    ends, total = [], jnp.int32(0)
    for j in range(docs):
        total = total + lengths_ref[sequence, j]
        ends.append(total)
    first_pad = LEN - pads_ref[sequence]

    def segment(places):
        seg = jnp.zeros(places.shape, jnp.int32)
        for end in ends:
            seg = seg + (places >= end).astype(jnp.int32)
        return seg

    rows, cols, row_seg, col_seg = {}, {}, {}, {}
    for base in (0, HALF):
        rows[base] = lax.broadcasted_iota(jnp.int32, (HALF, LANES), 0) + base
        cols[base] = lax.broadcasted_iota(jnp.int32, (HALF, LANES), 1) + base
        row_seg[base] = segment(rows[base])
        col_seg[base] = segment(cols[base])
    for tile, (query_kind, key_kind, query_base, key_base) in enumerate(TILES):
        q, k = rows[query_base], cols[key_base]
        query_block, key_block = q // BLOCK, k // BLOCK
        same_doc = (row_seg[query_base] == col_seg[key_base]) & (k < first_pad)
        if query_kind == 0 and key_kind == 0:
            ok = (key_block == query_block) & (same_doc | (q == k))
        elif query_kind == 0:
            ok = (key_block < query_block) & same_doc
        else:
            ok = (key_block <= query_block) & (same_doc | (q == k))
        bias_ref[:, tile * LANES : (tile + 1) * LANES] = jnp.where(ok, 0.0, masked_score)


def fetch(pairs, sems):
    copies = [pltpu.make_async_copy(source, target, sems.at[i]) for i, (source, target) in enumerate(pairs)]
    for copy in copies:
        copy.start()
    return copies


class Sender:
    def __init__(self, sems):
        self.sems, self.copies = sems, []

    def send(self, source, target):
        self.copies.append(pltpu.make_async_copy(source, target, self.sems.at[len(self.copies)]))
        self.copies[-1].start()

    def finish(self):
        for copy in self.copies:
            copy.wait()


def attention_forward(
    lengths_in, pads_in, gain_in, x_in, wq_in, wk_in, wv_in, cos_in, sin_in, wo_in,
    normed_out, q_out, k_out, v_out, att_out, prob_out, part_out,
    bias_ref, lengths_ref, pads_ref, gain_ref, x_ref, wq_ref, wk_ref, wv_ref, cos_ref, sin_ref, wo_ref,
    normed_ref, q_ref, k_ref, v_ref, att_ref, prob_ref, part_ref, sems, out_sems,
):
    first = fetch(((lengths_in, lengths_ref), (pads_in, pads_ref), (x_in, x_ref), (gain_in, gain_ref)), sems.at[:4])
    copies = fetch(
        (
            (wq_in, wq_ref), (wk_in, wk_ref), (wv_in, wv_ref), (cos_in, cos_ref), (sin_in, sin_ref), (wo_in, wo_ref),
        ),
        sems.at[4:],
    )
    sender = Sender(out_sems)
    first[0].wait()
    first[1].wait()
    heads_cols = wq_ref.shape[1]
    pairs = heads_cols // LANES
    fill_bias(lengths_ref, pads_ref, bias_ref)
    first[2].wait()
    first[3].wait()
    gain = gain_ref[...].reshape(1, -1)

    @pl.loop(0, x_ref.shape[0] // 64)
    def _(i):
        rows = pl.ds(pl.multiple_of(i * 64, 64), 64)
        normed_ref[rows, :] = layer_norm_rows(x_ref[rows, :].astype(f32), gain).astype(bf16)

    sender.send(normed_ref, normed_out)
    for copy in copies[:5]:
        copy.wait()
    for block in range(4):
        rows = slice(block * HALF, block * HALF + HALF)
        places = slice((block % 2) * HALF, (block % 2) * HALF + HALF)
        key_rows = slice(KEY_PLACE[block] * HALF, KEY_PLACE[block] * HALF + HALF)
        normed = normed_ref[rows, :]
        cosine, sine = cos_ref[places, :], sin_ref[places, :]
        query, key = mm(normed, wq_ref[...]), mm(normed, wk_ref[...])
        for t in range(pairs):
            cols = slice(t * LANES, (t + 1) * LANES)
            turned = query[:, cols] * cosine + swap_halves(query[:, cols]) * sine
            q_ref[rows, cols] = (turned.astype(bf16).astype(f32) * score_scale).astype(bf16)
            turned = key[:, cols] * cosine + swap_halves(key[:, cols]) * sine
            k_ref[key_rows, cols] = turned.astype(bf16)
        v_ref[key_rows, :] = mm(normed, wv_ref[...]).astype(bf16)
    for source, target in ((q_ref, q_out), (k_ref, k_out), (v_ref, v_out)):
        sender.send(source, target)

    for t in range(pairs):
        cols = slice(t * LANES, (t + 1) * LANES)
        key_pair, value_pair = k_ref[:, cols], v_ref[:, cols]
        mixed = [None] * 4
        for which in range(2):
            mask = head_mask(key_pair.shape[0], which)
            key_head = jnp.where(mask, key_pair, jnp.zeros_like(key_pair))
            value_head = jnp.where(mask, value_pair, jnp.zeros_like(value_pair))
            for case, (query_row, first, width, key_row) in enumerate(CASES):
                scores = nt(q_ref[query_row : query_row + HALF, cols], key_head[key_row : key_row + width])
                scores = scores + bias_ref[:, first : first + width]
                weights = jnp.exp(scores - jnp.max(scores, axis=1, keepdims=True))
                low = (weights * (1.0 / jnp.sum(weights, axis=1, keepdims=True))).astype(bf16)
                prob_ref[2 * t + which, :, first : first + width] = low
                part = mm(low, value_head[key_row : key_row + width])
                mixed[case] = part if mixed[case] is None else mixed[case] + part
        for case, (query_row, _, _, _) in enumerate(CASES):
            att_ref[query_row : query_row + HALF, cols] = mixed[case].astype(bf16)
        sender.send(prob_ref.at[2 * t : 2 * t + 2], prob_out.at[2 * t : 2 * t + 2])

    sender.send(att_ref, att_out)
    copies[5].wait()
    for block in range(2):
        rows = slice(block * 256, block * 256 + 256)
        part_ref[rows, :] = mm(att_ref[rows, :], wo_ref[...])
        sender.send(part_ref.at[rows, :], part_out.at[rows, :])
    sender.finish()


def fourths(start, part):
    return pl.ds(pl.multiple_of(start * part, 8), part)


def slot_at(place):
    core = lax.axis_index("mp") % 2
    return (place // 2) * (1 + core) + (place % 2) * (2 - core)


def quarter_at(place):
    return lax.axis_index("dp") % PLANE ^ slot_at(place)


def fourth_at(place):
    return lax.axis_index("dp") % GROUP // PLANE ^ slot_at(place)


def z_place(block):
    slot = lax.axis_index("dp") % GROUP // PLANE ^ block
    return jnp.where(lax.axis_index("mp") % 2 == 0, (slot % 2) * 2 + slot // 2, slot)


def place_quarter(outs, place, value):
    part = value.shape[0] // STACK
    for block in range(STACK):
        outs[place // 2][place % 2, z_place(block)] = value[block * part : (block + 1) * part]


def place_quarter_z_first(outs, place, first_row, value):
    part = value.shape[0] // STACK
    for block in range(STACK):
        z = z_place(block)
        for sent in range(2):

            @pl.when(z // 2 == sent)
            def _(out=outs[sent], z=z, piece=value[block * part : (block + 1) * part]):
                out[z % 2, place, first_row : first_row + part, :] = piece


def mlp_kernel(
    gain_in, bu_in, x_in, mine_in, theirs_in, cot_in, wu_in, wd_in,
    residual_out, gbu_ref, gbd_ref, d_kept, d_sent, c_kept, c_sent, u_kept, u_sent, shares_out,
    gain_ref, bu_ref, x_ref, mine_ref, theirs_ref, cot_ref, wu_ref, wd_ref,
    residual_ref, normed_ref, act_ref, du_ref, d_kept_ref, d_sent_ref, c_kept_ref, c_sent_ref, u_kept_ref, u_sent_ref, shares_ref,
    sems, out_sems,
):
    row_count = x_ref.shape[0]
    units = wu_ref.shape[1]
    halves = (slice(0, row_count // 2), slice(row_count // 2, row_count))
    pairs = [(gain_in, gain_ref), (bu_in, bu_ref)]
    for rows in halves:
        pairs += [(a.at[rows, :], b.at[rows, :]) for a, b in ((x_in, x_ref), (mine_in, mine_ref), (theirs_in, theirs_ref))]
    copies = fetch(pairs + [(cot_in, cot_ref), (wu_in, wu_ref), (wd_in, wd_ref)], sems)
    sender = Sender(out_sems)
    gbu_ref[...] = jnp.zeros_like(gbu_ref)
    gbd_ref[...] = jnp.zeros_like(gbd_ref)
    copies[0].wait()
    gain = gain_ref[...].reshape(1, -1)
    for half in range(2):
        for copy in copies[2 + 3 * half : 5 + 3 * half]:
            copy.wait()

        @pl.loop(0, row_count // 128)
        def _(i, half=half):
            rows = pl.ds(pl.multiple_of(half * (row_count // 2) + i * 64, 64), 64)
            residual = x_ref[rows, :].astype(f32) + (mine_ref[rows, :] + theirs_ref[rows, :])
            residual_ref[rows, :] = residual
            normed_ref[rows, :] = layer_norm_rows(residual, gain).astype(bf16)

    sender.send(residual_ref, residual_out)
    for copy in (copies[1], *copies[8:]):
        copy.wait()
    c0 = math.sqrt(2.0 / math.pi)
    c1 = c0 * 0.044715

    @pl.loop(0, units // 256)
    def _(j):
        cols = pl.ds(pl.multiple_of(j * 256, 256), 256)
        for block in range(row_count // 256):
            rows = slice(block * 256, block * 256 + 256)
            u = mm(normed_ref[rows, :], wu_ref[:, cols]) + bu_ref[cols].reshape(1, -1)
            delta = nt(cot_ref[rows, :], wd_ref[cols, :])
            square = u * u
            t = jnp.tanh(u * (c0 + c1 * square))
            half_up = 0.5 * (1.0 + t)
            act_ref[rows, cols] = (u * half_up).astype(bf16)
            slope = half_up + (0.5 * u) * (1.0 - t * t) * (c0 + (3.0 * c1) * square)
            low = (delta * slope).astype(bf16)
            du_ref[rows, cols] = low
            gbu_ref[:, cols] += jnp.sum(low.astype(f32), axis=0, keepdims=True)

    quarter = units // PLANE
    fourth = units // GROUP
    cut = cot_ref.shape[1] * 2 // 3
    up_cut = quarter * 2 // 3
    quarters = {}
    for place in range(PLANE):
        quarters[place] = pl.ds(pl.multiple_of(quarter_at(place) * quarter, LANES), quarter)
    for place in (2, 3, 0, 1):
        grad = tn(act_ref[:, quarters[place]], cot_ref[...])
        place_quarter((d_kept_ref, d_sent_ref), place, grad[:, :cut])
        place_quarter_z_first((c_kept_ref, c_sent_ref), place, 0, grad[:, cut:])
        if place == 3:
            sender.send(d_sent_ref, d_sent)
    sender.send(d_kept_ref, d_kept)
    for place in (2, 3, 0, 1):
        grad = tn(normed_ref[...], du_ref[:, quarters[place]])
        place_quarter((u_kept_ref, u_sent_ref), place, grad[:, :up_cut])
        rest = grad[:, up_cut:].reshape(STACK, 2, fourth, -1)
        rest = jnp.concatenate([rest[:, 0], rest[:, 1]], 2).reshape(STACK * fourth, -1)
        place_quarter_z_first((c_kept_ref, c_sent_ref), place, fourth, rest)
        if place == 3:
            sender.send(u_sent_ref, u_sent)
    for source, target in ((c_sent_ref, c_sent), (u_kept_ref, u_kept), (c_kept_ref, c_kept)):
        sender.send(source, target)
    for share in range(2):
        for rows in halves:
            if share == 0:
                shares_ref[share, rows, :] = nt(du_ref[rows, :], wu_ref[...])
            else:
                shares_ref[share, rows, :] = mm(act_ref[rows, :], wd_ref[...])
        sender.send(shares_ref.at[share], shares_out.at[share])

    @pl.loop(0, row_count // 64)
    def _(i):
        rows = pl.ds(pl.multiple_of(i * 64, 64), 64)
        gbd_ref[...] += jnp.sum(cot_ref[rows, :].astype(f32), axis=0, keepdims=True)

    sender.finish()


def attention_backward(
    mine_ref, theirs_ref, residual_ref, gain_ref, cot_ref, att_ref, wo_ref, q_ref, k_ref, v_ref, prob_ref,
    normed_ref, wq_ref, wk_ref, wv_ref, cos_ref, sin_ref, x_ref, bd_ref, gbd_ref, gbu_ref,
    output_ref, delta_ref, vec_ref, part_ref, *outs_and_scratch,
):
    *outs, branch_ref, datt_ref, dq_ref, dk_ref, dv_ref, dk_acc, dv_acc, grads_ref, gnorm_ref = outs_and_scratch
    row_count = residual_ref.shape[0]
    heads_cols = wq_ref.shape[1]
    pairs = heads_cols // LANES
    gnorm_ref[...] = jnp.zeros_like(gnorm_ref)

    @pl.loop(0, row_count // 64)
    def _(i):
        rows = pl.ds(pl.multiple_of(i * 64, 64), 64)
        delta = mine_ref[0, rows, :] + theirs_ref[0, rows, :]
        residual = residual_ref[rows, :]
        output_ref[rows, :] = (residual + (mine_ref[1, rows, :] + theirs_ref[1, rows, :]) + bd_ref[...]).astype(bf16)
        back, gain_part = norm_back_rows(residual, gain_ref[...], delta)
        back = back + cot_ref[rows, :].astype(f32)
        delta_ref[rows, :] = back
        branch_ref[rows, :] = back.astype(bf16)
        gnorm_ref[0:1, :] += gain_part

    for block in range(2):
        rows = slice(block * 256, block * 256 + 256)
        datt_ref[rows, :] = nt(branch_ref[rows, :], wo_ref[...]).astype(bf16)
    half = heads_cols
    grad = tn(att_ref[...], branch_ref[...])
    grads_ref[0, 0], grads_ref[0, 1] = grad[:, :half], grad[:, half:]

    for t in range(pairs):
        cols = slice(t * LANES, (t + 1) * LANES)
        key_pair, value_pair = k_ref[:, cols], v_ref[:, cols]
        dk_acc[...] = jnp.zeros_like(dk_acc)
        dv_acc[...] = jnp.zeros_like(dv_acc)
        query_grads = [None] * 4
        for which in range(2):
            mask = head_mask(key_pair.shape[0], which)
            key_head = jnp.where(mask, key_pair, jnp.zeros_like(key_pair))
            value_head = jnp.where(mask, value_pair, jnp.zeros_like(value_pair))
            small = head_mask(HALF, which)
            for case, (query_row, first, width, key_row) in enumerate(CASES):
                rows = slice(query_row, query_row + HALF)
                keys = slice(key_row, key_row + width)
                low = prob_ref[2 * t + which, :, first : first + width]
                wide = low.astype(f32)
                delta_head = datt_ref[rows, cols]
                g = nt(delta_head, value_head[keys])
                weighted = wide * g
                scores_back = (weighted - wide * jnp.sum(weighted, axis=1, keepdims=True)).astype(bf16)
                part = mm(scores_back, key_head[keys])
                query_grads[case] = part if query_grads[case] is None else query_grads[case] + part
                query = q_ref[rows, cols]
                query = jnp.where(small, query, jnp.zeros_like(query))
                delta_head = jnp.where(small, delta_head, jnp.zeros_like(delta_head))
                dk_acc[keys, :] += tn(scores_back, query)
                dv_acc[keys, :] += tn(low, delta_head)
        for block in range(4):
            rows = slice(block * HALF, block * HALF + HALF)
            places = slice((block % 2) * HALF, (block % 2) * HALF + HALF)
            key_rows = slice(KEY_PLACE[block] * HALF, KEY_PLACE[block] * HALF + HALF)
            cosine, sine = cos_ref[places, :], sin_ref[places, :]
            grad = query_grads[block] * score_scale
            dq_ref[rows, cols] = (grad * cosine - swap_halves(grad) * sine).astype(bf16)
            grad = dk_acc[key_rows, :]
            dk_ref[rows, cols] = (grad * cosine - swap_halves(grad) * sine).astype(bf16)
            dv_ref[rows, cols] = dv_acc[key_rows, :].astype(bf16)

    for block in range(2):
        rows = slice(block * 256, block * 256 + 256)
        part_ref[rows, :] = (
            nt(dq_ref[rows, :], wq_ref[...]) + nt(dk_ref[rows, :], wk_ref[...]) + nt(dv_ref[rows, :], wv_ref[...])
        )

    @pl.loop(0, row_count // 64)
    def _(i):
        rows = pl.ds(pl.multiple_of(i * 64, 64), 64)
        gnorm_ref[1:2, :] += jnp.sum(part_ref[rows, :] * scaled_rows(x_ref[rows, :].astype(f32)), axis=0, keepdims=True)

    vec_ref[...] = jnp.zeros_like(vec_ref)
    row = 0
    once = jnp.where(lax.axis_index("mp") == 0, 1.0, 0.0)
    for values in (gnorm_ref[1:2, :], gnorm_ref[0:1, :] * once, gbd_ref[...] * once, gbu_ref[...]):
        for first in range(0, values.shape[1], half):
            vec_ref[row : row + 1, :] = values[:, first : first + half]
            row += 1

    for matrix, grad_rows in ((1, dq_ref), (2, dk_ref), (3, dv_ref)):
        grad = tn(normed_ref[...], grad_rows[...])
        grads_ref[matrix, 0], grads_ref[matrix, 1] = grad[:half], grad[half:]
    for place in range(PLANE):
        quarter = quarter_at(place)
        place_quarter(outs[:2], place, grads_ref[quarter, 0])
        place_quarter(outs[2:], place, grads_ref[quarter, 1])


def input_kernel(mine_ref, theirs_ref, x_ref, gain_ref, delta_ref, grad_ref):
    @pl.loop(0, x_ref.shape[0] // 64)
    def _(i):
        rows = pl.ds(pl.multiple_of(i * 64, 64), 64)
        delta = mine_ref[rows, :] + theirs_ref[rows, :]
        back, _ = norm_back_rows(x_ref[rows, :].astype(f32), gain_ref[...], delta)
        grad_ref[rows, :] = (delta_ref[rows, :] + back).astype(bf16)


def put_in_place(views, z_first, sent, olds, piece_ref, *refs):
    *refs, sems = refs
    outs = refs[olds:]
    for start in (True, False):
        count = 0
        for i in range(2):
            for j in range(STACK):
                z, place = (2 * sent + i, j) if z_first else (j, 2 * sent + i)
                for wanted, source, target in views(outs, quarter_at(place), fourth_at(z), piece_ref.at[i, j]):
                    copy = pltpu.make_async_copy(source, target, sems.at[count])
                    count += 1
                    act = copy.start if start else copy.wait
                    if wanted is None:
                        act()
                    else:
                        pl.when(wanted)(act)


def down_views(outs, quarter, fourth, block):
    part, cols = block.shape
    yield None, block, outs[0].at[fourths(quarter * STACK + fourth, part), pl.ds(0, cols)]


def up_views(outs, quarter, fourth, block):
    part, cols = block.shape
    whole = outs[0].shape[1] // PLANE
    yield None, block, outs[0].at[fourths(fourth, part), pl.ds(pl.multiple_of(quarter * whole, LANES), cols)]


def stack_views(outs, quarter, fourth, block):
    part, cols = block.shape[0] // 2, block.shape[1]
    whole, rest = outs[1].shape[1] // PLANE, cols // 2
    down_rows, down_cols = fourths(quarter * STACK + fourth, part), pl.ds(outs[0].shape[1] - cols, cols)
    yield None, block.at[pl.ds(0, part), :], outs[0].at[down_rows, down_cols]
    up_cols = pl.ds(pl.multiple_of((quarter + 1) * whole - rest, LANES), rest)
    for half in range(2):
        source = block.at[pl.ds(part, part), pl.ds(half * rest, rest)]
        yield None, source, outs[1].at[fourths(fourth * 2 + half, part), up_cols]


def attention_views(portion, outs, quarter, fourth, block):
    part, half = block.shape[0], block.shape[1]
    for matrix, out in enumerate(outs):
        if matrix:
            target = out.at[pl.ds(pl.multiple_of(portion * half + fourth * part, 8), part), :]
        else:
            target = out.at[fourths(fourth, part), pl.ds(portion * half, half)]
        yield quarter == matrix, block, target


VMEM = pl.BlockSpec(memory_space=pltpu.VMEM)
HBM = pl.BlockSpec(memory_space=pltpu.HBM)


def call(kernel, outs, held=(), loose=(), scratch=(), flops=0, limit=40, loose_outs=None):
    ins = [*held, *loose]
    shapes = [jax.ShapeDtypeStruct(shape, dtype) for shape, dtype in outs]
    moved = sum(math.prod(a.shape) * a.dtype.itemsize for a in ins + shapes)
    out_specs = [HBM if loose_outs and i in loose_outs else VMEM for i in range(len(outs))]
    return pl.pallas_call(
        kernel,
        name=kernel.__name__,
        out_shape=shapes,
        in_specs=[VMEM] * len(held) + [HBM] * len(loose),
        out_specs=out_specs,
        scratch_shapes=[s if not isinstance(s, tuple) else pltpu.VMEM(*s) for s in scratch],
        compiler_params=pltpu.CompilerParams(vmem_limit_bytes=limit * 1024 * 1024),
        cost_estimate=pl.CostEstimate(flops=flops, bytes_accessed=moved, transcendentals=0),
    )(*ins)


def on_device(
    count,
    inputs, norm_attn, w_query, w_key, w_value, w_out, norm_mlp, w_up, b_up, w_down, b_down, cotangent,
    doc_lengths, pad_counts,
):
    rows, width = inputs.shape
    heads_cols = w_query.shape[1]
    units = w_up.shape[1]
    heads = heads_cols // HEAD
    cosine, sine = (jnp.asarray(t) for t in rope_tables())
    gain_attn, gain_mlp = norm_attn.reshape(1, -1), norm_mlp.reshape(1, -1)

    def swap(values):
        return lax.ppermute(values, "mp", [(0, 1), (1, 0)])

    def flip(values, bits, name):
        pairs = [(2 * i + core, 2 * (i ^ bits[core]) + core) for i in range(count) for core in range(2)]
        with jax.named_scope(name):
            return lax.ppermute(values, ("dp", "mp"), pairs)

    def sems(n):
        return pltpu.SemaphoreType.DMA((n,))

    half = heads_cols

    def portions(*shape):
        return [((2, STACK) + shape, f32)] * 2

    last = []

    def turn(*values):
        if not last:
            return values
        values, _ = lax.optimization_barrier((values, last.pop()))
        return values

    def did(value):
        last[:] = [value]
        return value

    def over_groups(values):
        if count == GROUP:
            return values
        groups = [[k * GROUP + j for k in range(count // GROUP)] for j in range(GROUP)]
        return lax.psum(values, "dp", axis_index_groups=groups)

    def chain(name, parts, result, z_first=False, vec=None):
        keep, send = parts
        plane, stack = [(FIRST, "first"), (SECOND, "second")], [(Z_FIRST, "z_first"), (Z_SECOND, "z_second")]
        steps = stack + plane if z_first else plane + stack

        def join(values):
            return values if vec is None else jnp.concatenate([values.reshape(-1, values.shape[-1]), vec], 0)

        def part_of(got, like, vec):
            if vec is None:
                return got, None
            return got[: -vec.shape[0]].reshape(like.shape), vec + got[-vec.shape[0] :]

        for step, (bits, label) in enumerate(steps):
            if step:
                keep, got, vec = turn(keep, got, vec)
                got, vec = part_of(got, keep, vec)
            if step == 0:
                send = join(send)
            elif step == 1:
                send, keep = did(join(keep[1] + got[1])), keep[0] + got[0]
            elif step == 2:
                send, keep = did(join(keep[2:] + got[2:])), keep[:2] + got[:2]
            else:
                keep = keep + got
                send = did(join(keep))
            got = flip(send, bits, f"{name}_sum_{label}")
            yield
        keep, got, vec = turn(keep, got, vec)
        got, vec = part_of(got, keep, vec)
        own = over_groups(did(keep + got[::-1]))
        if vec is not None:
            sums.append(over_groups(vec))
        for step, (bits, label) in enumerate(reversed(steps[:3])):
            got = flip(own, bits, f"{name}_gather_{label}")
            if step == 2:
                result.append(own)
            yield
            own, got = turn(own, got)
            if step < 2:
                own = did(jnp.stack([own, got]) if step == 1 else jnp.concatenate([own, got], 0))
        did(got)
        result.append(got)
        yield

    scores = (heads, HALF, 8 * LANES)
    rows_of = {"width": ((rows, width), bf16), "heads": ((rows, heads_cols), bf16), "sum": ((rows, width), f32)}
    outs = [rows_of["width"]] + [rows_of["heads"]] * 4 + [(scores, bf16), rows_of["sum"]]
    normed, q, k, v, attended, probs, branch = call(
        attention_forward,
        outs,
        loose=[doc_lengths, pad_counts, norm_attn, inputs, w_query, w_key, w_value, cosine, sine, w_out],
        scratch=[
            (scores[1:], f32),
            pltpu.SMEM(doc_lengths.shape, jnp.int32),
            pltpu.SMEM(pad_counts.shape, jnp.int32),
            (norm_attn.shape, f32),
            rows_of["width"],
            *[((width, heads_cols), bf16)] * 3,
            (cosine.shape, f32),
            (sine.shape, f32),
            ((heads_cols, width), bf16),
            *outs,
            sems(10),
            sems(10),
        ],
        flops=2 * rows * width * heads_cols * 4,
        limit=62,
        loose_outs=range(7),
    )
    branch_other = swap(branch)

    big = [
        *portions(units // GROUP, width * 2 // 3),
        *portions(units // GROUP + width // STACK // 2, width // 3),
        *portions(width // STACK, units // PLANE * 2 // 3),
        ((2, rows, width), f32),
    ]
    residual, grad_bu, grad_bd, *parts, shares = call(
        mlp_kernel,
        [rows_of["sum"], ((1, units), f32), ((1, width), f32), *big],
        loose=[norm_mlp, b_up, inputs, branch, branch_other, cotangent, w_up, w_down],
        scratch=[
            (norm_mlp.shape, f32),
            (b_up.shape, f32),
            rows_of["width"],
            rows_of["sum"],
            rows_of["sum"],
            rows_of["width"],
            ((width, units), bf16),
            ((units, width), bf16),
            rows_of["sum"],
            rows_of["width"],
            ((rows, units), bf16),
            ((rows, units), bf16),
            *big,
            sems(11),
            sems(9),
        ],
        flops=2 * rows * width * units * 6,
        limit=62,
        loose_outs=(0, *range(3, 10)),
    )
    made, grads, sums = {key: [] for key in "dcuab"}, {}, []
    chains = {
        "d": chain("down", parts[:2], made["d"]),
        "c": chain("down_stack", parts[2:4], made["c"], True),
        "u": chain("up", parts[4:], made["u"]),
    }
    state = {"shares_other": swap(shares)}

    def backward():
        (shares_other,) = turn(state["shares_other"])
        state["output"], state["delta_residual"], vec, state["normed_part"], *parts = call(
            attention_backward,
            [((rows, width), bf16), ((rows, width), f32), ((16, half), f32), ((rows, width), f32)]
            + portions(half // STACK, half) * 2,
            held=[
                shares, shares_other, residual, gain_mlp, cotangent, attended, w_out, q, k, v, probs,
                normed, w_query, w_key, w_value, cosine, sine, inputs, b_down.reshape(1, -1), grad_bd, grad_bu,
            ],
            scratch=[
                ((rows, width), bf16),
                ((rows, heads_cols), bf16),
                ((rows, heads_cols), bf16),
                ((rows, heads_cols), bf16),
                ((rows, heads_cols), bf16),
                ((rows, LANES), f32),
                ((rows, LANES), f32),
                ((PLANE, 2, half, half), f32),
                ((8, width), f32),
            ],
            flops=2 * rows * width * heads_cols * 10,
        )
        did(vec)
        state["normed_other"] = swap(state["normed_part"])
        chains["a"] = chain("attention", parts[:2], made["a"], vec=vec)
        chains["b"] = chain("attention_rest", parts[2:], made["b"])

    def input_back():
        (normed_other,) = turn(state["normed_other"])
        (state["grad_inputs"],) = call(
            input_kernel,
            [((rows, width), bf16)],
            held=[state["normed_part"], normed_other, inputs, gain_attn, state["delta_residual"]],
        )
        did(state["grad_inputs"])

    shapes = {
        "down": ((units, width), f32),
        "up": ((width, units), f32),
        "out": ((heads_cols, width), f32),
        "query": ((width, heads_cols), f32),
        "key": ((width, heads_cols), f32),
        "value": ((width, heads_cols), f32),
    }
    attention = ("out", "query", "key", "value")
    targets = {
        "d": (down_views, ("down",)),
        "u": (up_views, ("up",)),
        "c": (stack_views, ("down", "up")),
        "a": (partial(attention_views, 0), attention),
        "b": (partial(attention_views, 1), attention),
    }

    def put(key, sent):
        views, names = targets[key]
        olds = [name for name in names if name in grads]
        assert len(olds) in (0, len(names))
        (piece,) = turn(made[key][sent])
        results = pl.pallas_call(
            partial(put_in_place, views, key == "c", sent, len(olds)),
            name=f"put_{key}",
            out_shape=[jax.ShapeDtypeStruct(*shapes[name]) for name in names],
            in_specs=[VMEM] + [HBM] * len(olds),
            out_specs=[HBM] * len(names),
            scratch_shapes=[sems(32)],
            input_output_aliases={1 + i: i for i in range(len(olds))},
            compiler_params=pltpu.CompilerParams(vmem_limit_bytes=8 * 1024 * 1024),
            cost_estimate=pl.CostEstimate(flops=0, bytes_accessed=2 * piece.size * 4, transcendentals=0),
        )(piece, *[grads[name] for name in olds])
        grads.update(zip(names, results))
        did(results[0])

    did(grad_bd)
    pieces = {"K": backward, "I": input_back}
    waiting = []
    for key in ORDER:
        if key in waiting:
            waiting.remove(key)
            put(key, 0)
        if key in pieces:
            pieces[key]()
        else:
            next(chains[key])
        for other in list(waiting):
            if other != "c" or ("down" in grads and "up" in grads):
                waiting.remove(other)
                put(other, 0)
        if len(made.get(key, ())) == 1:
            waiting.append(key)
        elif len(made.get(key, ())) == 2:
            put(key, 1)

    vec = sums[0]
    n = width // half
    shared = (vec[: 3 * n] + swap(vec[: 3 * n])).reshape(3, width)
    grad_bu = vec[3 * n :].reshape(-1)[:units]
    grad_down, grad_up = grads["down"], grads["up"]
    grad_out, grad_query, grad_key, grad_value = (grads[name] for name in attention)
    output, grad_inputs = state["output"], state["grad_inputs"]
    return (
        output,
        grad_inputs,
        shared[0],
        grad_query,
        grad_key,
        grad_value,
        grad_out,
        shared[1],
        grad_up,
        grad_bu,
        grad_down,
        shared[2],
    )


def solution(mesh):
    count = mesh.shape["dp"]

    def step(*args):
        return on_device(count, *args)

    return jax.shard_map(
        step,
        mesh=mesh,
        in_specs=(
            P("dp", None),
            P(),
            P(None, "mp"),
            P(None, "mp"),
            P(None, "mp"),
            P("mp", None),
            P(),
            P(None, "mp"),
            P("mp"),
            P("mp", None),
            P(),
            P("dp", None),
            P(),
            P(),
        ),
        out_specs=(
            P("dp", None),
            P("dp", None),
            P(),
            P(None, "mp"),
            P(None, "mp"),
            P(None, "mp"),
            P("mp", None),
            P(),
            P(None, "mp"),
            P("mp"),
            P("mp", None),
            P(),
        ),
        check_vma=False,
    )
```

```python
from functools import partial
import math

import numpy as np

import jax
import jax.numpy as jnp
from jax import lax
from jax.experimental import pallas as pl
from jax.experimental.pallas import tpu as pltpu
from jax.sharding import PartitionSpec as P

HEAD = 64
BLOCK = 16
LEN = 256
HALF = 128
LANES = 128
PLANE = 4
STACK = 4
GROUP = PLANE * STACK

norm_eps = 1e-05
rope_base = 10000.0
masked_score = -1e30
score_scale = HEAD ** (-0.5)
bf16 = jnp.bfloat16
f32 = jnp.float32

X, Y, Z1, Z2 = 1, 2, 4, 8
FIRST, SECOND = (X, Y), (Y, X)
Z_FIRST, Z_SECOND = (Z1, Z2), (Z2, Z1)

ORDER = "cudKubcdIudabucdbuacdcaucbdauduabbcadbabac"

CASES = ((0, 0, 256, 0), (128, 256, 384, 128), (256, 640, 128, 128), (384, 768, 256, 128))
TILES = (
    (0, 0, 0, 0),
    (0, 1, 0, 0),
    (0, 1, 128, 0),
    (0, 1, 128, 128),
    (0, 0, 128, 128),
    (1, 1, 0, 0),
    (1, 1, 128, 0),
    (1, 1, 128, 128),
)
KEY_PLACE = (0, 3, 1, 2)


def mm(left, right):
    return jnp.dot(left, right, preferred_element_type=f32)


def tn(left, right):
    return lax.dot_general(left, right, (((0,), (0,)), ((), ())), preferred_element_type=f32)


def nt(left, right):
    return lax.dot_general(left, right, (((1,), (1,)), ((), ())), preferred_element_type=f32)


def rope_tables():
    half = HEAD // 2
    frequency = np.exp(np.arange(half) * (-2.0 * math.log(rope_base) / HEAD)).astype(np.float32)
    turn = (np.arange(LEN, dtype=np.float32)[:, None] * frequency[None, :]).astype(np.float32)
    cosine, sine = np.cos(turn.astype(np.float64)), np.sin(turn.astype(np.float64))
    cosine = np.tile(cosine, (1, LANES // half)).astype(np.float32)
    sine = np.tile(np.concatenate([-sine, sine], 1), (1, LANES // HEAD)).astype(np.float32)
    return cosine, sine


def swap_halves(values):
    lane = lax.broadcasted_iota(jnp.int32, values.shape, 1)
    return jnp.where(
        lane % HEAD < HEAD // 2, pltpu.roll(values, LANES - HEAD // 2, 1), pltpu.roll(values, HEAD // 2, 1)
    )


def head_mask(rows, which):
    lane = lax.broadcasted_iota(jnp.int32, (rows, LANES), 1)
    return (lane >= HEAD) if which else (lane < HEAD)


def layer_norm_rows(values, gain):
    centred = values - jnp.mean(values, axis=-1, keepdims=True)
    spread = jnp.mean(centred * centred, axis=-1, keepdims=True)
    return centred * lax.rsqrt(spread + norm_eps) * gain


def scaled_rows(values):
    centred = values - jnp.mean(values, axis=-1, keepdims=True)
    return centred * lax.rsqrt(jnp.mean(centred * centred, axis=-1, keepdims=True) + norm_eps)


def norm_back_rows(values, gain, delta):
    centred = values - jnp.mean(values, axis=-1, keepdims=True)
    spread = jnp.mean(centred * centred, axis=-1, keepdims=True)
    s = lax.rsqrt(spread + norm_eps)
    xhat = centred * s
    e = delta * gain
    back = s * (e - jnp.mean(e, axis=-1, keepdims=True) - xhat * jnp.mean(e * xhat, axis=-1, keepdims=True))
    return back, jnp.sum(delta * xhat, axis=0, keepdims=True)


def fill_bias(lengths_ref, pads_ref, bias_ref):
    sequence = lax.axis_index("dp")
    docs = lengths_ref.shape[1]
    ends, total = [], jnp.int32(0)
    for j in range(docs):
        total = total + lengths_ref[sequence, j]
        ends.append(total)
    first_pad = LEN - pads_ref[sequence]

    def segment(places):
        seg = jnp.zeros(places.shape, jnp.int32)
        for end in ends:
            seg = seg + (places >= end).astype(jnp.int32)
        return seg

    rows, cols, row_seg, col_seg = {}, {}, {}, {}
    for base in (0, HALF):
        rows[base] = lax.broadcasted_iota(jnp.int32, (HALF, LANES), 0) + base
        cols[base] = lax.broadcasted_iota(jnp.int32, (HALF, LANES), 1) + base
        row_seg[base] = segment(rows[base])
        col_seg[base] = segment(cols[base])
    for tile, (query_kind, key_kind, query_base, key_base) in enumerate(TILES):
        q, k = rows[query_base], cols[key_base]
        query_block, key_block = q // BLOCK, k // BLOCK
        same_doc = (row_seg[query_base] == col_seg[key_base]) & (k < first_pad)
        if query_kind == 0 and key_kind == 0:
            ok = (key_block == query_block) & (same_doc | (q == k))
        elif query_kind == 0:
            ok = (key_block < query_block) & same_doc
        else:
            ok = (key_block <= query_block) & (same_doc | (q == k))
        bias_ref[:, tile * LANES : (tile + 1) * LANES] = jnp.where(ok, 0.0, masked_score)


def fetch(pairs, sems):
    copies = [pltpu.make_async_copy(source, target, sems.at[i]) for i, (source, target) in enumerate(pairs)]
    for copy in copies:
        copy.start()
    return copies


class Sender:
    def __init__(self, sems):
        self.sems, self.copies = sems, []

    def send(self, source, target):
        self.copies.append(pltpu.make_async_copy(source, target, self.sems.at[len(self.copies)]))
        self.copies[-1].start()

    def finish(self):
        for copy in self.copies:
            copy.wait()


def attention_forward(
    lengths_in, pads_in, gain_in, x_in, wq_in, wk_in, wv_in, cos_in, sin_in, wo_in,
    normed_out, q_out, k_out, v_out, att_out, prob_out, part_out,
    bias_ref, lengths_ref, pads_ref, gain_ref, x_ref, wq_ref, wk_ref, wv_ref, cos_ref, sin_ref, wo_ref,
    normed_ref, q_ref, k_ref, v_ref, att_ref, prob_ref, part_ref, sems, out_sems,
):
    first = fetch(((lengths_in, lengths_ref), (pads_in, pads_ref), (x_in, x_ref), (gain_in, gain_ref)), sems.at[:4])
    copies = fetch(
        (
            (wq_in, wq_ref), (wk_in, wk_ref), (wv_in, wv_ref), (cos_in, cos_ref), (sin_in, sin_ref), (wo_in, wo_ref),
        ),
        sems.at[4:],
    )
    sender = Sender(out_sems)
    first[0].wait()
    first[1].wait()
    heads_cols = wq_ref.shape[1]
    pairs = heads_cols // LANES
    fill_bias(lengths_ref, pads_ref, bias_ref)
    first[2].wait()
    first[3].wait()
    gain = gain_ref[...].reshape(1, -1)

    @pl.loop(0, x_ref.shape[0] // 64)
    def _(i):
        rows = pl.ds(pl.multiple_of(i * 64, 64), 64)
        normed_ref[rows, :] = layer_norm_rows(x_ref[rows, :].astype(f32), gain).astype(bf16)

    sender.send(normed_ref, normed_out)
    for copy in copies[:5]:
        copy.wait()
    for block in range(4):
        rows = slice(block * HALF, block * HALF + HALF)
        places = slice((block % 2) * HALF, (block % 2) * HALF + HALF)
        key_rows = slice(KEY_PLACE[block] * HALF, KEY_PLACE[block] * HALF + HALF)
        normed = normed_ref[rows, :]
        cosine, sine = cos_ref[places, :], sin_ref[places, :]
        query, key = mm(normed, wq_ref[...]), mm(normed, wk_ref[...])
        for t in range(pairs):
            cols = slice(t * LANES, (t + 1) * LANES)
            turned = query[:, cols] * cosine + swap_halves(query[:, cols]) * sine
            q_ref[rows, cols] = (turned.astype(bf16).astype(f32) * score_scale).astype(bf16)
            turned = key[:, cols] * cosine + swap_halves(key[:, cols]) * sine
            k_ref[key_rows, cols] = turned.astype(bf16)
        v_ref[key_rows, :] = mm(normed, wv_ref[...]).astype(bf16)
    for source, target in ((q_ref, q_out), (k_ref, k_out), (v_ref, v_out)):
        sender.send(source, target)

    for t in range(pairs):
        cols = slice(t * LANES, (t + 1) * LANES)
        key_pair, value_pair = k_ref[:, cols], v_ref[:, cols]
        mixed = [None] * 4
        for which in range(2):
            mask = head_mask(key_pair.shape[0], which)
            key_head = jnp.where(mask, key_pair, jnp.zeros_like(key_pair))
            value_head = jnp.where(mask, value_pair, jnp.zeros_like(value_pair))
            for case, (query_row, first, width, key_row) in enumerate(CASES):
                scores = nt(q_ref[query_row : query_row + HALF, cols], key_head[key_row : key_row + width])
                scores = scores + bias_ref[:, first : first + width]
                weights = jnp.exp(scores - jnp.max(scores, axis=1, keepdims=True))
                low = (weights * (1.0 / jnp.sum(weights, axis=1, keepdims=True))).astype(bf16)
                prob_ref[2 * t + which, :, first : first + width] = low
                part = mm(low, value_head[key_row : key_row + width])
                mixed[case] = part if mixed[case] is None else mixed[case] + part
        for case, (query_row, _, _, _) in enumerate(CASES):
            att_ref[query_row : query_row + HALF, cols] = mixed[case].astype(bf16)
        sender.send(prob_ref.at[2 * t : 2 * t + 2], prob_out.at[2 * t : 2 * t + 2])

    sender.send(att_ref, att_out)
    copies[5].wait()
    for block in range(2):
        rows = slice(block * 256, block * 256 + 256)
        part_ref[rows, :] = mm(att_ref[rows, :], wo_ref[...])
        sender.send(part_ref.at[rows, :], part_out.at[rows, :])
    sender.finish()


def fourths(start, part):
    return pl.ds(pl.multiple_of(start * part, 8), part)


def slot_at(place):
    core = lax.axis_index("mp") % 2
    return (place // 2) * (1 + core) + (place % 2) * (2 - core)


def quarter_at(place):
    return lax.axis_index("dp") % PLANE ^ slot_at(place)


def fourth_at(place):
    return lax.axis_index("dp") % GROUP // PLANE ^ slot_at(place)


def z_place(block):
    slot = lax.axis_index("dp") % GROUP // PLANE ^ block
    return jnp.where(lax.axis_index("mp") % 2 == 0, (slot % 2) * 2 + slot // 2, slot)


def place_quarter(outs, place, value):
    part = value.shape[0] // STACK
    for block in range(STACK):
        outs[place // 2][place % 2, z_place(block)] = value[block * part : (block + 1) * part]


def place_quarter_z_first(outs, place, first_row, value):
    part = value.shape[0] // STACK
    for block in range(STACK):
        z = z_place(block)
        for sent in range(2):

            @pl.when(z // 2 == sent)
            def _(out=outs[sent], z=z, piece=value[block * part : (block + 1) * part]):
                out[z % 2, place, first_row : first_row + part, :] = piece


def mlp_kernel(
    gain_in, bu_in, x_in, mine_in, theirs_in, cot_in, wu_in, wd_in,
    residual_out, gbu_ref, gbd_ref, d_kept, d_sent, c_kept, c_sent, u_kept, u_sent, shares_out,
    gain_ref, bu_ref, x_ref, mine_ref, theirs_ref, cot_ref, wu_ref, wd_ref,
    residual_ref, normed_ref, act_ref, du_ref, d_kept_ref, d_sent_ref, c_kept_ref, c_sent_ref, u_kept_ref, u_sent_ref, shares_ref,
    sems, out_sems,
):
    row_count = x_ref.shape[0]
    units = wu_ref.shape[1]
    halves = (slice(0, row_count // 2), slice(row_count // 2, row_count))
    pairs = [(gain_in, gain_ref), (bu_in, bu_ref)]
    for rows in halves:
        pairs += [(a.at[rows, :], b.at[rows, :]) for a, b in ((x_in, x_ref), (mine_in, mine_ref), (theirs_in, theirs_ref))]
    copies = fetch(pairs + [(cot_in, cot_ref), (wu_in, wu_ref), (wd_in, wd_ref)], sems)
    sender = Sender(out_sems)
    gbu_ref[...] = jnp.zeros_like(gbu_ref)
    gbd_ref[...] = jnp.zeros_like(gbd_ref)
    copies[0].wait()
    gain = gain_ref[...].reshape(1, -1)
    for half in range(2):
        for copy in copies[2 + 3 * half : 5 + 3 * half]:
            copy.wait()

        @pl.loop(0, row_count // 128)
        def _(i, half=half):
            rows = pl.ds(pl.multiple_of(half * (row_count // 2) + i * 64, 64), 64)
            residual = x_ref[rows, :].astype(f32) + (mine_ref[rows, :] + theirs_ref[rows, :])
            residual_ref[rows, :] = residual
            normed_ref[rows, :] = layer_norm_rows(residual, gain).astype(bf16)

    sender.send(residual_ref, residual_out)
    for copy in (copies[1], *copies[8:]):
        copy.wait()
    c0 = math.sqrt(2.0 / math.pi)
    c1 = c0 * 0.044715

    @pl.loop(0, units // 256)
    def _(j):
        cols = pl.ds(pl.multiple_of(j * 256, 256), 256)
        for block in range(row_count // 256):
            rows = slice(block * 256, block * 256 + 256)
            u = mm(normed_ref[rows, :], wu_ref[:, cols]) + bu_ref[cols].reshape(1, -1)
            delta = nt(cot_ref[rows, :], wd_ref[cols, :])
            square = u * u
            t = jnp.tanh(u * (c0 + c1 * square))
            half_up = 0.5 * (1.0 + t)
            act_ref[rows, cols] = (u * half_up).astype(bf16)
            slope = half_up + (0.5 * u) * (1.0 - t * t) * (c0 + (3.0 * c1) * square)
            low = (delta * slope).astype(bf16)
            du_ref[rows, cols] = low
            gbu_ref[:, cols] += jnp.sum(low.astype(f32), axis=0, keepdims=True)

    quarter = units // PLANE
    fourth = units // GROUP
    cut = cot_ref.shape[1] * 2 // 3
    up_cut = quarter * 2 // 3
    quarters = {}
    for place in range(PLANE):
        quarters[place] = pl.ds(pl.multiple_of(quarter_at(place) * quarter, LANES), quarter)
    for place in (2, 3, 0, 1):
        grad = tn(act_ref[:, quarters[place]], cot_ref[...])
        place_quarter((d_kept_ref, d_sent_ref), place, grad[:, :cut])
        place_quarter_z_first((c_kept_ref, c_sent_ref), place, 0, grad[:, cut:])
        if place == 3:
            sender.send(d_sent_ref, d_sent)
    sender.send(d_kept_ref, d_kept)
    for place in (2, 3, 0, 1):
        grad = tn(normed_ref[...], du_ref[:, quarters[place]])
        place_quarter((u_kept_ref, u_sent_ref), place, grad[:, :up_cut])
        rest = grad[:, up_cut:].reshape(STACK, 2, fourth, -1)
        rest = jnp.concatenate([rest[:, 0], rest[:, 1]], 2).reshape(STACK * fourth, -1)
        place_quarter_z_first((c_kept_ref, c_sent_ref), place, fourth, rest)
        if place == 3:
            sender.send(u_sent_ref, u_sent)
    for source, target in ((c_sent_ref, c_sent), (u_kept_ref, u_kept), (c_kept_ref, c_kept)):
        sender.send(source, target)
    for share in range(2):
        for rows in halves:
            if share == 0:
                shares_ref[share, rows, :] = nt(du_ref[rows, :], wu_ref[...])
            else:
                shares_ref[share, rows, :] = mm(act_ref[rows, :], wd_ref[...])
        sender.send(shares_ref.at[share], shares_out.at[share])

    @pl.loop(0, row_count // 64)
    def _(i):
        rows = pl.ds(pl.multiple_of(i * 64, 64), 64)
        gbd_ref[...] += jnp.sum(cot_ref[rows, :].astype(f32), axis=0, keepdims=True)

    sender.finish()


def attention_backward(*refs):
    ins, refs = refs[:21], refs[21:]
    (output_out, delta_out, part_out, vec_ref), outs_at, refs = refs[:4], refs[4:8], refs[8:]
    held, refs = refs[:21], refs[21:]
    (output_ref, delta_ref, part_ref), outs, refs = refs[:3], refs[3:7], refs[7:]
    branch_ref, datt_ref, dq_ref, dk_ref, dv_ref, dk_acc, dv_acc, grads_ref, gnorm_ref, sems, out_sems = refs
    mine_ref, theirs_ref, residual_ref, cot_ref, gain_ref, bd_ref, att_ref, wo_ref, q_ref, k_ref, v_ref = held[:11]
    prob_ref, cos_ref, sin_ref, wq_ref, wk_ref, wv_ref, x_ref, normed_ref, gbd_ref, gbu_ref = held[11:]
    row_count = residual_ref.shape[0]
    heads_cols = wq_ref.shape[1]
    pairs = heads_cols // LANES
    halves = (slice(0, row_count // 2), slice(row_count // 2, row_count))
    first = []
    for rows in halves:
        first += [(a.at[:, rows, :], b.at[:, rows, :]) for a, b in zip(ins[:2], held[:2])]
        first += [(a.at[rows, :], b.at[rows, :]) for a, b in zip(ins[2:4], held[2:4])]
    copies = fetch(first + list(zip(ins[4:], held[4:])), sems)
    sender = Sender(out_sems)
    gnorm_ref[...] = jnp.zeros_like(gnorm_ref)
    copies[8].wait()
    copies[9].wait()
    gain, bias_down = gain_ref[...].reshape(1, -1), bd_ref[...].reshape(1, -1)
    for half in range(2):
        for copy in copies[4 * half : 4 * half + 4]:
            copy.wait()

        @pl.loop(0, row_count // 128)
        def _(i, half=half):
            rows = pl.ds(pl.multiple_of(half * (row_count // 2) + i * 64, 64), 64)
            delta = mine_ref[0, rows, :] + theirs_ref[0, rows, :]
            residual = residual_ref[rows, :]
            output_ref[rows, :] = (residual + (mine_ref[1, rows, :] + theirs_ref[1, rows, :]) + bias_down).astype(bf16)
            back, gain_part = norm_back_rows(residual, gain, delta)
            back = back + cot_ref[rows, :].astype(f32)
            delta_ref[rows, :] = back
            branch_ref[rows, :] = back.astype(bf16)
            gnorm_ref[0:1, :] += gain_part

    sender.send(output_ref, output_out)
    sender.send(delta_ref, delta_out)
    for copy in copies[10:]:
        copy.wait()
    for block in range(2):
        rows = slice(block * 256, block * 256 + 256)
        datt_ref[rows, :] = nt(branch_ref[rows, :], wo_ref[...]).astype(bf16)
    half = heads_cols
    grad = tn(att_ref[...], branch_ref[...])
    grads_ref[0, 0], grads_ref[0, 1] = grad[:, :half], grad[:, half:]

    for t in range(pairs):
        cols = slice(t * LANES, (t + 1) * LANES)
        key_pair, value_pair = k_ref[:, cols], v_ref[:, cols]
        dk_acc[...] = jnp.zeros_like(dk_acc)
        dv_acc[...] = jnp.zeros_like(dv_acc)
        query_grads = [None] * 4
        for which in range(2):
            mask = head_mask(key_pair.shape[0], which)
            key_head = jnp.where(mask, key_pair, jnp.zeros_like(key_pair))
            value_head = jnp.where(mask, value_pair, jnp.zeros_like(value_pair))
            small = head_mask(HALF, which)
            for case, (query_row, first, width, key_row) in enumerate(CASES):
                rows = slice(query_row, query_row + HALF)
                keys = slice(key_row, key_row + width)
                low = prob_ref[2 * t + which, :, first : first + width]
                wide = low.astype(f32)
                delta_head = datt_ref[rows, cols]
                g = nt(delta_head, value_head[keys])
                weighted = wide * g
                scores_back = (weighted - wide * jnp.sum(weighted, axis=1, keepdims=True)).astype(bf16)
                part = mm(scores_back, key_head[keys])
                query_grads[case] = part if query_grads[case] is None else query_grads[case] + part
                query = q_ref[rows, cols]
                query = jnp.where(small, query, jnp.zeros_like(query))
                delta_head = jnp.where(small, delta_head, jnp.zeros_like(delta_head))
                dk_acc[keys, :] += tn(scores_back, query)
                dv_acc[keys, :] += tn(low, delta_head)
        for block in range(4):
            rows = slice(block * HALF, block * HALF + HALF)
            places = slice((block % 2) * HALF, (block % 2) * HALF + HALF)
            key_rows = slice(KEY_PLACE[block] * HALF, KEY_PLACE[block] * HALF + HALF)
            cosine, sine = cos_ref[places, :], sin_ref[places, :]
            grad = query_grads[block] * score_scale
            dq_ref[rows, cols] = (grad * cosine - swap_halves(grad) * sine).astype(bf16)
            grad = dk_acc[key_rows, :]
            dk_ref[rows, cols] = (grad * cosine - swap_halves(grad) * sine).astype(bf16)
            dv_ref[rows, cols] = dv_acc[key_rows, :].astype(bf16)

    for block in range(2):
        rows = slice(block * 256, block * 256 + 256)
        part_ref[rows, :] = (
            nt(dq_ref[rows, :], wq_ref[...]) + nt(dk_ref[rows, :], wk_ref[...]) + nt(dv_ref[rows, :], wv_ref[...])
        )
    sender.send(part_ref, part_out)

    @pl.loop(0, row_count // 64)
    def _(i):
        rows = pl.ds(pl.multiple_of(i * 64, 64), 64)
        gnorm_ref[1:2, :] += jnp.sum(part_ref[rows, :] * scaled_rows(x_ref[rows, :].astype(f32)), axis=0, keepdims=True)

    vec_ref[...] = jnp.zeros_like(vec_ref)
    row = 0
    once = jnp.where(lax.axis_index("mp") == 0, 1.0, 0.0)
    for values in (gnorm_ref[1:2, :], gnorm_ref[0:1, :] * once, gbd_ref[...] * once, gbu_ref[...]):
        for first in range(0, values.shape[1], half):
            vec_ref[row : row + 1, :] = values[:, first : first + half]
            row += 1

    for matrix, grad_rows in ((1, dq_ref), (2, dk_ref), (3, dv_ref)):
        grad = tn(normed_ref[...], grad_rows[...])
        grads_ref[matrix, 0], grads_ref[matrix, 1] = grad[:half], grad[half:]
    for places in ((2, 3), (0, 1)):
        for place in places:
            quarter = quarter_at(place)
            place_quarter(outs[:2], place, grads_ref[quarter, 0])
            place_quarter(outs[2:], place, grads_ref[quarter, 1])
        for portion in range(2):
            which = 2 * portion + places[0] // 2
            sender.send(outs[which], outs_at[which])
    sender.finish()


def input_kernel(mine_ref, theirs_ref, x_ref, gain_ref, delta_ref, grad_ref):
    @pl.loop(0, x_ref.shape[0] // 64)
    def _(i):
        rows = pl.ds(pl.multiple_of(i * 64, 64), 64)
        delta = mine_ref[rows, :] + theirs_ref[rows, :]
        back, _ = norm_back_rows(x_ref[rows, :].astype(f32), gain_ref[...], delta)
        grad_ref[rows, :] = (delta_ref[rows, :] + back).astype(bf16)


def put_in_place(views, z_first, sent, olds, piece_ref, *refs):
    *refs, sems = refs
    outs = refs[olds:]
    for start in (True, False):
        count = 0
        for i in range(2):
            for j in range(STACK):
                z, place = (2 * sent + i, j) if z_first else (j, 2 * sent + i)
                for wanted, source, target in views(outs, quarter_at(place), fourth_at(z), piece_ref.at[i, j]):
                    copy = pltpu.make_async_copy(source, target, sems.at[count])
                    count += 1
                    act = copy.start if start else copy.wait
                    if wanted is None:
                        act()
                    else:
                        pl.when(wanted)(act)


def down_views(outs, quarter, fourth, block):
    part, cols = block.shape
    yield None, block, outs[0].at[fourths(quarter * STACK + fourth, part), pl.ds(0, cols)]


def up_views(outs, quarter, fourth, block):
    part, cols = block.shape
    whole = outs[0].shape[1] // PLANE
    yield None, block, outs[0].at[fourths(fourth, part), pl.ds(pl.multiple_of(quarter * whole, LANES), cols)]


def stack_views(outs, quarter, fourth, block):
    part, cols = block.shape[0] // 2, block.shape[1]
    whole, rest = outs[1].shape[1] // PLANE, cols // 2
    down_rows, down_cols = fourths(quarter * STACK + fourth, part), pl.ds(outs[0].shape[1] - cols, cols)
    yield None, block.at[pl.ds(0, part), :], outs[0].at[down_rows, down_cols]
    up_cols = pl.ds(pl.multiple_of((quarter + 1) * whole - rest, LANES), rest)
    for half in range(2):
        source = block.at[pl.ds(part, part), pl.ds(half * rest, rest)]
        yield None, source, outs[1].at[fourths(fourth * 2 + half, part), up_cols]


def attention_views(portion, outs, quarter, fourth, block):
    part, half = block.shape[0], block.shape[1]
    for matrix, out in enumerate(outs):
        if matrix:
            target = out.at[pl.ds(pl.multiple_of(portion * half + fourth * part, 8), part), :]
        else:
            target = out.at[fourths(fourth, part), pl.ds(portion * half, half)]
        yield quarter == matrix, block, target


VMEM = pl.BlockSpec(memory_space=pltpu.VMEM)
HBM = pl.BlockSpec(memory_space=pltpu.HBM)


def call(kernel, outs, held=(), loose=(), scratch=(), flops=0, limit=40, loose_outs=None):
    ins = [*held, *loose]
    shapes = [jax.ShapeDtypeStruct(shape, dtype) for shape, dtype in outs]
    moved = sum(math.prod(a.shape) * a.dtype.itemsize for a in ins + shapes)
    out_specs = [HBM if loose_outs and i in loose_outs else VMEM for i in range(len(outs))]
    return pl.pallas_call(
        kernel,
        name=kernel.__name__,
        out_shape=shapes,
        in_specs=[VMEM] * len(held) + [HBM] * len(loose),
        out_specs=out_specs,
        scratch_shapes=[s if not isinstance(s, tuple) else pltpu.VMEM(*s) for s in scratch],
        compiler_params=pltpu.CompilerParams(vmem_limit_bytes=limit * 1024 * 1024),
        cost_estimate=pl.CostEstimate(flops=flops, bytes_accessed=moved, transcendentals=0),
    )(*ins)


def on_device(
    count,
    inputs, norm_attn, w_query, w_key, w_value, w_out, norm_mlp, w_up, b_up, w_down, b_down, cotangent,
    doc_lengths, pad_counts,
):
    rows, width = inputs.shape
    heads_cols = w_query.shape[1]
    units = w_up.shape[1]
    heads = heads_cols // HEAD
    cosine, sine = (jnp.asarray(t) for t in rope_tables())
    gain_attn = norm_attn.reshape(1, -1)

    def swap(values):
        return lax.ppermute(values, "mp", [(0, 1), (1, 0)])

    def flip(values, bits, name):
        pairs = [(2 * i + core, 2 * (i ^ bits[core]) + core) for i in range(count) for core in range(2)]
        with jax.named_scope(name):
            return lax.ppermute(values, ("dp", "mp"), pairs)

    def sems(n):
        return pltpu.SemaphoreType.DMA((n,))

    half = heads_cols

    def portions(*shape):
        return [((2, STACK) + shape, f32)] * 2

    last = []

    def turn(*values):
        if not last:
            return values
        values, _ = lax.optimization_barrier((values, last.pop()))
        return values

    def did(value):
        last[:] = [value]
        return value

    def over_groups(values):
        if count == GROUP:
            return values
        groups = [[k * GROUP + j for k in range(count // GROUP)] for j in range(GROUP)]
        return lax.psum(values, "dp", axis_index_groups=groups)

    def chain(name, parts, result, z_first=False, vec=None):
        keep, send = parts
        plane, stack = [(FIRST, "first"), (SECOND, "second")], [(Z_FIRST, "z_first"), (Z_SECOND, "z_second")]
        steps = stack + plane if z_first else plane + stack

        def join(values):
            return values if vec is None else jnp.concatenate([values.reshape(-1, values.shape[-1]), vec], 0)

        def part_of(got, like, vec):
            if vec is None:
                return got, None
            return got[: -vec.shape[0]].reshape(like.shape), vec + got[-vec.shape[0] :]

        for step, (bits, label) in enumerate(steps):
            if step:
                keep, got, vec = turn(keep, got, vec)
                got, vec = part_of(got, keep, vec)
            if step == 0:
                send = join(send)
            elif step == 1:
                send, keep = did(join(keep[1] + got[1])), keep[0] + got[0]
            elif step == 2:
                send, keep = did(join(keep[2:] + got[2:])), keep[:2] + got[:2]
            else:
                keep = keep + got
                send = did(join(keep))
            got = flip(send, bits, f"{name}_sum_{label}")
            yield
        keep, got, vec = turn(keep, got, vec)
        got, vec = part_of(got, keep, vec)
        own = over_groups(did(keep + got[::-1]))
        if vec is not None:
            sums.append(over_groups(vec))
        for step, (bits, label) in enumerate(reversed(steps[:3])):
            got = flip(own, bits, f"{name}_gather_{label}")
            if step == 2:
                result.append(own)
            yield
            own, got = turn(own, got)
            if step < 2:
                own = did(jnp.stack([own, got]) if step == 1 else jnp.concatenate([own, got], 0))
        did(got)
        result.append(got)
        yield

    scores = (heads, HALF, 8 * LANES)
    rows_of = {"width": ((rows, width), bf16), "heads": ((rows, heads_cols), bf16), "sum": ((rows, width), f32)}
    outs = [rows_of["width"]] + [rows_of["heads"]] * 4 + [(scores, bf16), rows_of["sum"]]
    normed, q, k, v, attended, probs, branch = call(
        attention_forward,
        outs,
        loose=[doc_lengths, pad_counts, norm_attn, inputs, w_query, w_key, w_value, cosine, sine, w_out],
        scratch=[
            (scores[1:], f32),
            pltpu.SMEM(doc_lengths.shape, jnp.int32),
            pltpu.SMEM(pad_counts.shape, jnp.int32),
            (norm_attn.shape, f32),
            rows_of["width"],
            *[((width, heads_cols), bf16)] * 3,
            (cosine.shape, f32),
            (sine.shape, f32),
            ((heads_cols, width), bf16),
            *outs,
            sems(10),
            sems(10),
        ],
        flops=2 * rows * width * heads_cols * 4,
        limit=62,
        loose_outs=range(7),
    )
    branch_other = swap(branch)

    big = [
        *portions(units // GROUP, width * 2 // 3),
        *portions(units // GROUP + width // STACK // 2, width // 3),
        *portions(width // STACK, units // PLANE * 2 // 3),
        ((2, rows, width), f32),
    ]
    residual, grad_bu, grad_bd, *parts, shares = call(
        mlp_kernel,
        [rows_of["sum"], ((1, units), f32), ((1, width), f32), *big],
        loose=[norm_mlp, b_up, inputs, branch, branch_other, cotangent, w_up, w_down],
        scratch=[
            (norm_mlp.shape, f32),
            (b_up.shape, f32),
            rows_of["width"],
            rows_of["sum"],
            rows_of["sum"],
            rows_of["width"],
            ((width, units), bf16),
            ((units, width), bf16),
            rows_of["sum"],
            rows_of["width"],
            ((rows, units), bf16),
            ((rows, units), bf16),
            *big,
            sems(11),
            sems(9),
        ],
        flops=2 * rows * width * units * 6,
        limit=62,
        loose_outs=(0, *range(3, 10)),
    )
    made, grads, sums = {key: [] for key in "dcuab"}, {}, []
    chains = {
        "d": chain("down", parts[:2], made["d"]),
        "c": chain("down_stack", parts[2:4], made["c"], True),
        "u": chain("up", parts[4:], made["u"]),
    }
    state = {"shares_other": swap(shares)}

    def backward():
        (shares_other,) = turn(state["shares_other"])
        ins = [
            shares, shares_other, residual, cotangent, norm_mlp, b_down, attended, w_out, q, k, v,
            probs, cosine, sine, w_query, w_key, w_value, inputs, normed, grad_bd, grad_bu,
        ]
        outs = [rows_of["width"], rows_of["sum"], rows_of["sum"]]
        pieces = portions(half // STACK, half) * 2
        state["output"], state["delta_residual"], state["normed_part"], vec, *parts = call(
            attention_backward,
            [*outs, ((16, half), f32), *pieces],
            loose=ins,
            scratch=[
                *[(a.shape, a.dtype) for a in ins],
                *outs,
                *pieces,
                rows_of["width"],
                *[rows_of["heads"]] * 4,
                ((rows, LANES), f32),
                ((rows, LANES), f32),
                ((PLANE, 2, half, half), f32),
                ((8, width), f32),
                sems(25),
                sems(7),
            ],
            flops=2 * rows * width * heads_cols * 10,
            limit=62,
            loose_outs=(0, 1, 2, 4, 5, 6, 7),
        )
        did(vec)
        state["normed_other"] = swap(state["normed_part"])
        chains["a"] = chain("attention", parts[:2], made["a"], vec=vec)
        chains["b"] = chain("attention_rest", parts[2:], made["b"])

    def input_back():
        (normed_other,) = turn(state["normed_other"])
        (state["grad_inputs"],) = call(
            input_kernel,
            [((rows, width), bf16)],
            held=[state["normed_part"], normed_other, inputs, gain_attn, state["delta_residual"]],
        )
        did(state["grad_inputs"])

    shapes = {
        "down": ((units, width), f32),
        "up": ((width, units), f32),
        "out": ((heads_cols, width), f32),
        "query": ((width, heads_cols), f32),
        "key": ((width, heads_cols), f32),
        "value": ((width, heads_cols), f32),
    }
    attention = ("out", "query", "key", "value")
    targets = {
        "d": (down_views, ("down",)),
        "u": (up_views, ("up",)),
        "c": (stack_views, ("down", "up")),
        "a": (partial(attention_views, 0), attention),
        "b": (partial(attention_views, 1), attention),
    }

    def put(key, sent):
        views, names = targets[key]
        olds = [name for name in names if name in grads]
        assert len(olds) in (0, len(names))
        (piece,) = turn(made[key][sent])
        results = pl.pallas_call(
            partial(put_in_place, views, key == "c", sent, len(olds)),
            name=f"put_{key}",
            out_shape=[jax.ShapeDtypeStruct(*shapes[name]) for name in names],
            in_specs=[VMEM] + [HBM] * len(olds),
            out_specs=[HBM] * len(names),
            scratch_shapes=[sems(32)],
            input_output_aliases={1 + i: i for i in range(len(olds))},
            compiler_params=pltpu.CompilerParams(vmem_limit_bytes=8 * 1024 * 1024),
            cost_estimate=pl.CostEstimate(flops=0, bytes_accessed=2 * piece.size * 4, transcendentals=0),
        )(piece, *[grads[name] for name in olds])
        grads.update(zip(names, results))
        did(results[0])

    did(grad_bd)
    pieces = {"K": backward, "I": input_back}
    waiting = []
    for key in ORDER:
        if key in waiting:
            waiting.remove(key)
            put(key, 0)
        if key in pieces:
            pieces[key]()
        else:
            next(chains[key])
        for other in list(waiting):
            if other != "c" or ("down" in grads and "up" in grads):
                waiting.remove(other)
                put(other, 0)
        if len(made.get(key, ())) == 1:
            waiting.append(key)
        elif len(made.get(key, ())) == 2:
            put(key, 1)

    vec = sums[0]
    n = width // half
    shared = (vec[: 3 * n] + swap(vec[: 3 * n])).reshape(3, width)
    grad_bu = vec[3 * n :].reshape(-1)[:units]
    grad_down, grad_up = grads["down"], grads["up"]
    grad_out, grad_query, grad_key, grad_value = (grads[name] for name in attention)
    output, grad_inputs = state["output"], state["grad_inputs"]
    return (
        output,
        grad_inputs,
        shared[0],
        grad_query,
        grad_key,
        grad_value,
        grad_out,
        shared[1],
        grad_up,
        grad_bu,
        grad_down,
        shared[2],
    )


def solution(mesh):
    count = mesh.shape["dp"]

    def step(*args):
        return on_device(count, *args)

    return jax.shard_map(
        step,
        mesh=mesh,
        in_specs=(
            P("dp", None),
            P(),
            P(None, "mp"),
            P(None, "mp"),
            P(None, "mp"),
            P("mp", None),
            P(),
            P(None, "mp"),
            P("mp"),
            P("mp", None),
            P(),
            P("dp", None),
            P(),
            P(),
        ),
        out_specs=(
            P("dp", None),
            P("dp", None),
            P(),
            P(None, "mp"),
            P(None, "mp"),
            P(None, "mp"),
            P("mp", None),
            P(),
            P(None, "mp"),
            P("mp"),
            P("mp", None),
            P(),
        ),
        check_vma=False,
    )
```

```python
from functools import partial
import math

import numpy as np

import jax
import jax.numpy as jnp
from jax import lax
from jax.experimental import pallas as pl
from jax.experimental.pallas import tpu as pltpu
from jax.sharding import PartitionSpec as P

HEAD = 64
BLOCK = 16
LEN = 256
HALF = 128
LANES = 128
PLANE = 4
STACK = 4
GROUP = PLANE * STACK

norm_eps = 1e-05
rope_base = 10000.0
masked_score = -1e30
score_scale = HEAD ** (-0.5)
bf16 = jnp.bfloat16
f32 = jnp.float32

X, Y, Z1, Z2 = 1, 2, 4, 8
FIRST, SECOND = (X, Y), (Y, X)
Z_FIRST, Z_SECOND = (Z1, Z2), (Z2, Z1)

ORDER = "cudKucbdIudabucdbuacdcaucbdaudabubcadbabac"

CASES = ((0, 0, 256, 0), (128, 256, 384, 128), (256, 640, 128, 128), (384, 768, 256, 128))
TILES = (
    (0, 0, 0, 0),
    (0, 1, 0, 0),
    (0, 1, 128, 0),
    (0, 1, 128, 128),
    (0, 0, 128, 128),
    (1, 1, 0, 0),
    (1, 1, 128, 0),
    (1, 1, 128, 128),
)
KEY_PLACE = (0, 3, 1, 2)


def mm(left, right):
    return jnp.dot(left, right, preferred_element_type=f32)


def tn(left, right):
    return lax.dot_general(left, right, (((0,), (0,)), ((), ())), preferred_element_type=f32)


def nt(left, right):
    return lax.dot_general(left, right, (((1,), (1,)), ((), ())), preferred_element_type=f32)


def rope_tables():
    half = HEAD // 2
    frequency = np.exp(np.arange(half) * (-2.0 * math.log(rope_base) / HEAD)).astype(np.float32)
    turn = (np.arange(LEN, dtype=np.float32)[:, None] * frequency[None, :]).astype(np.float32)
    cosine, sine = np.cos(turn.astype(np.float64)), np.sin(turn.astype(np.float64))
    cosine = np.tile(cosine, (1, LANES // half)).astype(np.float32)
    sine = np.tile(np.concatenate([-sine, sine], 1), (1, LANES // HEAD)).astype(np.float32)
    return cosine, sine


def swap_halves(values):
    lane = lax.broadcasted_iota(jnp.int32, values.shape, 1)
    return jnp.where(
        lane % HEAD < HEAD // 2, pltpu.roll(values, LANES - HEAD // 2, 1), pltpu.roll(values, HEAD // 2, 1)
    )


def head_mask(rows, which):
    lane = lax.broadcasted_iota(jnp.int32, (rows, LANES), 1)
    return (lane >= HEAD) if which else (lane < HEAD)


def layer_norm_rows(values, gain):
    centred = values - jnp.mean(values, axis=-1, keepdims=True)
    spread = jnp.mean(centred * centred, axis=-1, keepdims=True)
    return centred * lax.rsqrt(spread + norm_eps) * gain


def scaled_rows(values):
    centred = values - jnp.mean(values, axis=-1, keepdims=True)
    return centred * lax.rsqrt(jnp.mean(centred * centred, axis=-1, keepdims=True) + norm_eps)


def norm_back_rows(values, gain, delta):
    centred = values - jnp.mean(values, axis=-1, keepdims=True)
    spread = jnp.mean(centred * centred, axis=-1, keepdims=True)
    s = lax.rsqrt(spread + norm_eps)
    xhat = centred * s
    e = delta * gain
    back = s * (e - jnp.mean(e, axis=-1, keepdims=True) - xhat * jnp.mean(e * xhat, axis=-1, keepdims=True))
    return back, jnp.sum(delta * xhat, axis=0, keepdims=True)


def fill_bias(lengths_ref, pads_ref, bias_ref):
    sequence = lax.axis_index("dp")
    docs = lengths_ref.shape[0]
    ends, total = [], jnp.int32(0)
    for j in range(docs):
        total = total + lengths_ref[j, sequence]
        ends.append(total)
    first_pad = LEN - pads_ref[sequence]

    def segment(places):
        seg = jnp.zeros(places.shape, jnp.int32)
        for end in ends:
            seg = seg + (places >= end).astype(jnp.int32)
        return seg

    rows, cols, row_seg, col_seg = {}, {}, {}, {}
    for base in (0, HALF):
        rows[base] = lax.broadcasted_iota(jnp.int32, (HALF, LANES), 0) + base
        cols[base] = lax.broadcasted_iota(jnp.int32, (HALF, LANES), 1) + base
        row_seg[base] = segment(rows[base])
        col_seg[base] = segment(cols[base])
    for tile, (query_kind, key_kind, query_base, key_base) in enumerate(TILES):
        q, k = rows[query_base], cols[key_base]
        query_block, key_block = q // BLOCK, k // BLOCK
        same_doc = (row_seg[query_base] == col_seg[key_base]) & (k < first_pad)
        if query_kind == 0 and key_kind == 0:
            ok = (key_block == query_block) & (same_doc | (q == k))
        elif query_kind == 0:
            ok = (key_block < query_block) & same_doc
        else:
            ok = (key_block <= query_block) & (same_doc | (q == k))
        bias_ref[:, tile * LANES : (tile + 1) * LANES] = jnp.where(ok, 0.0, masked_score)


def fetch(pairs, sems):
    copies = [pltpu.make_async_copy(source, target, sems.at[i]) for i, (source, target) in enumerate(pairs)]
    for copy in copies:
        copy.start()
    return copies


class Sender:
    def __init__(self, sems):
        self.sems, self.copies = sems, []

    def send(self, source, target):
        self.copies.append(pltpu.make_async_copy(source, target, self.sems.at[len(self.copies)]))
        self.copies[-1].start()

    def finish(self):
        for copy in self.copies:
            copy.wait()


def attention_forward(
    lengths_in, pads_in, gain_in, x_in, wq_in, wk_in, wv_in, cos_in, sin_in, wo_in,
    normed_out, q_out, k_out, v_out, att_out, prob_out, part_out,
    bias_ref, lengths_ref, pads_ref, gain_ref, x_ref, wq_ref, wk_ref, wv_ref, cos_ref, sin_ref, wo_ref,
    normed_ref, q_ref, k_ref, v_ref, att_ref, prob_ref, part_ref, sems, out_sems,
):
    first = fetch(((lengths_in, lengths_ref), (pads_in, pads_ref), (x_in, x_ref), (gain_in, gain_ref)), sems.at[:4])
    copies = fetch(
        (
            (wq_in, wq_ref), (wk_in, wk_ref), (wv_in, wv_ref), (cos_in, cos_ref), (sin_in, sin_ref), (wo_in, wo_ref),
        ),
        sems.at[4:],
    )
    sender = Sender(out_sems)
    first[0].wait()
    first[1].wait()
    heads_cols = wq_ref.shape[1]
    pairs = heads_cols // LANES
    fill_bias(lengths_ref, pads_ref, bias_ref)
    first[2].wait()
    first[3].wait()
    gain = gain_ref[...].reshape(1, -1)

    @pl.loop(0, x_ref.shape[0] // 64)
    def _(i):
        rows = pl.ds(pl.multiple_of(i * 64, 64), 64)
        normed_ref[rows, :] = layer_norm_rows(x_ref[rows, :].astype(f32), gain).astype(bf16)

    sender.send(normed_ref, normed_out)
    for copy in copies[:5]:
        copy.wait()
    for block in range(4):
        rows = slice(block * HALF, block * HALF + HALF)
        places = slice((block % 2) * HALF, (block % 2) * HALF + HALF)
        key_rows = slice(KEY_PLACE[block] * HALF, KEY_PLACE[block] * HALF + HALF)
        normed = normed_ref[rows, :]
        cosine, sine = cos_ref[places, :], sin_ref[places, :]
        query, key = mm(normed, wq_ref[...]), mm(normed, wk_ref[...])
        for t in range(pairs):
            cols = slice(t * LANES, (t + 1) * LANES)
            turned = query[:, cols] * cosine + swap_halves(query[:, cols]) * sine
            q_ref[rows, cols] = (turned.astype(bf16).astype(f32) * score_scale).astype(bf16)
            turned = key[:, cols] * cosine + swap_halves(key[:, cols]) * sine
            k_ref[key_rows, cols] = turned.astype(bf16)
        v_ref[key_rows, :] = mm(normed, wv_ref[...]).astype(bf16)
    for source, target in ((q_ref, q_out), (k_ref, k_out), (v_ref, v_out)):
        sender.send(source, target)

    for t in range(pairs):
        cols = slice(t * LANES, (t + 1) * LANES)
        key_pair, value_pair = k_ref[:, cols], v_ref[:, cols]
        mixed = [None] * 4
        jobs, scores, values = [(which, case) for which in range(2) for case in range(4)], [], []
        for which in range(2):
            mask = head_mask(key_pair.shape[0], which)
            key_head = jnp.where(mask, key_pair, jnp.zeros_like(key_pair))
            values.append(jnp.where(mask, value_pair, jnp.zeros_like(value_pair)))
            for query_row, first, width, key_row in CASES:
                found = nt(q_ref[query_row : query_row + HALF, cols], key_head[key_row : key_row + width])
                scores.append(found + bias_ref[:, first : first + width])
        tops = [jnp.max(a, axis=1, keepdims=True) for a in scores]
        weights = [jnp.exp(a - top) for a, top in zip(scores, tops)]
        shares = [1.0 / jnp.sum(a, axis=1, keepdims=True) for a in weights]
        lows = [(a * share).astype(bf16) for a, share in zip(weights, shares)]
        for (which, case), low in zip(jobs, lows):
            _, first, width, key_row = CASES[case]
            prob_ref[2 * t + which, :, first : first + width] = low
            part = mm(low, values[which][key_row : key_row + width])
            mixed[case] = part if mixed[case] is None else mixed[case] + part
        for case, (query_row, _, _, _) in enumerate(CASES):
            att_ref[query_row : query_row + HALF, cols] = mixed[case].astype(bf16)
        sender.send(prob_ref.at[2 * t : 2 * t + 2], prob_out.at[2 * t : 2 * t + 2])

    sender.send(att_ref, att_out)
    copies[5].wait()
    for block in range(2):
        rows = slice(block * 256, block * 256 + 256)
        part_ref[rows, :] = mm(att_ref[rows, :], wo_ref[...])
        sender.send(part_ref.at[rows, :], part_out.at[rows, :])
    sender.finish()


def fourths(start, part):
    return pl.ds(pl.multiple_of(start * part, 8), part)


def slot_at(place):
    core = lax.axis_index("mp") % 2
    return (place // 2) * (1 + core) + (place % 2) * (2 - core)


def quarter_at(place):
    return lax.axis_index("dp") % PLANE ^ slot_at(place)


def fourth_at(place):
    return lax.axis_index("dp") % GROUP // PLANE ^ slot_at(place)


def z_place(block):
    slot = lax.axis_index("dp") % GROUP // PLANE ^ block
    return jnp.where(lax.axis_index("mp") % 2 == 0, (slot % 2) * 2 + slot // 2, slot)


def place_quarter(outs, place, value):
    part = value.shape[0] // STACK
    for block in range(STACK):
        outs[place // 2][place % 2, z_place(block)] = value[block * part : (block + 1) * part]


def place_quarter_z_first(outs, place, first_row, value):
    part = value.shape[0] // STACK
    for block in range(STACK):
        z = z_place(block)
        for sent in range(2):

            @pl.when(z // 2 == sent)
            def _(out=outs[sent], z=z, piece=value[block * part : (block + 1) * part]):
                out[z % 2, place, first_row : first_row + part, :] = piece


def mlp_kernel(
    gain_in, bu_in, x_in, mine_in, theirs_in, cot_in, wu_in, wd_in,
    residual_out, gbu_ref, d_kept, d_sent, c_kept, c_sent, u_kept, u_sent, shares_out,
    gain_ref, bu_ref, x_ref, mine_ref, theirs_ref, cot_ref, wu_ref, wd_ref,
    residual_ref, normed_ref, act_ref, du_ref, d_kept_ref, d_sent_ref, c_kept_ref, c_sent_ref, u_kept_ref, u_sent_ref, shares_ref,
    sems, out_sems,
):
    row_count = x_ref.shape[0]
    units = wu_ref.shape[1]
    halves = (slice(0, row_count // 2), slice(row_count // 2, row_count))
    pairs = [(gain_in, gain_ref), (bu_in, bu_ref)]
    for rows in halves:
        pairs += [(a.at[rows, :], b.at[rows, :]) for a, b in ((x_in, x_ref), (mine_in, mine_ref), (theirs_in, theirs_ref))]
    copies = fetch(pairs + [(cot_in, cot_ref), (wu_in, wu_ref), (wd_in, wd_ref)], sems)
    sender = Sender(out_sems)
    gbu_ref[...] = jnp.zeros_like(gbu_ref)
    copies[0].wait()
    gain = gain_ref[...].reshape(1, -1)
    for half in range(2):
        for copy in copies[2 + 3 * half : 5 + 3 * half]:
            copy.wait()

        @pl.loop(0, row_count // 128)
        def _(i, half=half):
            rows = pl.ds(pl.multiple_of(half * (row_count // 2) + i * 64, 64), 64)
            residual = x_ref[rows, :].astype(f32) + (mine_ref[rows, :] + theirs_ref[rows, :])
            residual_ref[rows, :] = residual
            normed_ref[rows, :] = layer_norm_rows(residual, gain).astype(bf16)

    sender.send(residual_ref, residual_out)
    for copy in (copies[1], *copies[8:]):
        copy.wait()
    c0 = math.sqrt(2.0 / math.pi)
    c1 = c0 * 0.044715

    @pl.loop(0, units // 512)
    def _(j):
        cols = pl.ds(pl.multiple_of(j * 512, 512), 512)
        blocks = [slice(block * 256, block * 256 + 256) for block in range(row_count // 256)]
        ups = [mm(normed_ref[rows, :], wu_ref[:, cols]) + bu_ref[cols].reshape(1, -1) for rows in blocks]
        deltas = [nt(cot_ref[rows, :], wd_ref[cols, :]) for rows in blocks]
        for rows, u, delta in zip(blocks, ups, deltas):
            square = u * u
            t = jnp.tanh(u * (c0 + c1 * square))
            half_up = 0.5 + 0.5 * t
            act = u * half_up
            act_ref[rows, cols] = act.astype(bf16)
            slope = half_up + act * ((1.0 - t) * (c0 + (3.0 * c1) * square))
            low = (delta * slope).astype(bf16)
            du_ref[rows, cols] = low
            gbu_ref[:, cols] += jnp.sum(low.astype(f32), axis=0, keepdims=True)

    quarter = units // PLANE
    fourth = units // GROUP
    cut = cot_ref.shape[1] * 2 // 3
    up_cut = quarter * 2 // 3
    quarters = {}
    for place in range(PLANE):
        quarters[place] = pl.ds(pl.multiple_of(quarter_at(place) * quarter, LANES), quarter)
    for share in range(2):
        for rows in halves:
            if share == 0:
                shares_ref[share, rows, :] = nt(du_ref[rows, :], wu_ref[...])
            else:
                shares_ref[share, rows, :] = mm(act_ref[rows, :], wd_ref[...])
        sender.send(shares_ref.at[share], shares_out.at[share])
    c_pairs = ((c_kept_ref, c_kept), (c_sent_ref, c_sent))
    for place in (2, 3, 0, 1):
        grad = tn(act_ref[:, quarters[place]], cot_ref[...])
        place_quarter((d_kept_ref, d_sent_ref), place, grad[:, :cut])
        place_quarter_z_first((c_kept_ref, c_sent_ref), place, 0, grad[:, cut:])
        source, target = ((d_kept_ref, d_kept), (d_sent_ref, d_sent))[place // 2]
        sender.send(source.at[place % 2], target.at[place % 2])
        for source, target in c_pairs:
            rows = pl.ds(0, fourth)
            sender.send(source.at[:, place, rows, :], target.at[:, place, rows, :])
    for place in (2, 3, 0, 1):
        grad = tn(normed_ref[...], du_ref[:, quarters[place]])
        place_quarter((u_kept_ref, u_sent_ref), place, grad[:, :up_cut])
        rest = grad[:, up_cut:].reshape(STACK, 2, fourth, -1)
        rest = jnp.concatenate([rest[:, 0], rest[:, 1]], 2).reshape(STACK * fourth, -1)
        place_quarter_z_first((c_kept_ref, c_sent_ref), place, fourth, rest)
        source, target = ((u_kept_ref, u_kept), (u_sent_ref, u_sent))[place // 2]
        sender.send(source.at[place % 2], target.at[place % 2])
        for source, target in c_pairs:
            rows = pl.ds(fourth, fourth)
            sender.send(source.at[:, place, rows, :], target.at[:, place, rows, :])
    sender.finish()


def attention_backward(*refs):
    ins, refs = refs[:20], refs[20:]
    (output_out, delta_out, part_out, vec_ref), outs_at, refs = refs[:4], refs[4:8], refs[8:]
    held, refs = refs[:20], refs[20:]
    (output_ref, delta_ref, part_ref), outs, refs = refs[:3], refs[3:7], refs[7:]
    branch_ref, datt_ref, dq_ref, dk_ref, dv_ref, dk_acc, dv_acc, grads_ref, gnorm_ref, sems, out_sems = refs
    mine_ref, theirs_ref, residual_ref, cot_ref, gain_ref, bd_ref, att_ref, wo_ref, q_ref, k_ref, v_ref = held[:11]
    prob_ref, cos_ref, sin_ref, wq_ref, wk_ref, wv_ref, x_ref, normed_ref, gbu_ref = held[11:]
    row_count = residual_ref.shape[0]
    heads_cols = wq_ref.shape[1]
    pairs = heads_cols // LANES
    halves = (slice(0, row_count // 2), slice(row_count // 2, row_count))
    first = []
    for rows in halves:
        first += [(a.at[:, rows, :], b.at[:, rows, :]) for a, b in zip(ins[:2], held[:2])]
        first += [(a.at[rows, :], b.at[rows, :]) for a, b in zip(ins[2:4], held[2:4])]
    copies = fetch(first + list(zip(ins[4:], held[4:])), sems)
    sender = Sender(out_sems)
    gnorm_ref[...] = jnp.zeros_like(gnorm_ref)
    copies[8].wait()
    copies[9].wait()
    gain, bias_down = gain_ref[...].reshape(1, -1), bd_ref[...].reshape(1, -1)
    for half in range(2):
        for copy in copies[4 * half : 4 * half + 4]:
            copy.wait()

        @pl.loop(0, row_count // 128)
        def _(i, half=half):
            rows = pl.ds(pl.multiple_of(half * (row_count // 2) + i * 64, 64), 64)
            delta = mine_ref[0, rows, :] + theirs_ref[0, rows, :]
            residual = residual_ref[rows, :]
            output_ref[rows, :] = (residual + (mine_ref[1, rows, :] + theirs_ref[1, rows, :]) + bias_down).astype(bf16)
            back, gain_part = norm_back_rows(residual, gain, delta)
            cotangent = cot_ref[rows, :].astype(f32)
            back = back + cotangent
            delta_ref[rows, :] = back
            branch_ref[rows, :] = back.astype(bf16)
            gnorm_ref[0:1, :] += gain_part
            gnorm_ref[2:3, :] += jnp.sum(cotangent, axis=0, keepdims=True)

    sender.send(output_ref, output_out)
    sender.send(delta_ref, delta_out)
    for copy in copies[10:]:
        copy.wait()
    for block in range(2):
        rows = slice(block * 256, block * 256 + 256)
        datt_ref[rows, :] = nt(branch_ref[rows, :], wo_ref[...]).astype(bf16)
    half = heads_cols
    grad = tn(att_ref[...], branch_ref[...])
    grads_ref[0, 0], grads_ref[0, 1] = grad[:, :half], grad[:, half:]

    for t in range(pairs):
        cols = slice(t * LANES, (t + 1) * LANES)
        key_pair, value_pair = k_ref[:, cols], v_ref[:, cols]
        dk_acc[...] = jnp.zeros_like(dk_acc)
        dv_acc[...] = jnp.zeros_like(dv_acc)
        query_grads = [None] * 4
        jobs, deltas, lows, keys_of = [], [], [], []
        for which in range(2):
            mask = head_mask(key_pair.shape[0], which)
            keys_of.append(jnp.where(mask, key_pair, jnp.zeros_like(key_pair)))
            value_head = jnp.where(mask, value_pair, jnp.zeros_like(value_pair))
            for case, (query_row, first, width, key_row) in enumerate(CASES):
                jobs.append((which, case))
                lows.append(prob_ref[2 * t + which, :, first : first + width])
                rows = slice(query_row, query_row + HALF)
                deltas.append(nt(datt_ref[rows, cols], value_head[key_row : key_row + width]))
        wides = [low.astype(f32) for low in lows]
        weighted = [wide * g for wide, g in zip(wides, deltas)]
        totals = [jnp.sum(a, axis=1, keepdims=True) for a in weighted]
        backs = [(a - wide * total).astype(bf16) for a, wide, total in zip(weighted, wides, totals)]
        for (which, case), low, back in zip(jobs, lows, backs):
            query_row, _, width, key_row = CASES[case]
            rows, keys = slice(query_row, query_row + HALF), slice(key_row, key_row + width)
            small = head_mask(HALF, which)
            part = mm(back, keys_of[which][keys])
            query_grads[case] = part if query_grads[case] is None else query_grads[case] + part
            query, delta_head = q_ref[rows, cols], datt_ref[rows, cols]
            dk_acc[keys, :] += tn(back, jnp.where(small, query, jnp.zeros_like(query)))
            dv_acc[keys, :] += tn(low, jnp.where(small, delta_head, jnp.zeros_like(delta_head)))
        for block in range(4):
            rows = slice(block * HALF, block * HALF + HALF)
            places = slice((block % 2) * HALF, (block % 2) * HALF + HALF)
            key_rows = slice(KEY_PLACE[block] * HALF, KEY_PLACE[block] * HALF + HALF)
            cosine, sine = cos_ref[places, :], sin_ref[places, :]
            grad = query_grads[block] * score_scale
            dq_ref[rows, cols] = (grad * cosine - swap_halves(grad) * sine).astype(bf16)
            grad = dk_acc[key_rows, :]
            dk_ref[rows, cols] = (grad * cosine - swap_halves(grad) * sine).astype(bf16)
            dv_ref[rows, cols] = dv_acc[key_rows, :].astype(bf16)

    for block in range(2):
        rows = slice(block * 256, block * 256 + 256)
        part_ref[rows, :] = (
            nt(dq_ref[rows, :], wq_ref[...]) + nt(dk_ref[rows, :], wk_ref[...]) + nt(dv_ref[rows, :], wv_ref[...])
        )
    sender.send(part_ref, part_out)

    @pl.loop(0, row_count // 64)
    def _(i):
        rows = pl.ds(pl.multiple_of(i * 64, 64), 64)
        gnorm_ref[1:2, :] += jnp.sum(part_ref[rows, :] * scaled_rows(x_ref[rows, :].astype(f32)), axis=0, keepdims=True)

    vec_ref[...] = jnp.zeros_like(vec_ref)
    row = 0
    once = jnp.where(lax.axis_index("mp") == 0, 1.0, 0.0)
    for values in (gnorm_ref[1:2, :], gnorm_ref[0:1, :] * once, gnorm_ref[2:3, :] * once, gbu_ref[...]):
        for first in range(0, values.shape[1], half):
            vec_ref[row : row + 1, :] = values[:, first : first + half]
            row += 1

    for matrix, grad_rows in ((1, dq_ref), (2, dk_ref), (3, dv_ref)):
        grad = tn(normed_ref[...], grad_rows[...])
        grads_ref[matrix, 0], grads_ref[matrix, 1] = grad[:half], grad[half:]
    for places in ((2, 3), (0, 1)):
        for place in places:
            quarter = quarter_at(place)
            place_quarter(outs[:2], place, grads_ref[quarter, 0])
            place_quarter(outs[2:], place, grads_ref[quarter, 1])
        for portion in range(2):
            which = 2 * portion + places[0] // 2
            sender.send(outs[which], outs_at[which])
    sender.finish()


def input_kernel(mine_ref, theirs_ref, x_ref, gain_ref, delta_ref, grad_ref):
    @pl.loop(0, x_ref.shape[0] // 64)
    def _(i):
        rows = pl.ds(pl.multiple_of(i * 64, 64), 64)
        delta = mine_ref[rows, :] + theirs_ref[rows, :]
        back, _ = norm_back_rows(x_ref[rows, :].astype(f32), gain_ref[...], delta)
        grad_ref[rows, :] = (delta_ref[rows, :] + back).astype(bf16)


def put_in_place(views, z_first, sent, olds, piece_ref, *refs):
    *refs, sems = refs
    outs = refs[olds:]
    for start in (True, False):
        count = 0
        for i in range(2):
            for j in range(STACK):
                z, place = (2 * sent + i, j) if z_first else (j, 2 * sent + i)
                for wanted, source, target in views(outs, quarter_at(place), fourth_at(z), piece_ref.at[i, j]):
                    copy = pltpu.make_async_copy(source, target, sems.at[count])
                    count += 1
                    act = copy.start if start else copy.wait
                    if wanted is None:
                        act()
                    else:
                        pl.when(wanted)(act)


def down_views(outs, quarter, fourth, block):
    part, cols = block.shape
    yield None, block, outs[0].at[fourths(quarter * STACK + fourth, part), pl.ds(0, cols)]


def up_views(outs, quarter, fourth, block):
    part, cols = block.shape
    whole = outs[0].shape[1] // PLANE
    yield None, block, outs[0].at[fourths(fourth, part), pl.ds(pl.multiple_of(quarter * whole, LANES), cols)]


def stack_views(outs, quarter, fourth, block):
    part, cols = block.shape[0] // 2, block.shape[1]
    whole, rest = outs[1].shape[1] // PLANE, cols // 2
    down_rows, down_cols = fourths(quarter * STACK + fourth, part), pl.ds(outs[0].shape[1] - cols, cols)
    yield None, block.at[pl.ds(0, part), :], outs[0].at[down_rows, down_cols]
    up_cols = pl.ds(pl.multiple_of((quarter + 1) * whole - rest, LANES), rest)
    for half in range(2):
        source = block.at[pl.ds(part, part), pl.ds(half * rest, rest)]
        yield None, source, outs[1].at[fourths(fourth * 2 + half, part), up_cols]


def attention_views(portion, outs, quarter, fourth, block):
    part, half = block.shape[0], block.shape[1]
    for matrix, out in enumerate(outs):
        if matrix:
            target = out.at[pl.ds(pl.multiple_of(portion * half + fourth * part, 8), part), :]
        else:
            target = out.at[fourths(fourth, part), pl.ds(portion * half, half)]
        yield quarter == matrix, block, target


VMEM = pl.BlockSpec(memory_space=pltpu.VMEM)
HBM = pl.BlockSpec(memory_space=pltpu.HBM)


def call(kernel, outs, held=(), loose=(), scratch=(), flops=0, limit=40, loose_outs=None):
    ins = [*held, *loose]
    shapes = [jax.ShapeDtypeStruct(shape, dtype) for shape, dtype in outs]
    moved = sum(math.prod(a.shape) * a.dtype.itemsize for a in ins + shapes)
    out_specs = [HBM if loose_outs and i in loose_outs else VMEM for i in range(len(outs))]
    return pl.pallas_call(
        kernel,
        name=kernel.__name__,
        out_shape=shapes,
        in_specs=[VMEM] * len(held) + [HBM] * len(loose),
        out_specs=out_specs,
        scratch_shapes=[s if not isinstance(s, tuple) else pltpu.VMEM(*s) for s in scratch],
        compiler_params=pltpu.CompilerParams(vmem_limit_bytes=limit * 1024 * 1024),
        cost_estimate=pl.CostEstimate(flops=flops, bytes_accessed=moved, transcendentals=0),
    )(*ins)


def on_device(
    count,
    inputs, norm_attn, w_query, w_key, w_value, w_out, norm_mlp, w_up, b_up, w_down, b_down, cotangent,
    doc_lengths, pad_counts,
):
    rows, width = inputs.shape
    heads_cols = w_query.shape[1]
    units = w_up.shape[1]
    heads = heads_cols // HEAD
    cosine, sine = (jnp.asarray(t) for t in rope_tables())
    gain_attn = norm_attn.reshape(1, -1)

    def swap(values):
        return lax.ppermute(values, "mp", [(0, 1), (1, 0)])

    def flip(values, bits, name):
        pairs = [(2 * i + core, 2 * (i ^ bits[core]) + core) for i in range(count) for core in range(2)]
        with jax.named_scope(name):
            return lax.ppermute(values, ("dp", "mp"), pairs)

    def sems(n):
        return pltpu.SemaphoreType.DMA((n,))

    half = heads_cols

    def portions(*shape):
        return [((2, STACK) + shape, f32)] * 2

    last = []

    def turn(*values):
        if not last:
            return values
        values, _ = lax.optimization_barrier((values, last.pop()))
        return values

    def did(value):
        last[:] = [value]
        return value

    def over_groups(values):
        if count == GROUP:
            return values
        groups = [[k * GROUP + j for k in range(count // GROUP)] for j in range(GROUP)]
        return lax.psum(values, "dp", axis_index_groups=groups)

    def chain(name, parts, result, z_first=False, vec=None):
        keep, send = parts
        plane, stack = [(FIRST, "first"), (SECOND, "second")], [(Z_FIRST, "z_first"), (Z_SECOND, "z_second")]
        steps = stack + plane if z_first else plane + stack

        def join(values):
            return values if vec is None else jnp.concatenate([values.reshape(-1, values.shape[-1]), vec], 0)

        def part_of(got, like, vec):
            if vec is None:
                return got, None
            return got[: -vec.shape[0]].reshape(like.shape), vec + got[-vec.shape[0] :]

        for step, (bits, label) in enumerate(steps):
            if step:
                keep, got, vec = turn(keep, got, vec)
                got, vec = part_of(got, keep, vec)
            if step == 0:
                send = join(send)
            elif step == 1:
                send, keep = did(join(keep[1] + got[1])), keep[0] + got[0]
            elif step == 2:
                send, keep = did(join(keep[2:] + got[2:])), keep[:2] + got[:2]
            else:
                keep = keep + got
                send = did(join(keep))
            got = flip(send, bits, f"{name}_sum_{label}")
            yield
        keep, got, vec = turn(keep, got, vec)
        got, vec = part_of(got, keep, vec)
        own = over_groups(did(keep + got[::-1]))
        if vec is not None:
            sums.append(over_groups(vec))
        for step, (bits, label) in enumerate(reversed(steps[:3])):
            got = flip(own, bits, f"{name}_gather_{label}")
            if step == 2:
                result.append(own)
            yield
            own, got = turn(own, got)
            if step < 2:
                own = did(jnp.stack([own, got]) if step == 1 else jnp.concatenate([own, got], 0))
        did(got)
        result.append(got)
        yield

    scores = (heads, HALF, 8 * LANES)
    rows_of = {"width": ((rows, width), bf16), "heads": ((rows, heads_cols), bf16), "sum": ((rows, width), f32)}
    outs = [rows_of["width"]] + [rows_of["heads"]] * 4 + [(scores, bf16), rows_of["sum"]]
    normed, q, k, v, attended, probs, branch = call(
        attention_forward,
        outs,
        loose=[doc_lengths.T, pad_counts, norm_attn, inputs, w_query, w_key, w_value, cosine, sine, w_out],
        scratch=[
            (scores[1:], f32),
            pltpu.SMEM(doc_lengths.shape[::-1], jnp.int32),
            pltpu.SMEM(pad_counts.shape, jnp.int32),
            (norm_attn.shape, f32),
            rows_of["width"],
            *[((width, heads_cols), bf16)] * 3,
            (cosine.shape, f32),
            (sine.shape, f32),
            ((heads_cols, width), bf16),
            *outs,
            sems(10),
            sems(10),
        ],
        flops=2 * rows * width * heads_cols * 4,
        limit=62,
        loose_outs=range(7),
    )
    branch_other = swap(branch)

    big = [
        *portions(units // GROUP, width * 2 // 3),
        *portions(units // GROUP + width // STACK // 2, width // 3),
        *portions(width // STACK, units // PLANE * 2 // 3),
        ((2, rows, width), f32),
    ]
    residual, grad_bu, *parts, shares = call(
        mlp_kernel,
        [rows_of["sum"], ((1, units), f32), *big],
        loose=[norm_mlp, b_up, inputs, branch, branch_other, cotangent, w_up, w_down],
        scratch=[
            (norm_mlp.shape, f32),
            (b_up.shape, f32),
            rows_of["width"],
            rows_of["sum"],
            rows_of["sum"],
            rows_of["width"],
            ((width, units), bf16),
            ((units, width), bf16),
            rows_of["sum"],
            rows_of["width"],
            ((rows, units), bf16),
            ((rows, units), bf16),
            *big,
            sems(11),
            sems(27),
        ],
        flops=2 * rows * width * units * 6,
        limit=62,
        loose_outs=(0, *range(2, 9)),
    )
    made, grads, sums = {key: [] for key in "dcuab"}, {}, []
    chains = {
        "d": chain("down", parts[:2], made["d"]),
        "c": chain("down_stack", parts[2:4], made["c"], True),
        "u": chain("up", parts[4:], made["u"]),
    }
    state = {"shares_other": swap(shares)}

    def backward():
        (shares_other,) = turn(state["shares_other"])
        ins = [
            shares, shares_other, residual, cotangent, norm_mlp, b_down, attended, w_out, q, k, v,
            probs, cosine, sine, w_query, w_key, w_value, inputs, normed, grad_bu,
        ]
        outs = [rows_of["width"], rows_of["sum"], rows_of["sum"]]
        pieces = portions(half // STACK, half) * 2
        state["output"], state["delta_residual"], state["normed_part"], vec, *parts = call(
            attention_backward,
            [*outs, ((16, half), f32), *pieces],
            loose=ins,
            scratch=[
                *[(a.shape, a.dtype) for a in ins],
                *outs,
                *pieces,
                rows_of["width"],
                *[rows_of["heads"]] * 4,
                ((rows, LANES), f32),
                ((rows, LANES), f32),
                ((PLANE, 2, half, half), f32),
                ((8, width), f32),
                sems(24),
                sems(7),
            ],
            flops=2 * rows * width * heads_cols * 10,
            limit=62,
            loose_outs=(0, 1, 2, 4, 5, 6, 7),
        )
        did(vec)
        state["normed_other"] = swap(state["normed_part"])
        chains["a"] = chain("attention", parts[:2], made["a"], vec=vec)
        chains["b"] = chain("attention_rest", parts[2:], made["b"])

    def input_back():
        (normed_other,) = turn(state["normed_other"])
        (state["grad_inputs"],) = call(
            input_kernel,
            [((rows, width), bf16)],
            held=[state["normed_part"], normed_other, inputs, gain_attn, state["delta_residual"]],
        )
        did(state["grad_inputs"])

    shapes = {
        "down": ((units, width), f32),
        "up": ((width, units), f32),
        "out": ((heads_cols, width), f32),
        "query": ((width, heads_cols), f32),
        "key": ((width, heads_cols), f32),
        "value": ((width, heads_cols), f32),
    }
    attention = ("out", "query", "key", "value")
    targets = {
        "d": (down_views, ("down",)),
        "u": (up_views, ("up",)),
        "c": (stack_views, ("down", "up")),
        "a": (partial(attention_views, 0), attention),
        "b": (partial(attention_views, 1), attention),
    }

    def put(key, sent):
        views, names = targets[key]
        olds = [name for name in names if name in grads]
        assert len(olds) in (0, len(names))
        (piece,) = turn(made[key][sent])
        results = pl.pallas_call(
            partial(put_in_place, views, key == "c", sent, len(olds)),
            name=f"put_{key}",
            out_shape=[jax.ShapeDtypeStruct(*shapes[name]) for name in names],
            in_specs=[VMEM] + [HBM] * len(olds),
            out_specs=[HBM] * len(names),
            scratch_shapes=[sems(32)],
            input_output_aliases={1 + i: i for i in range(len(olds))},
            compiler_params=pltpu.CompilerParams(vmem_limit_bytes=8 * 1024 * 1024),
            cost_estimate=pl.CostEstimate(flops=0, bytes_accessed=2 * piece.size * 4, transcendentals=0),
        )(piece, *[grads[name] for name in olds])
        grads.update(zip(names, results))
        did(results[0])

    did(grad_bu)
    pieces = {"K": backward, "I": input_back}
    waiting = []
    for key in ORDER:
        if key in waiting:
            waiting.remove(key)
            put(key, 0)
        if key in pieces:
            pieces[key]()
        else:
            next(chains[key])
        for other in list(waiting):
            if other != "c" or ("down" in grads and "up" in grads):
                waiting.remove(other)
                put(other, 0)
        if len(made.get(key, ())) == 1:
            waiting.append(key)
        elif len(made.get(key, ())) == 2:
            put(key, 1)

    vec = sums[0]
    n = width // half
    shared = (vec[: 3 * n] + swap(vec[: 3 * n])).reshape(3, width)
    grad_bu = vec[3 * n :].reshape(-1)[:units]
    grad_down, grad_up = grads["down"], grads["up"]
    grad_out, grad_query, grad_key, grad_value = (grads[name] for name in attention)
    output, grad_inputs = state["output"], state["grad_inputs"]
    return (
        output,
        grad_inputs,
        shared[0],
        grad_query,
        grad_key,
        grad_value,
        grad_out,
        shared[1],
        grad_up,
        grad_bu,
        grad_down,
        shared[2],
    )


def solution(mesh):
    count = mesh.shape["dp"]

    def step(*args):
        return on_device(count, *args)

    return jax.shard_map(
        step,
        mesh=mesh,
        in_specs=(
            P("dp", None),
            P(),
            P(None, "mp"),
            P(None, "mp"),
            P(None, "mp"),
            P("mp", None),
            P(),
            P(None, "mp"),
            P("mp"),
            P("mp", None),
            P(),
            P("dp", None),
            P(),
            P(),
        ),
        out_specs=(
            P("dp", None),
            P("dp", None),
            P(),
            P(None, "mp"),
            P(None, "mp"),
            P(None, "mp"),
            P("mp", None),
            P(),
            P(None, "mp"),
            P("mp"),
            P("mp", None),
            P(),
        ),
        check_vma=False,
    )
```

```python
from functools import partial
import math

import numpy as np

import jax
import jax.numpy as jnp
from jax import lax
from jax.experimental import pallas as pl
from jax.experimental.pallas import tpu as pltpu
from jax.sharding import PartitionSpec as P

HEAD = 64
BLOCK = 16
LEN = 256
HALF = 128
LANES = 128
PLANE = 4
STACK = 4
GROUP = PLANE * STACK

norm_eps = 1e-05
rope_base = 10000.0
masked_score = -1e30
score_scale = HEAD ** (-0.5)
bf16 = jnp.bfloat16
f32 = jnp.float32

X, Y, Z1, Z2 = 1, 2, 4, 8
FIRST, SECOND = (X, Y), (Y, X)
Z_FIRST, Z_SECOND = (Z1, Z2), (Z2, Z1)

ORDER = "cudKubcdIuabducdbuacdcaucbdaudabubcadbabac"

CASES = ((0, 0, 256, 0), (128, 256, 384, 128), (256, 640, 128, 128), (384, 768, 256, 128))
TILES = (
    (0, 0, 0, 0),
    (0, 1, 0, 0),
    (0, 1, 128, 0),
    (0, 1, 128, 128),
    (0, 0, 128, 128),
    (1, 1, 0, 0),
    (1, 1, 128, 0),
    (1, 1, 128, 128),
)
KEY_PLACE = (0, 3, 1, 2)


def mm(left, right):
    return jnp.dot(left, right, preferred_element_type=f32)


def tn(left, right):
    return lax.dot_general(left, right, (((0,), (0,)), ((), ())), preferred_element_type=f32)


def nt(left, right):
    return lax.dot_general(left, right, (((1,), (1,)), ((), ())), preferred_element_type=f32)


def rope_tables():
    half = HEAD // 2
    frequency = np.exp(np.arange(half) * (-2.0 * math.log(rope_base) / HEAD)).astype(np.float32)
    turn = (np.arange(LEN, dtype=np.float32)[:, None] * frequency[None, :]).astype(np.float32)
    cosine, sine = np.cos(turn.astype(np.float64)), np.sin(turn.astype(np.float64))
    cosine = np.tile(cosine, (1, LANES // half)).astype(np.float32)
    sine = np.tile(np.concatenate([-sine, sine], 1), (1, LANES // HEAD)).astype(np.float32)
    return cosine, sine


def swap_halves(values):
    lane = lax.broadcasted_iota(jnp.int32, values.shape, 1)
    return jnp.where(
        lane % HEAD < HEAD // 2, pltpu.roll(values, LANES - HEAD // 2, 1), pltpu.roll(values, HEAD // 2, 1)
    )


def head_mask(rows, which):
    lane = lax.broadcasted_iota(jnp.int32, (rows, LANES), 1)
    return (lane >= HEAD) if which else (lane < HEAD)


def layer_norm_rows(values, gain):
    centred = values - jnp.mean(values, axis=-1, keepdims=True)
    spread = jnp.mean(centred * centred, axis=-1, keepdims=True)
    return centred * lax.rsqrt(spread + norm_eps) * gain


def scaled_rows(values):
    centred = values - jnp.mean(values, axis=-1, keepdims=True)
    return centred * lax.rsqrt(jnp.mean(centred * centred, axis=-1, keepdims=True) + norm_eps)


def norm_back_rows(values, gain, delta):
    centred = values - jnp.mean(values, axis=-1, keepdims=True)
    spread = jnp.mean(centred * centred, axis=-1, keepdims=True)
    s = lax.rsqrt(spread + norm_eps)
    xhat = centred * s
    e = delta * gain
    back = s * (e - jnp.mean(e, axis=-1, keepdims=True) - xhat * jnp.mean(e * xhat, axis=-1, keepdims=True))
    return back, jnp.sum(delta * xhat, axis=0, keepdims=True)


def fill_bias(lengths_ref, pads_ref, bias_ref):
    sequence = lax.axis_index("dp")
    docs = lengths_ref.shape[0]
    ends, total = [], jnp.int32(0)
    for j in range(docs):
        total = total + lengths_ref[j, sequence]
        ends.append(total)
    first_pad = LEN - pads_ref[sequence]

    def segment(places):
        seg = jnp.zeros(places.shape, jnp.int32)
        for end in ends:
            seg = seg + (places >= end).astype(jnp.int32)
        return seg

    rows, cols, row_seg, col_seg = {}, {}, {}, {}
    for base in (0, HALF):
        rows[base] = lax.broadcasted_iota(jnp.int32, (HALF, LANES), 0) + base
        cols[base] = lax.broadcasted_iota(jnp.int32, (HALF, LANES), 1) + base
        row_seg[base] = segment(rows[base])
        col_seg[base] = segment(cols[base])
    for tile, (query_kind, key_kind, query_base, key_base) in enumerate(TILES):
        q, k = rows[query_base], cols[key_base]
        query_block, key_block = q // BLOCK, k // BLOCK
        same_doc = (row_seg[query_base] == col_seg[key_base]) & (k < first_pad)
        if query_kind == 0 and key_kind == 0:
            ok = (key_block == query_block) & (same_doc | (q == k))
        elif query_kind == 0:
            ok = (key_block < query_block) & same_doc
        else:
            ok = (key_block <= query_block) & (same_doc | (q == k))
        bias_ref[:, tile * LANES : (tile + 1) * LANES] = jnp.where(ok, 0.0, masked_score)


def fetch(pairs, sems):
    copies = [pltpu.make_async_copy(source, target, sems.at[i]) for i, (source, target) in enumerate(pairs)]
    for copy in copies:
        copy.start()
    return copies


class Sender:
    def __init__(self, sems):
        self.sems, self.copies = sems, []

    def send(self, source, target):
        self.copies.append(pltpu.make_async_copy(source, target, self.sems.at[len(self.copies)]))
        self.copies[-1].start()

    def finish(self):
        for copy in self.copies:
            copy.wait()


def attention_forward(
    lengths_in, pads_in, gain_in, x_in, wq_in, wk_in, wv_in, cos_in, sin_in, wo_in,
    normed_out, q_out, k_out, v_out, att_out, prob_out, part_out,
    bias_ref, lengths_ref, pads_ref, gain_ref, x_ref, wq_ref, wk_ref, wv_ref, cos_ref, sin_ref, wo_ref,
    normed_ref, q_ref, k_ref, v_ref, att_ref, prob_ref, part_ref, sems, out_sems,
):
    first = fetch(((lengths_in, lengths_ref), (pads_in, pads_ref), (x_in, x_ref), (gain_in, gain_ref)), sems.at[:4])
    copies = fetch(
        (
            (wq_in, wq_ref), (wk_in, wk_ref), (wv_in, wv_ref), (cos_in, cos_ref), (sin_in, sin_ref), (wo_in, wo_ref),
        ),
        sems.at[4:],
    )
    sender = Sender(out_sems)
    first[0].wait()
    first[1].wait()
    heads_cols = wq_ref.shape[1]
    pairs = heads_cols // LANES
    fill_bias(lengths_ref, pads_ref, bias_ref)
    first[2].wait()
    first[3].wait()
    gain = gain_ref[...].reshape(1, -1)

    @pl.loop(0, x_ref.shape[0] // 64)
    def _(i):
        rows = pl.ds(pl.multiple_of(i * 64, 64), 64)
        normed_ref[rows, :] = layer_norm_rows(x_ref[rows, :].astype(f32), gain).astype(bf16)

    sender.send(normed_ref, normed_out)
    for copy in copies[:5]:
        copy.wait()
    for block in range(4):
        rows = slice(block * HALF, block * HALF + HALF)
        places = slice((block % 2) * HALF, (block % 2) * HALF + HALF)
        key_rows = slice(KEY_PLACE[block] * HALF, KEY_PLACE[block] * HALF + HALF)
        normed = normed_ref[rows, :]
        cosine, sine = cos_ref[places, :], sin_ref[places, :]
        query, key = mm(normed, wq_ref[...]), mm(normed, wk_ref[...])
        for t in range(pairs):
            cols = slice(t * LANES, (t + 1) * LANES)
            turned = query[:, cols] * cosine + swap_halves(query[:, cols]) * sine
            q_ref[rows, cols] = (turned.astype(bf16).astype(f32) * score_scale).astype(bf16)
            turned = key[:, cols] * cosine + swap_halves(key[:, cols]) * sine
            k_ref[key_rows, cols] = turned.astype(bf16)
        v_ref[key_rows, :] = mm(normed, wv_ref[...]).astype(bf16)
    for source, target in ((q_ref, q_out), (k_ref, k_out), (v_ref, v_out)):
        sender.send(source, target)

    for t in range(pairs):
        cols = slice(t * LANES, (t + 1) * LANES)
        key_pair, value_pair = k_ref[:, cols], v_ref[:, cols]
        mixed = [None] * 4
        jobs, scores, values = [(which, case) for which in range(2) for case in range(4)], [], []
        for which in range(2):
            mask = head_mask(key_pair.shape[0], which)
            key_head = jnp.where(mask, key_pair, jnp.zeros_like(key_pair))
            values.append(jnp.where(mask, value_pair, jnp.zeros_like(value_pair)))
            for query_row, first, width, key_row in CASES:
                found = nt(q_ref[query_row : query_row + HALF, cols], key_head[key_row : key_row + width])
                scores.append(found + bias_ref[:, first : first + width])
        tops = [jnp.max(a, axis=1, keepdims=True) for a in scores]
        weights = [jnp.exp(a - top) for a, top in zip(scores, tops)]
        shares = [1.0 / jnp.sum(a, axis=1, keepdims=True) for a in weights]
        lows = [(a * share).astype(bf16) for a, share in zip(weights, shares)]
        for (which, case), low in zip(jobs, lows):
            _, first, width, key_row = CASES[case]
            prob_ref[2 * t + which, :, first : first + width] = low
            part = mm(low, values[which][key_row : key_row + width])
            mixed[case] = part if mixed[case] is None else mixed[case] + part
        for case, (query_row, _, _, _) in enumerate(CASES):
            att_ref[query_row : query_row + HALF, cols] = mixed[case].astype(bf16)
        sender.send(prob_ref.at[2 * t : 2 * t + 2], prob_out.at[2 * t : 2 * t + 2])

    sender.send(att_ref, att_out)
    copies[5].wait()
    for block in range(2):
        rows = slice(block * 256, block * 256 + 256)
        part_ref[rows, :] = mm(att_ref[rows, :], wo_ref[...])
        sender.send(part_ref.at[rows, :], part_out.at[rows, :])
    sender.finish()


def fourths(start, part):
    return pl.ds(pl.multiple_of(start * part, 8), part)


def slot_at(place):
    core = lax.axis_index("mp") % 2
    return (place // 2) * (1 + core) + (place % 2) * (2 - core)


def quarter_at(place):
    return lax.axis_index("dp") % PLANE ^ slot_at(place)


def fourth_at(place):
    return lax.axis_index("dp") % GROUP // PLANE ^ slot_at(place)


def z_place(block):
    slot = lax.axis_index("dp") % GROUP // PLANE ^ block
    return jnp.where(lax.axis_index("mp") % 2 == 0, (slot % 2) * 2 + slot // 2, slot)


def place_quarter(outs, place, value):
    part = value.shape[0] // STACK
    for block in range(STACK):
        outs[place // 2][place % 2, z_place(block)] = value[block * part : (block + 1) * part]


def place_quarter_z_first(outs, place, first_row, value):
    part = value.shape[0] // STACK
    for block in range(STACK):
        z = z_place(block)
        for sent in range(2):

            @pl.when(z // 2 == sent)
            def _(out=outs[sent], z=z, piece=value[block * part : (block + 1) * part]):
                out[z % 2, place, first_row : first_row + part, :] = piece


def mlp_kernel(
    gain_in, bu_in, x_in, mine_in, theirs_in, cot_in, wu_in, wd_in,
    residual_out, gbu_ref, d_kept, d_sent, c_kept, c_sent, u_kept, u_sent, shares_out,
    gain_ref, bu_ref, x_ref, mine_ref, theirs_ref, cot_ref, wu_ref, wd_ref,
    residual_ref, normed_ref, act_ref, du_ref, d_kept_ref, d_sent_ref, c_kept_ref, c_sent_ref, u_kept_ref, u_sent_ref, shares_ref,
    sems, out_sems,
):
    row_count = x_ref.shape[0]
    units = wu_ref.shape[1]
    halves = (slice(0, row_count // 2), slice(row_count // 2, row_count))
    pairs = [(gain_in, gain_ref), (bu_in, bu_ref)]
    for rows in halves:
        pairs += [(a.at[rows, :], b.at[rows, :]) for a, b in ((x_in, x_ref), (mine_in, mine_ref), (theirs_in, theirs_ref))]
    copies = fetch(pairs + [(cot_in, cot_ref), (wu_in, wu_ref), (wd_in, wd_ref)], sems)
    sender = Sender(out_sems)
    gbu_ref[...] = jnp.zeros_like(gbu_ref)
    copies[0].wait()
    gain = gain_ref[...].reshape(1, -1)
    for half in range(2):
        for copy in copies[2 + 3 * half : 5 + 3 * half]:
            copy.wait()

        @pl.loop(0, row_count // 128)
        def _(i, half=half):
            rows = pl.ds(pl.multiple_of(half * (row_count // 2) + i * 64, 64), 64)
            residual = x_ref[rows, :].astype(f32) + (mine_ref[rows, :] + theirs_ref[rows, :])
            residual_ref[rows, :] = residual
            normed_ref[rows, :] = layer_norm_rows(residual, gain).astype(bf16)

    sender.send(residual_ref, residual_out)
    for copy in (copies[1], *copies[8:]):
        copy.wait()
    c0 = math.sqrt(2.0 / math.pi)
    c1 = c0 * 0.044715

    @pl.loop(0, units // 512)
    def _(j):
        cols = pl.ds(pl.multiple_of(j * 512, 512), 512)
        blocks = [slice(block * 256, block * 256 + 256) for block in range(row_count // 256)]
        ups = [mm(normed_ref[rows, :], wu_ref[:, cols]) + bu_ref[cols].reshape(1, -1) for rows in blocks]
        deltas = [nt(cot_ref[rows, :], wd_ref[cols, :]) for rows in blocks]
        for rows, u, delta in zip(blocks, ups, deltas):
            square = u * u
            t = jnp.tanh(u * (c0 + c1 * square))
            half_up = 0.5 + 0.5 * t
            act = u * half_up
            act_ref[rows, cols] = act.astype(bf16)
            slope = half_up + act * ((1.0 - t) * (c0 + (3.0 * c1) * square))
            low = (delta * slope).astype(bf16)
            du_ref[rows, cols] = low
            gbu_ref[:, cols] += jnp.sum(low.astype(f32), axis=0, keepdims=True)

    quarter = units // PLANE
    fourth = units // GROUP
    cut = cot_ref.shape[1] * 2 // 3
    up_cut = quarter * 2 // 3
    quarters = {}
    for place in range(PLANE):
        quarters[place] = pl.ds(pl.multiple_of(quarter_at(place) * quarter, LANES), quarter)
    for share in range(2):
        for rows in halves:
            if share == 0:
                shares_ref[share, rows, :] = nt(du_ref[rows, :], wu_ref[...])
            else:
                shares_ref[share, rows, :] = mm(act_ref[rows, :], wd_ref[...])
        sender.send(shares_ref.at[share], shares_out.at[share])
    c_pairs = ((c_kept_ref, c_kept), (c_sent_ref, c_sent))
    for place in (2, 3, 0, 1):
        grad = tn(act_ref[:, quarters[place]], cot_ref[...])
        place_quarter((d_kept_ref, d_sent_ref), place, grad[:, :cut])
        place_quarter_z_first((c_kept_ref, c_sent_ref), place, 0, grad[:, cut:])
        source, target = ((d_kept_ref, d_kept), (d_sent_ref, d_sent))[place // 2]
        sender.send(source.at[place % 2], target.at[place % 2])
        for source, target in c_pairs:
            rows = pl.ds(0, fourth)
            sender.send(source.at[:, place, rows, :], target.at[:, place, rows, :])
    for place in (2, 3, 0, 1):
        grad = tn(normed_ref[...], du_ref[:, quarters[place]])
        place_quarter((u_kept_ref, u_sent_ref), place, grad[:, :up_cut])
        rest = grad[:, up_cut:].reshape(STACK, 2, fourth, -1)
        rest = jnp.concatenate([rest[:, 0], rest[:, 1]], 2).reshape(STACK * fourth, -1)
        place_quarter_z_first((c_kept_ref, c_sent_ref), place, fourth, rest)
        source, target = ((u_kept_ref, u_kept), (u_sent_ref, u_sent))[place // 2]
        sender.send(source.at[place % 2], target.at[place % 2])
        for source, target in c_pairs:
            rows = pl.ds(fourth, fourth)
            sender.send(source.at[:, place, rows, :], target.at[:, place, rows, :])
    sender.finish()


def attention_backward(*refs):
    ins, refs = refs[:20], refs[20:]
    (output_out, delta_out, part_out, vec_ref), outs_at, refs = refs[:4], refs[4:8], refs[8:]
    held, refs = refs[:20], refs[20:]
    (output_ref, delta_ref, part_ref), outs, refs = refs[:3], refs[3:7], refs[7:]
    branch_ref, datt_ref, dq_ref, dk_ref, dv_ref, dk_acc, dv_acc, grads_ref, gnorm_ref, sems, out_sems = refs
    mine_ref, theirs_ref, residual_ref, cot_ref, gain_ref, bd_ref, att_ref, wo_ref, q_ref, k_ref, v_ref = held[:11]
    prob_ref, cos_ref, sin_ref, wq_ref, wk_ref, wv_ref, x_ref, normed_ref, gbu_ref = held[11:]
    row_count = residual_ref.shape[0]
    heads_cols = wq_ref.shape[1]
    pairs = heads_cols // LANES
    halves = (slice(0, row_count // 2), slice(row_count // 2, row_count))
    first = []
    for rows in halves:
        first += [(a.at[:, rows, :], b.at[:, rows, :]) for a, b in zip(ins[:2], held[:2])]
        first += [(a.at[rows, :], b.at[rows, :]) for a, b in zip(ins[2:4], held[2:4])]
    copies = fetch(first + list(zip(ins[4:], held[4:])), sems)
    sender = Sender(out_sems)
    gnorm_ref[...] = jnp.zeros_like(gnorm_ref)
    copies[8].wait()
    copies[9].wait()
    gain, bias_down = gain_ref[...].reshape(1, -1), bd_ref[...].reshape(1, -1)
    for half in range(2):
        for copy in copies[4 * half : 4 * half + 4]:
            copy.wait()

        @pl.loop(0, row_count // 128)
        def _(i, half=half):
            rows = pl.ds(pl.multiple_of(half * (row_count // 2) + i * 64, 64), 64)
            delta = mine_ref[0, rows, :] + theirs_ref[0, rows, :]
            residual = residual_ref[rows, :]
            output_ref[rows, :] = (residual + (mine_ref[1, rows, :] + theirs_ref[1, rows, :]) + bias_down).astype(bf16)
            back, gain_part = norm_back_rows(residual, gain, delta)
            cotangent = cot_ref[rows, :].astype(f32)
            back = back + cotangent
            delta_ref[rows, :] = back
            branch_ref[rows, :] = back.astype(bf16)
            gnorm_ref[0:1, :] += gain_part
            gnorm_ref[2:3, :] += jnp.sum(cotangent, axis=0, keepdims=True)

    sender.send(output_ref, output_out)
    sender.send(delta_ref, delta_out)
    for copy in copies[10:]:
        copy.wait()
    for block in range(2):
        rows = slice(block * 256, block * 256 + 256)
        datt_ref[rows, :] = nt(branch_ref[rows, :], wo_ref[...]).astype(bf16)
    half = heads_cols
    grad = tn(att_ref[...], branch_ref[...])
    grads_ref[0, 0], grads_ref[0, 1] = grad[:, :half], grad[:, half:]

    for t in range(pairs):
        cols = slice(t * LANES, (t + 1) * LANES)
        key_pair, value_pair = k_ref[:, cols], v_ref[:, cols]
        dk_acc[...] = jnp.zeros_like(dk_acc)
        dv_acc[...] = jnp.zeros_like(dv_acc)
        query_grads = [None] * 4
        jobs, deltas, lows, keys_of = [], [], [], []
        for which in range(2):
            mask = head_mask(key_pair.shape[0], which)
            keys_of.append(jnp.where(mask, key_pair, jnp.zeros_like(key_pair)))
            value_head = jnp.where(mask, value_pair, jnp.zeros_like(value_pair))
            for case, (query_row, first, width, key_row) in enumerate(CASES):
                jobs.append((which, case))
                lows.append(prob_ref[2 * t + which, :, first : first + width])
                rows = slice(query_row, query_row + HALF)
                deltas.append(nt(datt_ref[rows, cols], value_head[key_row : key_row + width]))
        wides = [low.astype(f32) for low in lows]
        weighted = [wide * g for wide, g in zip(wides, deltas)]
        totals = [jnp.sum(a, axis=1, keepdims=True) for a in weighted]
        backs = [(a - wide * total).astype(bf16) for a, wide, total in zip(weighted, wides, totals)]
        for (which, case), low, back in zip(jobs, lows, backs):
            query_row, _, width, key_row = CASES[case]
            rows, keys = slice(query_row, query_row + HALF), slice(key_row, key_row + width)
            small = head_mask(HALF, which)
            part = mm(back, keys_of[which][keys])
            query_grads[case] = part if query_grads[case] is None else query_grads[case] + part
            query, delta_head = q_ref[rows, cols], datt_ref[rows, cols]
            dk_acc[keys, :] += tn(back, jnp.where(small, query, jnp.zeros_like(query)))
            dv_acc[keys, :] += tn(low, jnp.where(small, delta_head, jnp.zeros_like(delta_head)))
        for block in range(4):
            rows = slice(block * HALF, block * HALF + HALF)
            places = slice((block % 2) * HALF, (block % 2) * HALF + HALF)
            key_rows = slice(KEY_PLACE[block] * HALF, KEY_PLACE[block] * HALF + HALF)
            cosine, sine = cos_ref[places, :], sin_ref[places, :]
            grad = query_grads[block] * score_scale
            dq_ref[rows, cols] = (grad * cosine - swap_halves(grad) * sine).astype(bf16)
            grad = dk_acc[key_rows, :]
            dk_ref[rows, cols] = (grad * cosine - swap_halves(grad) * sine).astype(bf16)
            dv_ref[rows, cols] = dv_acc[key_rows, :].astype(bf16)

    for block in range(2):
        rows = slice(block * 256, block * 256 + 256)
        part_ref[rows, :] = (
            nt(dq_ref[rows, :], wq_ref[...]) + nt(dk_ref[rows, :], wk_ref[...]) + nt(dv_ref[rows, :], wv_ref[...])
        )
    sender.send(part_ref, part_out)

    @pl.loop(0, row_count // 64)
    def _(i):
        rows = pl.ds(pl.multiple_of(i * 64, 64), 64)
        gnorm_ref[1:2, :] += jnp.sum(part_ref[rows, :] * scaled_rows(x_ref[rows, :].astype(f32)), axis=0, keepdims=True)

    vec_ref[...] = jnp.zeros_like(vec_ref)
    row = 0
    once = jnp.where(lax.axis_index("mp") == 0, 1.0, 0.0)
    for values in (gnorm_ref[1:2, :], gnorm_ref[0:1, :] * once, gnorm_ref[2:3, :] * once, gbu_ref[...]):
        for first in range(0, values.shape[1], half):
            vec_ref[row : row + 1, :] = values[:, first : first + half]
            row += 1

    for matrix, grad_rows in ((1, dq_ref), (2, dk_ref), (3, dv_ref)):
        grad = tn(normed_ref[...], grad_rows[...])
        grads_ref[matrix, 0], grads_ref[matrix, 1] = grad[:half], grad[half:]
    for places in ((2, 3), (0, 1)):
        for place in places:
            quarter = quarter_at(place)
            place_quarter(outs[:2], place, grads_ref[quarter, 0])
            place_quarter(outs[2:], place, grads_ref[quarter, 1])
        for portion in range(2):
            which = 2 * portion + places[0] // 2
            sender.send(outs[which], outs_at[which])
    sender.finish()


def input_kernel(mine_ref, theirs_ref, x_ref, gain_ref, delta_ref, grad_ref):
    @pl.loop(0, x_ref.shape[0] // 64)
    def _(i):
        rows = pl.ds(pl.multiple_of(i * 64, 64), 64)
        delta = mine_ref[rows, :] + theirs_ref[rows, :]
        back, _ = norm_back_rows(x_ref[rows, :].astype(f32), gain_ref[...], delta)
        grad_ref[rows, :] = (delta_ref[rows, :] + back).astype(bf16)


def put_in_place(views, z_first, sent, olds, piece_ref, *refs):
    *refs, sems = refs
    outs = refs[olds:]
    for start in (True, False):
        count = 0
        for i in range(2):
            for j in range(STACK):
                z, place = (2 * sent + i, j) if z_first else (j, 2 * sent + i)
                for wanted, source, target in views(outs, quarter_at(place), fourth_at(z), piece_ref.at[i, j]):
                    copy = pltpu.make_async_copy(source, target, sems.at[count])
                    count += 1
                    act = copy.start if start else copy.wait
                    if wanted is None:
                        act()
                    else:
                        pl.when(wanted)(act)


def down_views(outs, quarter, fourth, block):
    part, cols = block.shape
    yield None, block, outs[0].at[fourths(quarter * STACK + fourth, part), pl.ds(0, cols)]


def up_views(outs, quarter, fourth, block):
    part, cols = block.shape
    whole = outs[0].shape[1] // PLANE
    yield None, block, outs[0].at[fourths(fourth, part), pl.ds(pl.multiple_of(quarter * whole, LANES), cols)]


def stack_views(outs, quarter, fourth, block):
    part, cols = block.shape[0] // 2, block.shape[1]
    whole, rest = outs[1].shape[1] // PLANE, cols // 2
    down_rows, down_cols = fourths(quarter * STACK + fourth, part), pl.ds(outs[0].shape[1] - cols, cols)
    yield None, block.at[pl.ds(0, part), :], outs[0].at[down_rows, down_cols]
    up_cols = pl.ds(pl.multiple_of((quarter + 1) * whole - rest, LANES), rest)
    for half in range(2):
        source = block.at[pl.ds(part, part), pl.ds(half * rest, rest)]
        yield None, source, outs[1].at[fourths(fourth * 2 + half, part), up_cols]


def attention_views(portion, outs, quarter, fourth, block):
    part, half = block.shape[0], block.shape[1]
    for matrix, out in enumerate(outs):
        if matrix:
            target = out.at[pl.ds(pl.multiple_of(portion * half + fourth * part, 8), part), :]
        else:
            target = out.at[fourths(fourth, part), pl.ds(portion * half, half)]
        yield quarter == matrix, block, target


VMEM = pl.BlockSpec(memory_space=pltpu.VMEM)
HBM = pl.BlockSpec(memory_space=pltpu.HBM)


def call(kernel, outs, held=(), loose=(), scratch=(), flops=0, limit=40, loose_outs=None):
    ins = [*held, *loose]
    shapes = [jax.ShapeDtypeStruct(shape, dtype) for shape, dtype in outs]
    moved = sum(math.prod(a.shape) * a.dtype.itemsize for a in ins + shapes)
    out_specs = [HBM if loose_outs and i in loose_outs else VMEM for i in range(len(outs))]
    return pl.pallas_call(
        kernel,
        name=kernel.__name__,
        out_shape=shapes,
        in_specs=[VMEM] * len(held) + [HBM] * len(loose),
        out_specs=out_specs,
        scratch_shapes=[s if not isinstance(s, tuple) else pltpu.VMEM(*s) for s in scratch],
        compiler_params=pltpu.CompilerParams(vmem_limit_bytes=limit * 1024 * 1024),
        cost_estimate=pl.CostEstimate(flops=flops, bytes_accessed=moved, transcendentals=0),
    )(*ins)


def on_device(
    count,
    inputs, norm_attn, w_query, w_key, w_value, w_out, norm_mlp, w_up, b_up, w_down, b_down, cotangent,
    doc_lengths, pad_counts,
):
    rows, width = inputs.shape
    heads_cols = w_query.shape[1]
    units = w_up.shape[1]
    heads = heads_cols // HEAD
    cosine, sine = (jnp.asarray(t) for t in rope_tables())
    gain_attn = norm_attn.reshape(1, -1)

    def swap(values):
        return lax.ppermute(values, "mp", [(0, 1), (1, 0)])

    def flip(values, bits, name):
        pairs = [(2 * i + core, 2 * (i ^ bits[core]) + core) for i in range(count) for core in range(2)]
        with jax.named_scope(name):
            return lax.ppermute(values, ("dp", "mp"), pairs)

    def sems(n):
        return pltpu.SemaphoreType.DMA((n,))

    half = heads_cols

    def portions(*shape):
        return [((2, STACK) + shape, f32)] * 2

    last = []

    def turn(*values):
        if not last:
            return values
        values, _ = lax.optimization_barrier((values, last.pop()))
        return values

    def did(value):
        last[:] = [value]
        return value

    def over_groups(values):
        if count == GROUP:
            return values
        groups = [[k * GROUP + j for k in range(count // GROUP)] for j in range(GROUP)]
        return lax.psum(values, "dp", axis_index_groups=groups)

    def chain(name, parts, result, z_first=False, vec=None):
        keep, send = parts
        plane, stack = [(FIRST, "first"), (SECOND, "second")], [(Z_FIRST, "z_first"), (Z_SECOND, "z_second")]
        steps = stack + plane if z_first else plane + stack

        def join(values):
            return values if vec is None else jnp.concatenate([values.reshape(-1, values.shape[-1]), vec], 0)

        def part_of(got, like, vec):
            if vec is None:
                return got, None
            return got[: -vec.shape[0]].reshape(like.shape), vec + got[-vec.shape[0] :]

        for step, (bits, label) in enumerate(steps):
            if step:
                keep, got, vec = turn(keep, got, vec)
                got, vec = part_of(got, keep, vec)
            if step == 0:
                send = join(send)
            elif step == 1:
                send, keep = did(join(keep[1] + got[1])), keep[0] + got[0]
            elif step == 2:
                send, keep = did(join(keep[2:] + got[2:])), keep[:2] + got[:2]
            else:
                keep = keep + got
                send = did(join(keep))
            got = flip(send, bits, f"{name}_sum_{label}")
            yield
        keep, got, vec = turn(keep, got, vec)
        got, vec = part_of(got, keep, vec)
        own = over_groups(did(keep + got[::-1]))
        if vec is not None:
            sums.append(over_groups(vec))
        for step, (bits, label) in enumerate(reversed(steps[:3])):
            got = flip(own, bits, f"{name}_gather_{label}")
            if step == 2:
                result.append(own)
            yield
            own, got = turn(own, got)
            if step < 2:
                own = did(jnp.stack([own, got]) if step == 1 else jnp.concatenate([own, got], 0))
        did(got)
        result.append(got)
        yield

    scores = (heads, HALF, 8 * LANES)
    rows_of = {"width": ((rows, width), bf16), "heads": ((rows, heads_cols), bf16), "sum": ((rows, width), f32)}
    outs = [rows_of["width"]] + [rows_of["heads"]] * 4 + [(scores, bf16), rows_of["sum"]]
    normed, q, k, v, attended, probs, branch = call(
        attention_forward,
        outs,
        loose=[doc_lengths.T, pad_counts, norm_attn, inputs, w_query, w_key, w_value, cosine, sine, w_out],
        scratch=[
            (scores[1:], f32),
            pltpu.SMEM(doc_lengths.shape[::-1], jnp.int32),
            pltpu.SMEM(pad_counts.shape, jnp.int32),
            (norm_attn.shape, f32),
            rows_of["width"],
            *[((width, heads_cols), bf16)] * 3,
            (cosine.shape, f32),
            (sine.shape, f32),
            ((heads_cols, width), bf16),
            *outs,
            sems(10),
            sems(10),
        ],
        flops=2 * rows * width * heads_cols * 4,
        limit=62,
        loose_outs=range(7),
    )
    branch_other = swap(branch)

    big = [
        *portions(units // GROUP, width * 2 // 3),
        *portions(units // GROUP + width // STACK // 2, width // 3),
        *portions(width // STACK, units // PLANE * 2 // 3),
        ((2, rows, width), f32),
    ]
    residual, grad_bu, *parts, shares = call(
        mlp_kernel,
        [rows_of["sum"], ((1, units), f32), *big],
        loose=[norm_mlp, b_up, inputs, branch, branch_other, cotangent, w_up, w_down],
        scratch=[
            (norm_mlp.shape, f32),
            (b_up.shape, f32),
            rows_of["width"],
            rows_of["sum"],
            rows_of["sum"],
            rows_of["width"],
            ((width, units), bf16),
            ((units, width), bf16),
            rows_of["sum"],
            rows_of["width"],
            ((rows, units), bf16),
            ((rows, units), bf16),
            *big,
            sems(11),
            sems(27),
        ],
        flops=2 * rows * width * units * 6,
        limit=62,
        loose_outs=(0, *range(2, 9)),
    )
    made, grads, sums = {key: [] for key in "dcuab"}, {}, []
    chains = {
        "d": chain("down", parts[:2], made["d"]),
        "c": chain("down_stack", parts[2:4], made["c"], True),
        "u": chain("up", parts[4:], made["u"]),
    }
    state = {"shares_other": swap(shares)}

    def backward():
        (shares_other,) = turn(state["shares_other"])
        ins = [
            shares, shares_other, residual, cotangent, norm_mlp, b_down, attended, w_out, q, k, v,
            probs, cosine, sine, w_query, w_key, w_value, inputs, normed, grad_bu,
        ]
        outs = [rows_of["width"], rows_of["sum"], rows_of["sum"]]
        pieces = portions(half // STACK, half) * 2
        state["output"], state["delta_residual"], state["normed_part"], vec, *parts = call(
            attention_backward,
            [*outs, ((16, half), f32), *pieces],
            loose=ins,
            scratch=[
                *[(a.shape, a.dtype) for a in ins],
                *outs,
                *pieces,
                rows_of["width"],
                *[rows_of["heads"]] * 4,
                ((rows, LANES), f32),
                ((rows, LANES), f32),
                ((PLANE, 2, half, half), f32),
                ((8, width), f32),
                sems(24),
                sems(7),
            ],
            flops=2 * rows * width * heads_cols * 10,
            limit=62,
            loose_outs=(0, 1, 2, 4, 5, 6, 7),
        )
        did(vec)
        state["normed_other"] = swap(state["normed_part"])
        chains["a"] = chain("attention", parts[:2], made["a"], vec=vec)
        chains["b"] = chain("attention_rest", parts[2:], made["b"])

    def input_back():
        (normed_other,) = turn(state["normed_other"])
        (state["grad_inputs"],) = call(
            input_kernel,
            [((rows, width), bf16)],
            held=[state["normed_part"], normed_other, inputs, gain_attn, state["delta_residual"]],
        )
        did(state["grad_inputs"])

    shapes = {
        "down": ((units, width), f32),
        "up": ((width, units), f32),
        "out": ((heads_cols, width), f32),
        "query": ((width, heads_cols), f32),
        "key": ((width, heads_cols), f32),
        "value": ((width, heads_cols), f32),
    }
    attention = ("out", "query", "key", "value")
    targets = {
        "d": (down_views, ("down",)),
        "u": (up_views, ("up",)),
        "c": (stack_views, ("down", "up")),
        "a": (partial(attention_views, 0), attention),
        "b": (partial(attention_views, 1), attention),
    }

    def put(key, sent):
        views, names = targets[key]
        olds = [name for name in names if name in grads]
        assert len(olds) in (0, len(names))
        (piece,) = turn(made[key][sent])
        results = pl.pallas_call(
            partial(put_in_place, views, key == "c", sent, len(olds)),
            name=f"put_{key}",
            out_shape=[jax.ShapeDtypeStruct(*shapes[name]) for name in names],
            in_specs=[VMEM] + [HBM] * len(olds),
            out_specs=[HBM] * len(names),
            scratch_shapes=[sems(32)],
            input_output_aliases={1 + i: i for i in range(len(olds))},
            compiler_params=pltpu.CompilerParams(vmem_limit_bytes=8 * 1024 * 1024),
            cost_estimate=pl.CostEstimate(flops=0, bytes_accessed=2 * piece.size * 4, transcendentals=0),
        )(piece, *[grads[name] for name in olds])
        grads.update(zip(names, results))
        did(results[0])

    did(grad_bu)
    pieces = {"K": backward, "I": input_back}
    waiting = []
    for key in ORDER:
        if key in waiting:
            waiting.remove(key)
            put(key, 0)
        if key in pieces:
            pieces[key]()
        else:
            next(chains[key])
        for other in list(waiting):
            if other != "c" or ("down" in grads and "up" in grads):
                waiting.remove(other)
                put(other, 0)
        if len(made.get(key, ())) == 1:
            waiting.append(key)
        elif len(made.get(key, ())) == 2:
            put(key, 1)

    vec = sums[0]
    n = width // half
    shared = (vec[: 3 * n] + swap(vec[: 3 * n])).reshape(3, width)
    grad_bu = vec[3 * n :].reshape(-1)[:units]
    grad_down, grad_up = grads["down"], grads["up"]
    grad_out, grad_query, grad_key, grad_value = (grads[name] for name in attention)
    output, grad_inputs = state["output"], state["grad_inputs"]
    return (
        output,
        grad_inputs,
        shared[0],
        grad_query,
        grad_key,
        grad_value,
        grad_out,
        shared[1],
        grad_up,
        grad_bu,
        grad_down,
        shared[2],
    )


def solution(mesh):
    count = mesh.shape["dp"]

    def step(*args):
        return on_device(count, *args)

    return jax.shard_map(
        step,
        mesh=mesh,
        in_specs=(
            P("dp", None),
            P(),
            P(None, "mp"),
            P(None, "mp"),
            P(None, "mp"),
            P("mp", None),
            P(),
            P(None, "mp"),
            P("mp"),
            P("mp", None),
            P(),
            P("dp", None),
            P(),
            P(),
        ),
        out_specs=(
            P("dp", None),
            P("dp", None),
            P(),
            P(None, "mp"),
            P(None, "mp"),
            P(None, "mp"),
            P("mp", None),
            P(),
            P(None, "mp"),
            P("mp"),
            P("mp", None),
            P(),
        ),
        check_vma=False,
    )
```

```python
from functools import partial
import math

import numpy as np

import jax
import jax.numpy as jnp
from jax import lax
from jax.experimental import pallas as pl
from jax.experimental.pallas import tpu as pltpu
from jax.sharding import PartitionSpec as P

HEAD = 64
BLOCK = 16
LEN = 256
HALF = 128
LANES = 128
PLANE = 4
STACK = 4
GROUP = PLANE * STACK

norm_eps = 1e-05
rope_base = 10000.0
masked_score = -1e30
score_scale = HEAD ** (-0.5)
bf16 = jnp.bfloat16
f32 = jnp.float32

X, Y, Z1, Z2 = 1, 2, 4, 8
FIRST, SECOND = (X, Y), (Y, X)
Z_FIRST, Z_SECOND = (Z1, Z2), (Z2, Z1)

ORDER = "cudKubcdIuabducdbuacdcaucbdaudabubcadbabac"

CASES = ((0, 0, 256, 0), (128, 256, 384, 128), (256, 640, 128, 128), (384, 768, 256, 128))
TILES = (
    (0, 0, 0, 0),
    (0, 1, 0, 0),
    (0, 1, 128, 0),
    (0, 1, 128, 128),
    (0, 0, 128, 128),
    (1, 1, 0, 0),
    (1, 1, 128, 0),
    (1, 1, 128, 128),
)
KEY_PLACE = (0, 3, 1, 2)


def mm(left, right):
    return jnp.dot(left, right, preferred_element_type=f32)


def tn(left, right):
    return lax.dot_general(left, right, (((0,), (0,)), ((), ())), preferred_element_type=f32)


def nt(left, right):
    return lax.dot_general(left, right, (((1,), (1,)), ((), ())), preferred_element_type=f32)


def rope_tables():
    half = HEAD // 2
    frequency = np.exp(np.arange(half) * (-2.0 * math.log(rope_base) / HEAD)).astype(np.float32)
    turn = (np.arange(LEN, dtype=np.float32)[:, None] * frequency[None, :]).astype(np.float32)
    cosine, sine = np.cos(turn.astype(np.float64)), np.sin(turn.astype(np.float64))
    cosine = np.tile(cosine, (1, LANES // half)).astype(np.float32)
    sine = np.tile(np.concatenate([-sine, sine], 1), (1, LANES // HEAD)).astype(np.float32)
    return cosine, sine


def swap_halves(values):
    lane = lax.broadcasted_iota(jnp.int32, values.shape, 1)
    return jnp.where(
        lane % HEAD < HEAD // 2, pltpu.roll(values, LANES - HEAD // 2, 1), pltpu.roll(values, HEAD // 2, 1)
    )


def head_mask(rows, which):
    lane = lax.broadcasted_iota(jnp.int32, (rows, LANES), 1)
    return (lane >= HEAD) if which else (lane < HEAD)


def layer_norm_rows(values, gain):
    centred = values - jnp.mean(values, axis=-1, keepdims=True)
    spread = jnp.mean(centred * centred, axis=-1, keepdims=True)
    return centred * lax.rsqrt(spread + norm_eps) * gain


def scaled_rows(values):
    centred = values - jnp.mean(values, axis=-1, keepdims=True)
    return centred * lax.rsqrt(jnp.mean(centred * centred, axis=-1, keepdims=True) + norm_eps)


def norm_back_rows(values, gain, delta):
    centred = values - jnp.mean(values, axis=-1, keepdims=True)
    spread = jnp.mean(centred * centred, axis=-1, keepdims=True)
    s = lax.rsqrt(spread + norm_eps)
    xhat = centred * s
    e = delta * gain
    back = s * (e - jnp.mean(e, axis=-1, keepdims=True) - xhat * jnp.mean(e * xhat, axis=-1, keepdims=True))
    return back, jnp.sum(delta * xhat, axis=0, keepdims=True)


def fill_bias(lengths_ref, pads_ref, bias_ref):
    sequence = lax.axis_index("dp")
    docs = lengths_ref.shape[0]
    ends, total = [], jnp.int32(0)
    for j in range(docs):
        total = total + lengths_ref[j, sequence]
        ends.append(total)
    first_pad = LEN - pads_ref[sequence]

    def segment(places):
        seg = jnp.zeros(places.shape, jnp.int32)
        for end in ends:
            seg = seg + (places >= end).astype(jnp.int32)
        return seg

    rows, cols, row_seg, col_seg = {}, {}, {}, {}
    for base in (0, HALF):
        rows[base] = lax.broadcasted_iota(jnp.int32, (HALF, LANES), 0) + base
        cols[base] = lax.broadcasted_iota(jnp.int32, (HALF, LANES), 1) + base
        row_seg[base] = segment(rows[base])
        col_seg[base] = segment(cols[base])
    for tile, (query_kind, key_kind, query_base, key_base) in enumerate(TILES):
        q, k = rows[query_base], cols[key_base]
        query_block, key_block = q // BLOCK, k // BLOCK
        same_doc = (row_seg[query_base] == col_seg[key_base]) & (k < first_pad)
        if query_kind == 0 and key_kind == 0:
            ok = (key_block == query_block) & (same_doc | (q == k))
        elif query_kind == 0:
            ok = (key_block < query_block) & same_doc
        else:
            ok = (key_block <= query_block) & (same_doc | (q == k))
        bias_ref[:, tile * LANES : (tile + 1) * LANES] = jnp.where(ok, 0.0, masked_score)


def fetch(pairs, sems):
    copies = [pltpu.make_async_copy(source, target, sems.at[i]) for i, (source, target) in enumerate(pairs)]
    for copy in copies:
        copy.start()
    return copies


class Sender:
    def __init__(self, sems):
        self.sems, self.copies = sems, []

    def send(self, source, target):
        self.copies.append(pltpu.make_async_copy(source, target, self.sems.at[len(self.copies)]))
        self.copies[-1].start()

    def finish(self):
        for copy in self.copies:
            copy.wait()


def attention_forward(
    lengths_in, pads_in, gain_in, x_in, wq_in, wk_in, wv_in, cos_in, sin_in, wo_in,
    normed_out, q_out, k_out, v_out, att_out, prob_out, part_out,
    bias_ref, lengths_ref, pads_ref, gain_ref, x_ref, wq_ref, wk_ref, wv_ref, cos_ref, sin_ref, wo_ref,
    normed_ref, q_ref, k_ref, v_ref, att_ref, prob_ref, part_ref, sems, out_sems,
):
    first = fetch(((lengths_in, lengths_ref), (pads_in, pads_ref), (x_in, x_ref), (gain_in, gain_ref)), sems.at[:4])
    copies = fetch(
        (
            (wq_in, wq_ref), (wk_in, wk_ref), (wv_in, wv_ref), (cos_in, cos_ref), (sin_in, sin_ref), (wo_in, wo_ref),
        ),
        sems.at[4:],
    )
    sender = Sender(out_sems)
    first[0].wait()
    first[1].wait()
    heads_cols = wq_ref.shape[1]
    pairs = heads_cols // LANES
    fill_bias(lengths_ref, pads_ref, bias_ref)
    first[2].wait()
    first[3].wait()
    gain = gain_ref[...].reshape(1, -1)

    @pl.loop(0, x_ref.shape[0] // 64)
    def _(i):
        rows = pl.ds(pl.multiple_of(i * 64, 64), 64)
        normed_ref[rows, :] = layer_norm_rows(x_ref[rows, :].astype(f32), gain).astype(bf16)

    sender.send(normed_ref, normed_out)
    for copy in copies[:5]:
        copy.wait()
    for block in range(4):
        rows = slice(block * HALF, block * HALF + HALF)
        places = slice((block % 2) * HALF, (block % 2) * HALF + HALF)
        key_rows = slice(KEY_PLACE[block] * HALF, KEY_PLACE[block] * HALF + HALF)
        normed = normed_ref[rows, :]
        cosine, sine = cos_ref[places, :], sin_ref[places, :]
        query, key = mm(normed, wq_ref[...]), mm(normed, wk_ref[...])
        for t in range(pairs):
            cols = slice(t * LANES, (t + 1) * LANES)
            turned = query[:, cols] * cosine + swap_halves(query[:, cols]) * sine
            q_ref[rows, cols] = (turned.astype(bf16).astype(f32) * score_scale).astype(bf16)
            turned = key[:, cols] * cosine + swap_halves(key[:, cols]) * sine
            k_ref[key_rows, cols] = turned.astype(bf16)
        v_ref[key_rows, :] = mm(normed, wv_ref[...]).astype(bf16)
    for source, target in ((q_ref, q_out), (k_ref, k_out), (v_ref, v_out)):
        sender.send(source, target)

    for t in range(pairs):
        cols = slice(t * LANES, (t + 1) * LANES)
        key_pair, value_pair = k_ref[:, cols], v_ref[:, cols]
        mixed = [None] * 4
        jobs, scores, values = [(which, case) for which in range(2) for case in range(4)], [], []
        for which in range(2):
            mask = head_mask(key_pair.shape[0], which)
            key_head = jnp.where(mask, key_pair, jnp.zeros_like(key_pair))
            values.append(jnp.where(mask, value_pair, jnp.zeros_like(value_pair)))
            for query_row, first, width, key_row in CASES:
                found = nt(q_ref[query_row : query_row + HALF, cols], key_head[key_row : key_row + width])
                scores.append(found + bias_ref[:, first : first + width])
        tops = [jnp.max(a, axis=1, keepdims=True) for a in scores]
        weights = [jnp.exp(a - top) for a, top in zip(scores, tops)]
        shares = [1.0 / jnp.sum(a, axis=1, keepdims=True) for a in weights]
        lows = [(a * share).astype(bf16) for a, share in zip(weights, shares)]
        for (which, case), low in zip(jobs, lows):
            _, first, width, key_row = CASES[case]
            prob_ref[2 * t + which, :, first : first + width] = low
            part = mm(low, values[which][key_row : key_row + width])
            mixed[case] = part if mixed[case] is None else mixed[case] + part
        for case, (query_row, _, _, _) in enumerate(CASES):
            att_ref[query_row : query_row + HALF, cols] = mixed[case].astype(bf16)
        sender.send(prob_ref.at[2 * t : 2 * t + 2], prob_out.at[2 * t : 2 * t + 2])

    sender.send(att_ref, att_out)
    copies[5].wait()
    for block in range(2):
        rows = slice(block * 256, block * 256 + 256)
        part_ref[rows, :] = mm(att_ref[rows, :], wo_ref[...])
        sender.send(part_ref.at[rows, :], part_out.at[rows, :])
    sender.finish()


def fourths(start, part):
    return pl.ds(pl.multiple_of(start * part, 8), part)


def slot_at(place):
    core = lax.axis_index("mp") % 2
    return (place // 2) * (1 + core) + (place % 2) * (2 - core)


def quarter_at(place):
    return lax.axis_index("dp") % PLANE ^ slot_at(place)


def fourth_at(place):
    return lax.axis_index("dp") % GROUP // PLANE ^ slot_at(place)


def z_place(block):
    slot = lax.axis_index("dp") % GROUP // PLANE ^ block
    return jnp.where(lax.axis_index("mp") % 2 == 0, (slot % 2) * 2 + slot // 2, slot)


def place_quarter(outs, place, value):
    part = value.shape[0] // STACK
    for block in range(STACK):
        outs[place // 2][place % 2, z_place(block)] = value[block * part : (block + 1) * part]


def place_quarter_z_first(outs, place, first_row, value):
    part = value.shape[0] // STACK
    for block in range(STACK):
        z = z_place(block)
        for sent in range(2):

            @pl.when(z // 2 == sent)
            def _(out=outs[sent], z=z, piece=value[block * part : (block + 1) * part]):
                out[z % 2, place, first_row : first_row + part, :] = piece


def mlp_kernel(
    gain_in, bu_in, x_in, mine_in, theirs_in, cot_in, wu_in, wd_in,
    residual_out, gbu_ref, d_kept, d_sent, c_kept, c_sent, u_kept, u_sent, shares_out,
    gain_ref, bu_ref, x_ref, mine_ref, theirs_ref, cot_ref, wu_ref, wd_ref,
    residual_ref, normed_ref, act_ref, du_ref, d_kept_ref, d_sent_ref, c_kept_ref, c_sent_ref, u_kept_ref, u_sent_ref, shares_ref,
    sems, out_sems,
):
    row_count = x_ref.shape[0]
    units = wu_ref.shape[1]
    halves = (slice(0, row_count // 2), slice(row_count // 2, row_count))
    pairs = [(gain_in, gain_ref), (bu_in, bu_ref)]
    for rows in halves:
        pairs += [(a.at[rows, :], b.at[rows, :]) for a, b in ((x_in, x_ref), (mine_in, mine_ref), (theirs_in, theirs_ref))]
    copies = fetch(pairs + [(cot_in, cot_ref), (wu_in, wu_ref), (wd_in, wd_ref)], sems)
    sender = Sender(out_sems)
    gbu_ref[...] = jnp.zeros_like(gbu_ref)
    copies[0].wait()
    gain = gain_ref[...].reshape(1, -1)
    for half in range(2):
        for copy in copies[2 + 3 * half : 5 + 3 * half]:
            copy.wait()

        @pl.loop(0, row_count // 128)
        def _(i, half=half):
            rows = pl.ds(pl.multiple_of(half * (row_count // 2) + i * 64, 64), 64)
            residual = x_ref[rows, :].astype(f32) + (mine_ref[rows, :] + theirs_ref[rows, :])
            residual_ref[rows, :] = residual
            normed_ref[rows, :] = layer_norm_rows(residual, gain).astype(bf16)

    sender.send(residual_ref, residual_out)
    for copy in (copies[1], *copies[8:]):
        copy.wait()
    c0 = math.sqrt(2.0 / math.pi)
    c1 = c0 * 0.044715

    @pl.loop(0, units // 512)
    def _(j):
        cols = pl.ds(pl.multiple_of(j * 512, 512), 512)
        blocks = [slice(block * 256, block * 256 + 256) for block in range(row_count // 256)]
        ups = [mm(normed_ref[rows, :], wu_ref[:, cols]) + bu_ref[cols].reshape(1, -1) for rows in blocks]
        deltas = [nt(cot_ref[rows, :], wd_ref[cols, :]) for rows in blocks]
        for rows, u, delta in zip(blocks, ups, deltas):
            square = u * u
            t = jnp.tanh(u * (c0 + c1 * square))
            half_up = 0.5 + 0.5 * t
            act = u * half_up
            act_ref[rows, cols] = act.astype(bf16)
            slope = half_up + act * ((1.0 - t) * (c0 + (3.0 * c1) * square))
            low = (delta * slope).astype(bf16)
            du_ref[rows, cols] = low
            gbu_ref[:, cols] += jnp.sum(low.astype(f32), axis=0, keepdims=True)

    quarter = units // PLANE
    fourth = units // GROUP
    cut = cot_ref.shape[1] * 2 // 3
    up_cut = quarter * 2 // 3
    quarters = {}
    for place in range(PLANE):
        quarters[place] = pl.ds(pl.multiple_of(quarter_at(place) * quarter, LANES), quarter)
    for share in range(2):
        for rows in halves:
            if share == 0:
                shares_ref[share, rows, :] = nt(du_ref[rows, :], wu_ref[...])
            else:
                shares_ref[share, rows, :] = mm(act_ref[rows, :], wd_ref[...])
        sender.send(shares_ref.at[share], shares_out.at[share])
    c_pairs = ((c_kept_ref, c_kept), (c_sent_ref, c_sent))
    for place in (2, 3, 0, 1):
        grad = tn(act_ref[:, quarters[place]], cot_ref[...])
        place_quarter((d_kept_ref, d_sent_ref), place, grad[:, :cut])
        place_quarter_z_first((c_kept_ref, c_sent_ref), place, 0, grad[:, cut:])
        source, target = ((d_kept_ref, d_kept), (d_sent_ref, d_sent))[place // 2]
        sender.send(source.at[place % 2], target.at[place % 2])
        for source, target in c_pairs:
            rows = pl.ds(0, fourth)
            sender.send(source.at[:, place, rows, :], target.at[:, place, rows, :])
    for place in (2, 3, 0, 1):
        grad = tn(normed_ref[...], du_ref[:, quarters[place]])
        place_quarter((u_kept_ref, u_sent_ref), place, grad[:, :up_cut])
        rest = grad[:, up_cut:].reshape(STACK, 2, fourth, -1)
        rest = jnp.concatenate([rest[:, 0], rest[:, 1]], 2).reshape(STACK * fourth, -1)
        place_quarter_z_first((c_kept_ref, c_sent_ref), place, fourth, rest)
        source, target = ((u_kept_ref, u_kept), (u_sent_ref, u_sent))[place // 2]
        sender.send(source.at[place % 2], target.at[place % 2])
        for source, target in c_pairs:
            rows = pl.ds(fourth, fourth)
            sender.send(source.at[:, place, rows, :], target.at[:, place, rows, :])
    sender.finish()


def attention_backward(*refs):
    ins, refs = refs[:20], refs[20:]
    (output_out, delta_out, part_out, vec_ref), outs_at, refs = refs[:4], refs[4:8], refs[8:]
    held, refs = refs[:20], refs[20:]
    (output_ref, delta_ref, part_ref), outs, refs = refs[:3], refs[3:7], refs[7:]
    branch_ref, datt_ref, dq_ref, dk_ref, dv_ref, dk_acc, dv_acc, grads_ref, gnorm_ref, sems, out_sems = refs
    mine_ref, theirs_ref, residual_ref, cot_ref, gain_ref, bd_ref, att_ref, wo_ref, q_ref, k_ref, v_ref = held[:11]
    prob_ref, cos_ref, sin_ref, wq_ref, wk_ref, wv_ref, x_ref, normed_ref, gbu_ref = held[11:]
    row_count = residual_ref.shape[0]
    heads_cols = wq_ref.shape[1]
    pairs = heads_cols // LANES
    halves = (slice(0, row_count // 2), slice(row_count // 2, row_count))
    first = []
    for rows in halves:
        first += [(a.at[:, rows, :], b.at[:, rows, :]) for a, b in zip(ins[:2], held[:2])]
        first += [(a.at[rows, :], b.at[rows, :]) for a, b in zip(ins[2:4], held[2:4])]
    copies = fetch(first + list(zip(ins[4:], held[4:])), sems)
    sender = Sender(out_sems)
    gnorm_ref[...] = jnp.zeros_like(gnorm_ref)
    copies[8].wait()
    copies[9].wait()
    gain, bias_down = gain_ref[...].reshape(1, -1), bd_ref[...].reshape(1, -1)
    for half in range(2):
        for copy in copies[4 * half : 4 * half + 4]:
            copy.wait()

        @pl.loop(0, row_count // 128)
        def _(i, half=half):
            rows = pl.ds(pl.multiple_of(half * (row_count // 2) + i * 64, 64), 64)
            delta = mine_ref[0, rows, :] + theirs_ref[0, rows, :]
            residual = residual_ref[rows, :]
            output_ref[rows, :] = (residual + (mine_ref[1, rows, :] + theirs_ref[1, rows, :]) + bias_down).astype(bf16)
            back, gain_part = norm_back_rows(residual, gain, delta)
            cotangent = cot_ref[rows, :].astype(f32)
            back = back + cotangent
            delta_ref[rows, :] = back
            branch_ref[rows, :] = back.astype(bf16)
            gnorm_ref[0:1, :] += gain_part
            gnorm_ref[2:3, :] += jnp.sum(cotangent, axis=0, keepdims=True)

    sender.send(output_ref, output_out)
    sender.send(delta_ref, delta_out)
    for copy in copies[10:]:
        copy.wait()
    for block in range(2):
        rows = slice(block * 256, block * 256 + 256)
        datt_ref[rows, :] = nt(branch_ref[rows, :], wo_ref[...]).astype(bf16)
    half = heads_cols
    grad = tn(att_ref[...], branch_ref[...])
    grads_ref[0, 0], grads_ref[0, 1] = grad[:, :half], grad[:, half:]

    for t in range(pairs):
        cols = slice(t * LANES, (t + 1) * LANES)
        key_pair, value_pair = k_ref[:, cols], v_ref[:, cols]
        dk_acc[...] = jnp.zeros_like(dk_acc)
        dv_acc[...] = jnp.zeros_like(dv_acc)
        query_grads = [None] * 4
        jobs, deltas, lows, keys_of = [], [], [], []
        for which in range(2):
            mask = head_mask(key_pair.shape[0], which)
            keys_of.append(jnp.where(mask, key_pair, jnp.zeros_like(key_pair)))
            value_head = jnp.where(mask, value_pair, jnp.zeros_like(value_pair))
            for case, (query_row, first, width, key_row) in enumerate(CASES):
                jobs.append((which, case))
                lows.append(prob_ref[2 * t + which, :, first : first + width])
                rows = slice(query_row, query_row + HALF)
                deltas.append(nt(datt_ref[rows, cols], value_head[key_row : key_row + width]))
        wides = [low.astype(f32) for low in lows]
        weighted = [wide * g for wide, g in zip(wides, deltas)]
        totals = [jnp.sum(a, axis=1, keepdims=True) for a in weighted]
        backs = [(a - wide * total).astype(bf16) for a, wide, total in zip(weighted, wides, totals)]
        for (which, case), low, back in zip(jobs, lows, backs):
            query_row, _, width, key_row = CASES[case]
            rows, keys = slice(query_row, query_row + HALF), slice(key_row, key_row + width)
            small = head_mask(HALF, which)
            part = mm(back, keys_of[which][keys])
            query_grads[case] = part if query_grads[case] is None else query_grads[case] + part
            query, delta_head = q_ref[rows, cols], datt_ref[rows, cols]
            dk_acc[keys, :] += tn(back, jnp.where(small, query, jnp.zeros_like(query)))
            dv_acc[keys, :] += tn(low, jnp.where(small, delta_head, jnp.zeros_like(delta_head)))
        for block in range(4):
            rows = slice(block * HALF, block * HALF + HALF)
            places = slice((block % 2) * HALF, (block % 2) * HALF + HALF)
            key_rows = slice(KEY_PLACE[block] * HALF, KEY_PLACE[block] * HALF + HALF)
            cosine, sine = cos_ref[places, :], sin_ref[places, :]
            grad = query_grads[block] * score_scale
            dq_ref[rows, cols] = (grad * cosine - swap_halves(grad) * sine).astype(bf16)
            grad = dk_acc[key_rows, :]
            dk_ref[rows, cols] = (grad * cosine - swap_halves(grad) * sine).astype(bf16)
            dv_ref[rows, cols] = dv_acc[key_rows, :].astype(bf16)

    for block in range(2):
        rows = slice(block * 256, block * 256 + 256)
        part_ref[rows, :] = (
            nt(dq_ref[rows, :], wq_ref[...]) + nt(dk_ref[rows, :], wk_ref[...]) + nt(dv_ref[rows, :], wv_ref[...])
        )
    sender.send(part_ref, part_out)

    @pl.loop(0, row_count // 64)
    def _(i):
        rows = pl.ds(pl.multiple_of(i * 64, 64), 64)
        gnorm_ref[1:2, :] += jnp.sum(part_ref[rows, :] * scaled_rows(x_ref[rows, :].astype(f32)), axis=0, keepdims=True)

    vec_ref[...] = jnp.zeros_like(vec_ref)
    row = 0
    once = jnp.where(lax.axis_index("mp") == 0, 1.0, 0.0)
    for values in (gnorm_ref[1:2, :], gnorm_ref[0:1, :] * once, gnorm_ref[2:3, :] * once, gbu_ref[...]):
        for first in range(0, values.shape[1], half):
            vec_ref[row : row + 1, :] = values[:, first : first + half]
            row += 1

    for matrix, grad_rows in ((1, dq_ref), (2, dk_ref), (3, dv_ref)):
        grad = tn(normed_ref[...], grad_rows[...])
        grads_ref[matrix, 0], grads_ref[matrix, 1] = grad[:half], grad[half:]
    for places in ((2, 3), (0, 1)):
        for place in places:
            quarter = quarter_at(place)
            place_quarter(outs[:2], place, grads_ref[quarter, 0])
            place_quarter(outs[2:], place, grads_ref[quarter, 1])
        for portion in range(2):
            which = 2 * portion + places[0] // 2
            sender.send(outs[which], outs_at[which])
    sender.finish()


def input_kernel(mine_ref, theirs_ref, x_ref, gain_ref, delta_ref, grad_ref):
    @pl.loop(0, x_ref.shape[0] // 64)
    def _(i):
        rows = pl.ds(pl.multiple_of(i * 64, 64), 64)
        delta = mine_ref[rows, :] + theirs_ref[rows, :]
        back, _ = norm_back_rows(x_ref[rows, :].astype(f32), gain_ref[...], delta)
        grad_ref[rows, :] = (delta_ref[rows, :] + back).astype(bf16)


def put_in_place(views, z_first, sent, olds, piece_ref, *refs):
    *refs, held_ref, in_sems, sems = refs
    outs = refs[olds:]
    blocks = [(i, j) for i in range(2) for j in range(STACK)]
    copies = fetch([(piece_ref.at[i, j], held_ref.at[i, j]) for i, j in blocks], in_sems)
    for start in (True, False):
        count = 0
        for i in range(2):
            for j in range(STACK):
                if start:
                    copies[STACK * i + j].wait()
                z, place = (2 * sent + i, j) if z_first else (j, 2 * sent + i)
                for wanted, source, target in views(outs, quarter_at(place), fourth_at(z), held_ref.at[i, j]):
                    copy = pltpu.make_async_copy(source, target, sems.at[count])
                    count += 1
                    act = copy.start if start else copy.wait
                    if wanted is None:
                        act()
                    else:
                        pl.when(wanted)(act)


def down_views(outs, quarter, fourth, block):
    part, cols = block.shape
    yield None, block, outs[0].at[fourths(quarter * STACK + fourth, part), pl.ds(0, cols)]


def up_views(outs, quarter, fourth, block):
    part, cols = block.shape
    whole = outs[0].shape[1] // PLANE
    yield None, block, outs[0].at[fourths(fourth, part), pl.ds(pl.multiple_of(quarter * whole, LANES), cols)]


def stack_views(outs, quarter, fourth, block):
    part, cols = block.shape[0] // 2, block.shape[1]
    whole, rest = outs[1].shape[1] // PLANE, cols // 2
    down_rows, down_cols = fourths(quarter * STACK + fourth, part), pl.ds(outs[0].shape[1] - cols, cols)
    yield None, block.at[pl.ds(0, part), :], outs[0].at[down_rows, down_cols]
    up_cols = pl.ds(pl.multiple_of((quarter + 1) * whole - rest, LANES), rest)
    for half in range(2):
        source = block.at[pl.ds(part, part), pl.ds(half * rest, rest)]
        yield None, source, outs[1].at[fourths(fourth * 2 + half, part), up_cols]


def attention_views(portion, outs, quarter, fourth, block):
    part, half = block.shape[0], block.shape[1]
    for matrix, out in enumerate(outs):
        if matrix:
            target = out.at[pl.ds(pl.multiple_of(portion * half + fourth * part, 8), part), :]
        else:
            target = out.at[fourths(fourth, part), pl.ds(portion * half, half)]
        yield quarter == matrix, block, target


VMEM = pl.BlockSpec(memory_space=pltpu.VMEM)
HBM = pl.BlockSpec(memory_space=pltpu.HBM)


def call(kernel, outs, held=(), loose=(), scratch=(), flops=0, limit=40, loose_outs=None):
    ins = [*held, *loose]
    shapes = [jax.ShapeDtypeStruct(shape, dtype) for shape, dtype in outs]
    moved = sum(math.prod(a.shape) * a.dtype.itemsize for a in ins + shapes)
    out_specs = [HBM if loose_outs and i in loose_outs else VMEM for i in range(len(outs))]
    return pl.pallas_call(
        kernel,
        name=kernel.__name__,
        out_shape=shapes,
        in_specs=[VMEM] * len(held) + [HBM] * len(loose),
        out_specs=out_specs,
        scratch_shapes=[s if not isinstance(s, tuple) else pltpu.VMEM(*s) for s in scratch],
        compiler_params=pltpu.CompilerParams(vmem_limit_bytes=limit * 1024 * 1024),
        cost_estimate=pl.CostEstimate(flops=flops, bytes_accessed=moved, transcendentals=0),
    )(*ins)


def on_device(
    count,
    inputs, norm_attn, w_query, w_key, w_value, w_out, norm_mlp, w_up, b_up, w_down, b_down, cotangent,
    doc_lengths, pad_counts,
):
    rows, width = inputs.shape
    heads_cols = w_query.shape[1]
    units = w_up.shape[1]
    heads = heads_cols // HEAD
    cosine, sine = (jnp.asarray(t) for t in rope_tables())
    gain_attn = norm_attn.reshape(1, -1)

    def swap(values):
        return lax.ppermute(values, "mp", [(0, 1), (1, 0)])

    def flip(values, bits, name):
        pairs = [(2 * i + core, 2 * (i ^ bits[core]) + core) for i in range(count) for core in range(2)]
        with jax.named_scope(name):
            return lax.ppermute(values, ("dp", "mp"), pairs)

    def sems(n):
        return pltpu.SemaphoreType.DMA((n,))

    half = heads_cols

    def portions(*shape):
        return [((2, STACK) + shape, f32)] * 2

    last = []

    def turn(*values):
        if not last:
            return values
        values, _ = lax.optimization_barrier((values, last.pop()))
        return values

    def did(value):
        last[:] = [value]
        return value

    def over_groups(values):
        if count == GROUP:
            return values
        groups = [[k * GROUP + j for k in range(count // GROUP)] for j in range(GROUP)]
        return lax.psum(values, "dp", axis_index_groups=groups)

    def chain(name, parts, result, z_first=False, vec=None):
        keep, send = parts
        plane, stack = [(FIRST, "first"), (SECOND, "second")], [(Z_FIRST, "z_first"), (Z_SECOND, "z_second")]
        steps = stack + plane if z_first else plane + stack

        def join(values):
            return values if vec is None else jnp.concatenate([values.reshape(-1, values.shape[-1]), vec], 0)

        def part_of(got, like, vec):
            if vec is None:
                return got, None
            return got[: -vec.shape[0]].reshape(like.shape), vec + got[-vec.shape[0] :]

        for step, (bits, label) in enumerate(steps):
            if step:
                keep, got, vec = turn(keep, got, vec)
                got, vec = part_of(got, keep, vec)
            if step == 0:
                send = join(send)
            elif step == 1:
                send, keep = did(join(keep[1] + got[1])), keep[0] + got[0]
            elif step == 2:
                send, keep = did(join(keep[2:] + got[2:])), keep[:2] + got[:2]
            else:
                keep = keep + got
                send = did(join(keep))
            got = flip(send, bits, f"{name}_sum_{label}")
            yield
        keep, got, vec = turn(keep, got, vec)
        got, vec = part_of(got, keep, vec)
        own = over_groups(did(keep + got[::-1]))
        if vec is not None:
            sums.append(over_groups(vec))
        for step, (bits, label) in enumerate(reversed(steps[:3])):
            got = flip(own, bits, f"{name}_gather_{label}")
            if step == 2:
                result.append(own)
            yield
            own, got = turn(own, got)
            if step < 2:
                own = did(jnp.stack([own, got]) if step == 1 else jnp.concatenate([own, got], 0))
        did(got)
        result.append(got)
        yield

    scores = (heads, HALF, 8 * LANES)
    rows_of = {"width": ((rows, width), bf16), "heads": ((rows, heads_cols), bf16), "sum": ((rows, width), f32)}
    outs = [rows_of["width"]] + [rows_of["heads"]] * 4 + [(scores, bf16), rows_of["sum"]]
    normed, q, k, v, attended, probs, branch = call(
        attention_forward,
        outs,
        loose=[doc_lengths.T, pad_counts, norm_attn, inputs, w_query, w_key, w_value, cosine, sine, w_out],
        scratch=[
            (scores[1:], f32),
            pltpu.SMEM(doc_lengths.shape[::-1], jnp.int32),
            pltpu.SMEM(pad_counts.shape, jnp.int32),
            (norm_attn.shape, f32),
            rows_of["width"],
            *[((width, heads_cols), bf16)] * 3,
            (cosine.shape, f32),
            (sine.shape, f32),
            ((heads_cols, width), bf16),
            *outs,
            sems(10),
            sems(10),
        ],
        flops=2 * rows * width * heads_cols * 4,
        limit=62,
        loose_outs=range(7),
    )
    branch_other = swap(branch)

    big = [
        *portions(units // GROUP, width * 2 // 3),
        *portions(units // GROUP + width // STACK // 2, width // 3),
        *portions(width // STACK, units // PLANE * 2 // 3),
        ((2, rows, width), f32),
    ]
    residual, grad_bu, *parts, shares = call(
        mlp_kernel,
        [rows_of["sum"], ((1, units), f32), *big],
        loose=[norm_mlp, b_up, inputs, branch, branch_other, cotangent, w_up, w_down],
        scratch=[
            (norm_mlp.shape, f32),
            (b_up.shape, f32),
            rows_of["width"],
            rows_of["sum"],
            rows_of["sum"],
            rows_of["width"],
            ((width, units), bf16),
            ((units, width), bf16),
            rows_of["sum"],
            rows_of["width"],
            ((rows, units), bf16),
            ((rows, units), bf16),
            *big,
            sems(11),
            sems(27),
        ],
        flops=2 * rows * width * units * 6,
        limit=62,
        loose_outs=(0, *range(2, 9)),
    )
    made, grads, sums = {key: [] for key in "dcuab"}, {}, []
    chains = {
        "d": chain("down", parts[:2], made["d"]),
        "c": chain("down_stack", parts[2:4], made["c"], True),
        "u": chain("up", parts[4:], made["u"]),
    }
    state = {"shares_other": swap(shares)}

    def backward():
        (shares_other,) = turn(state["shares_other"])
        ins = [
            shares, shares_other, residual, cotangent, norm_mlp, b_down, attended, w_out, q, k, v,
            probs, cosine, sine, w_query, w_key, w_value, inputs, normed, grad_bu,
        ]
        outs = [rows_of["width"], rows_of["sum"], rows_of["sum"]]
        pieces = portions(half // STACK, half) * 2
        state["output"], state["delta_residual"], state["normed_part"], vec, *parts = call(
            attention_backward,
            [*outs, ((16, half), f32), *pieces],
            loose=ins,
            scratch=[
                *[(a.shape, a.dtype) for a in ins],
                *outs,
                *pieces,
                rows_of["width"],
                *[rows_of["heads"]] * 4,
                ((rows, LANES), f32),
                ((rows, LANES), f32),
                ((PLANE, 2, half, half), f32),
                ((8, width), f32),
                sems(24),
                sems(7),
            ],
            flops=2 * rows * width * heads_cols * 10,
            limit=62,
            loose_outs=(0, 1, 2, 4, 5, 6, 7),
        )
        did(vec)
        state["normed_other"] = swap(state["normed_part"])
        chains["a"] = chain("attention", parts[:2], made["a"], vec=vec)
        chains["b"] = chain("attention_rest", parts[2:], made["b"])

    def input_back():
        (normed_other,) = turn(state["normed_other"])
        (state["grad_inputs"],) = call(
            input_kernel,
            [((rows, width), bf16)],
            held=[state["normed_part"], normed_other, inputs, gain_attn, state["delta_residual"]],
        )
        did(state["grad_inputs"])

    shapes = {
        "down": ((units, width), f32),
        "up": ((width, units), f32),
        "out": ((heads_cols, width), f32),
        "query": ((width, heads_cols), f32),
        "key": ((width, heads_cols), f32),
        "value": ((width, heads_cols), f32),
    }
    attention = ("out", "query", "key", "value")
    targets = {
        "d": (down_views, ("down",)),
        "u": (up_views, ("up",)),
        "c": (stack_views, ("down", "up")),
        "a": (partial(attention_views, 0), attention),
        "b": (partial(attention_views, 1), attention),
    }

    def put(key, sent):
        views, names = targets[key]
        olds = [name for name in names if name in grads]
        assert len(olds) in (0, len(names))
        (piece,) = turn(made[key][sent])
        results = pl.pallas_call(
            partial(put_in_place, views, key == "c", sent, len(olds)),
            name=f"put_{key}",
            out_shape=[jax.ShapeDtypeStruct(*shapes[name]) for name in names],
            in_specs=[pl.BlockSpec(memory_space=pl.ANY)] + [HBM] * len(olds),
            out_specs=[HBM] * len(names),
            scratch_shapes=[pltpu.VMEM(piece.shape, f32), sems(8), sems(32)],
            input_output_aliases={1 + i: i for i in range(len(olds))},
            compiler_params=pltpu.CompilerParams(vmem_limit_bytes=8 * 1024 * 1024),
            cost_estimate=pl.CostEstimate(flops=0, bytes_accessed=2 * piece.size * 4, transcendentals=0),
        )(piece, *[grads[name] for name in olds])
        grads.update(zip(names, results))
        did(results[0])

    did(grad_bu)
    pieces = {"K": backward, "I": input_back}
    waiting = []
    for key in ORDER:
        if key in waiting:
            waiting.remove(key)
            put(key, 0)
        if key in pieces:
            pieces[key]()
        else:
            next(chains[key])
        for other in list(waiting):
            if other != "c" or ("down" in grads and "up" in grads):
                waiting.remove(other)
                put(other, 0)
        if len(made.get(key, ())) == 1:
            waiting.append(key)
        elif len(made.get(key, ())) == 2:
            put(key, 1)

    vec = sums[0]
    n = width // half
    shared = (vec[: 3 * n] + swap(vec[: 3 * n])).reshape(3, width)
    grad_bu = vec[3 * n :].reshape(-1)[:units]
    grad_down, grad_up = grads["down"], grads["up"]
    grad_out, grad_query, grad_key, grad_value = (grads[name] for name in attention)
    output, grad_inputs = state["output"], state["grad_inputs"]
    return (
        output,
        grad_inputs,
        shared[0],
        grad_query,
        grad_key,
        grad_value,
        grad_out,
        shared[1],
        grad_up,
        grad_bu,
        grad_down,
        shared[2],
    )


def solution(mesh):
    count = mesh.shape["dp"]

    def step(*args):
        return on_device(count, *args)

    return jax.shard_map(
        step,
        mesh=mesh,
        in_specs=(
            P("dp", None),
            P(),
            P(None, "mp"),
            P(None, "mp"),
            P(None, "mp"),
            P("mp", None),
            P(),
            P(None, "mp"),
            P("mp"),
            P("mp", None),
            P(),
            P("dp", None),
            P(),
            P(),
        ),
        out_specs=(
            P("dp", None),
            P("dp", None),
            P(),
            P(None, "mp"),
            P(None, "mp"),
            P(None, "mp"),
            P("mp", None),
            P(),
            P(None, "mp"),
            P("mp"),
            P("mp", None),
            P(),
        ),
        check_vma=False,
    )
```
